128 devices in a mesh: member: 8 (over z, y_hi), mp: 16 (over x, y_lo, core).
Axes of the slice: x: 4, y: 4 (y_hi: 2, y_lo: 2; y = y_hi * 2 + y_lo), z: 4, core: 2. Of those that a mesh axis runs over, the one named last changes fastest.
Arguments:
- grid_point_features: bfloat16 [8, 8192, 1024], P('member', 'mp'), may hold values from -6 to 6
- projection_weights_qkv: bfloat16 [1024, 3072], replicated, may hold values from -0.75 to 0.75
- merging_projection: bfloat16 [1024, 1024], replicated, may hold values from -0.1875 to 0.1875
- readout_weights_table: bfloat16 [1024, 128], replicated, may hold values from -0.1875 to 0.1875
- observed: float32 [8192, 128], P('mp'), may hold values from -6 to 6
- cell_surface_share: float32 [8192], P('mp'), may hold values from 0.25 to 4
- band_offsets: int32 [16, 3], replicated, may hold values from -2 to 2, as said below
- latitude_order: int32 [16, 512], P('mp'), may hold values from 0 to 511, each once within a row
Outputs:
- predictions: float32 [8, 8192, 128], P('member', 'mp')
- feature_derivative: float32 [8, 8192, 1024], P('member', 'mp')
- grad_input_weight: float32 [1024, 3072], P(('member', 'mp'))
- grad_output_weight: float32 [1024, 1024], P(('member', 'mp'))
- grad_decoder_weight: float32 [1024, 128], P(('member', 'mp'))
The draws below stay inside these ranges and needn't reach their ends.
Inputs may be any that keep to these rules, and one draw needn't show every extreme that they name: For each query block b, band_offsets[b] holds 3 different offsets, the first one 0, each with b + offset a block from 0 to 15.
All inputs are finite; a program needn't handle non-finite values.
Results may differ from the reference program's by a relative error of at most 0.024.
Values may be sent and summed in bfloat16 or wider, within the bound.
A program may use at most 128 MiB of HBM per device.

```python
import math
import jax
import jax.numpy as jnp
from jax import lax

D = 1024
HEADS = 16
HEAD_DIM = 64
OUTV = 128
BLOCK = 512
BAND = 3
REACH = 2
QBLOCKS = 16
NODES = 8192
MEMBERS = 8
N_MP = 16


def draw_projection_weights_qkv(key, part):
    key = jax.random.fold_in(key, 7)
    first, second, third = jax.random.split(key, 3)
    scaling = 1.0 / math.sqrt(D)
    query_part = jnp.clip(jax.random.normal(first, (D, D), jnp.float32), -4.0, 4.0) * scaling
    key_part = jnp.clip(jax.random.normal(second, (D, D), jnp.float32), -4.0, 4.0) * scaling
    value_part = jnp.clip(jax.random.normal(third, (D, D), jnp.float32), -4.0, 4.0) * scaling
    return jnp.concatenate([query_part, key_part, value_part], axis=1).astype(jnp.bfloat16)


def draw_band_offsets(key, part):
    key = jax.random.fold_in(key, 13)
    candidates = jnp.concatenate([jnp.arange(-REACH, 0), jnp.arange(1, REACH + 1)]).astype(jnp.int32)
    targets = jnp.arange(QBLOCKS, dtype=jnp.int32)[:, None] + candidates[None, :]
    allowed = (targets >= 0) & (targets < QBLOCKS)
    columns = 2 * REACH
    ranks = jax.random.randint(key, (QBLOCKS, columns), 0, 1 << 20) * columns + jnp.arange(columns, dtype=jnp.int32)[None, :]
    ranks = jnp.where(allowed, ranks, -1)
    unused, picked = lax.top_k(ranks, BAND - 1)
    chosen = candidates[picked]
    return jnp.concatenate([jnp.zeros((QBLOCKS, 1), jnp.int32), chosen], axis=1).astype(jnp.int32)


def block_scale(key, dims, cuts, least, top_value):
    def one(axis_at, shards_of):
        draws = jax.random.uniform(jax.random.fold_in(jax.random.fold_in(key, 6), axis_at), (shards_of,), jnp.float32, least / len(cuts), top_value / len(cuts))
        return jnp.repeat(jnp.exp(draws), dims[axis_at] // shards_of).reshape((-1,) + (1,) * (len(dims) - axis_at - 1))

    loudness = one(*cuts[0])
    for cut in cuts[1:]:
        loudness = loudness * one(*cut)
    return loudness


def gaussian(key, extent, width, bound, cuts=(), kind=jnp.bfloat16):
    level = block_scale(key, extent, cuts, -0.22, 0.18) if cuts else 1.0
    drawn = jax.random.normal(key, extent, jnp.float32) * width * level
    return jnp.minimum(jnp.maximum(drawn, -bound), bound).astype(kind)


def setup_inputs(seed: int = 0) -> dict:
    key_list = jax.random.split(jax.random.key(seed), 9)
    return {
        "grid_point_features": gaussian(key_list[0], (MEMBERS, NODES, D), 1.0, 6.0, ((0, 8), (1, 16))),
        "projection_weights_qkv": draw_projection_weights_qkv(jax.random.fold_in(key_list[8], 71), 0),
        "merging_projection": gaussian(key_list[2], (D, D), D ** -0.5, 0.1875),
        "readout_weights_table": gaussian(key_list[3], (D, OUTV), D ** -0.5, 0.1875),
        "observed": gaussian(key_list[4], (NODES, OUTV), 1.0, 6.0, ((0, 16),), jnp.float32),
        "cell_surface_share": jnp.clip(jnp.exp(math.log(4.0) - 2.7725887 * jax.random.uniform(key_list[5], (NODES,), jnp.float32) ** block_scale(key_list[5], (NODES,), ((0, 16),), -0.2, 0.2)), 0.25, 4.0),
        "band_offsets": draw_band_offsets(jax.random.fold_in(key_list[8], 71), 0),
        "latitude_order": jax.vmap(lambda own: jax.random.permutation(own, BLOCK))(jax.random.split(key_list[7], N_MP)).reshape((N_MP, BLOCK)).astype(jnp.int32),
    }


norm_epsilon = 1e-05
smooth_square = 0.0625

def layer_norm(values):
    average = lax.optimization_barrier(jnp.mean(values, axis=-1, keepdims=True))
    centred = values - average
    spread = lax.optimization_barrier(jnp.mean(centred * centred, axis=-1, keepdims=True))
    return centred * lax.rsqrt(spread + norm_epsilon)

def head_forward(asking_entries, lookup_entries, content_entries):
    scaling = 1.0 / math.sqrt(asking_entries.shape[-1])
    scores = jnp.dot(asking_entries, lookup_entries.T, preferred_element_type=jnp.float32) * scaling
    probabilities = jax.nn.softmax(scores, axis=-1).astype(jnp.bfloat16)
    return jnp.dot(probabilities, content_entries, preferred_element_type=jnp.float32).astype(jnp.bfloat16)

def head_backward(asking_entries, lookup_entries, content_entries, grad_context):
    scaling = 1.0 / math.sqrt(asking_entries.shape[-1])
    scores = jnp.dot(asking_entries, lookup_entries.T, preferred_element_type=jnp.float32) * scaling
    probabilities = jax.nn.softmax(scores, axis=-1)
    grad_weights = jnp.dot(grad_context, content_entries.T, preferred_element_type=jnp.float32)
    inner = lax.optimization_barrier(jnp.sum(probabilities * grad_weights, axis=-1, keepdims=True))
    grad_scores = (probabilities * (grad_weights - inner) * scaling).astype(jnp.bfloat16)
    grad_query = jnp.dot(grad_scores, lookup_entries, preferred_element_type=jnp.float32)
    key_terms = jnp.dot(grad_scores.T, asking_entries, preferred_element_type=jnp.float32).astype(jnp.bfloat16)
    value_terms = jnp.dot(probabilities.astype(jnp.bfloat16).T, grad_context, preferred_element_type=jnp.float32).astype(jnp.bfloat16)
    return (grad_query, key_terms, value_terms)

def each_head(function, arrays):
    by_head = tuple((jnp.moveaxis(entry, 1, 0) for entry in arrays))
    return lax.map(lambda element: function(*element), by_head)

def attend(asking_entries, lookup_entries, content_entries, lookup_tile_sequence):
    head_count = asking_entries.shape[2]
    head_size = asking_entries.shape[3]

    def one_block(element):
        query_block, block_ids = element
        key_block = lookup_entries[block_ids].reshape(-1, head_count, head_size)
        value_block = content_entries[block_ids].reshape(-1, head_count, head_size)
        result = each_head(head_forward, (query_block, key_block, value_block))
        return jnp.moveaxis(result, 0, 1)
    return lax.map(one_block, (asking_entries, lookup_tile_sequence))

def attend_back(asking_entries, lookup_entries, content_entries, lookup_tile_sequence, grad_context):
    head_count = asking_entries.shape[2]
    head_size = asking_entries.shape[3]
    band_count = lookup_tile_sequence.shape[1]

    def one_block(element):
        query_block, block_ids, grad_block = element
        key_block = lookup_entries[block_ids].reshape(-1, head_count, head_size)
        value_block = content_entries[block_ids].reshape(-1, head_count, head_size)
        grad_query, key_terms, value_terms = each_head(head_backward, (query_block, key_block, value_block, grad_block))
        key_terms = jnp.moveaxis(key_terms, 0, 1).reshape(band_count, -1, head_count, head_size)
        value_terms = jnp.moveaxis(value_terms, 0, 1).reshape(band_count, -1, head_count, head_size)
        return (jnp.moveaxis(grad_query, 0, 1), key_terms, value_terms)
    return lax.map(one_block, (asking_entries, lookup_tile_sequence, grad_context))

def collect(terms, lookup_tile_sequence, block_count):
    widened = lax.optimization_barrier(terms).astype(jnp.float32)
    flattened = widened.reshape((-1,) + terms.shape[2:])
    summed = jnp.zeros((block_count,) + terms.shape[2:], jnp.float32)
    return summed.at[lookup_tile_sequence.reshape(-1)].add(flattened)

def softened_derivative(difference):
    return difference * lax.rsqrt(difference * difference + smooth_square)

def crps_derivative(local_ensemble_outcomes, observed_truth, couple_spread_total, cell_surface_share, ensemble_collection):
    single = softened_derivative(local_ensemble_outcomes - observed_truth) / ensemble_collection
    paired = couple_spread_total / (ensemble_collection * (ensemble_collection - 1))
    return cell_surface_share[:, None] * (single - paired)

def ensemble_onward_sweep(feature_entries, projection_weights_qkv, merging_projection, readout_weights_table, lookup_tile_sequence):
    node_count = feature_entries.shape[0]
    rescaled_entry_features = layer_norm(feature_entries.astype(jnp.float32)).astype(jnp.bfloat16)
    packed = jnp.dot(rescaled_entry_features, projection_weights_qkv, preferred_element_type=jnp.float32).astype(jnp.bfloat16)
    pieces = packed.reshape(node_count // BLOCK, BLOCK, 3, HEADS, HEAD_DIM)
    asking_entries, lookup_entries, content_entries = (pieces[:, :, 0], pieces[:, :, 1], pieces[:, :, 2])
    mixed_heads_result = attend(asking_entries, lookup_entries, content_entries, lookup_tile_sequence).reshape(node_count, -1)
    latent_activation = (feature_entries.astype(jnp.float32) + jnp.dot(mixed_heads_result, merging_projection, preferred_element_type=jnp.float32)).astype(jnp.bfloat16)
    rescaled_interior_features = layer_norm(latent_activation.astype(jnp.float32)).astype(jnp.bfloat16)
    ensemble_prediction = jnp.dot(rescaled_interior_features, readout_weights_table, preferred_element_type=jnp.float32)
    return (rescaled_entry_features, asking_entries, lookup_entries, content_entries, mixed_heads_result, latent_activation, rescaled_interior_features, ensemble_prediction)

def ensemble_reverse_sweep(feature_entries, prediction_derivative, projection_weights_qkv, merging_projection, readout_weights_table, lookup_tile_sequence):
    node_count = feature_entries.shape[0]
    rescaled_entry_features, asking_entries, lookup_entries, content_entries, mixed_heads_result, latent_activation, rescaled_interior_features, ensemble_prediction = ensemble_onward_sweep(feature_entries, projection_weights_qkv, merging_projection, readout_weights_table, lookup_tile_sequence)
    midway_derivative = prediction_derivative.astype(jnp.bfloat16)
    grad_decoder = jnp.dot(rescaled_interior_features.T, midway_derivative, preferred_element_type=jnp.float32)
    grad_mid = jnp.dot(midway_derivative, readout_weights_table.T, preferred_element_type=jnp.float32)
    grad_hidden = jax.vjp(layer_norm, latent_activation.astype(jnp.float32))[1](grad_mid)[0]
    hidden_half = grad_hidden.astype(jnp.bfloat16)
    grad_output = jnp.dot(mixed_heads_result.T, hidden_half, preferred_element_type=jnp.float32)
    grad_context = jnp.dot(hidden_half, merging_projection.T, preferred_element_type=jnp.float32).astype(jnp.bfloat16)
    grad_context = grad_context.reshape(node_count // BLOCK, BLOCK, HEADS, HEAD_DIM)
    grad_query, key_terms, value_terms = attend_back(asking_entries, lookup_entries, content_entries, lookup_tile_sequence, grad_context)
    grad_keys = collect(key_terms, lookup_tile_sequence, node_count // BLOCK)
    grad_values = collect(value_terms, lookup_tile_sequence, node_count // BLOCK)
    grad_packed = jnp.stack([grad_query, grad_keys, grad_values], axis=2).astype(jnp.bfloat16).reshape(node_count, -1)
    grad_input = jnp.dot(rescaled_entry_features.T, grad_packed, preferred_element_type=jnp.float32)
    grad_normed = jnp.dot(grad_packed, projection_weights_qkv.T, preferred_element_type=jnp.float32)
    feature_derivative = grad_hidden + jax.vjp(layer_norm, feature_entries.astype(jnp.float32))[1](grad_normed)[0]
    return (feature_derivative, grad_input, grad_output, grad_decoder)

def reference(grid_point_features, projection_weights_qkv, merging_projection, readout_weights_table, observed, cell_surface_share, band_offsets, latitude_order):
    ensemble_collection = grid_point_features.shape[0]
    node_count = grid_point_features.shape[1]
    lookup_tile_sequence = (jnp.arange(node_count // BLOCK, dtype=jnp.int32)[:, None] + band_offsets).astype(jnp.int32)
    ensemble_prediction = lax.map(lambda feature_entries: ensemble_onward_sweep(feature_entries, projection_weights_qkv, merging_projection, readout_weights_table, lookup_tile_sequence)[-1], grid_point_features)
    grid_rows = jnp.arange(node_count, dtype=jnp.int32) // BLOCK * BLOCK + latitude_order.reshape(-1).astype(jnp.int32)
    observed_truth = observed[grid_rows]

    def ensemble_derivatives(local_ensemble_outcomes):
        couple_spread_total = lax.optimization_barrier(jnp.sum(softened_derivative(local_ensemble_outcomes[None] - ensemble_prediction), axis=0))
        return crps_derivative(local_ensemble_outcomes, observed_truth, couple_spread_total, cell_surface_share, ensemble_collection)
    prediction_derivative = lax.map(ensemble_derivatives, ensemble_prediction)

    def tally_combiner(cumulative_tallies, element):
        feature_entries, grad_member = element
        feature_derivative, grad_input, grad_output, grad_decoder = ensemble_reverse_sweep(feature_entries, grad_member, projection_weights_qkv, merging_projection, readout_weights_table, lookup_tile_sequence)
        return ((cumulative_tallies[0] + grad_input, cumulative_tallies[1] + grad_output, cumulative_tallies[2] + grad_decoder), feature_derivative)
    starting_tallies = (jnp.zeros(projection_weights_qkv.shape, jnp.float32), jnp.zeros(merging_projection.shape, jnp.float32), jnp.zeros(readout_weights_table.shape, jnp.float32))
    cumulative_tallies, feature_derivative = lax.scan(tally_combiner, starting_tallies, (grid_point_features, prediction_derivative))
    return (ensemble_prediction, feature_derivative, cumulative_tallies[0], cumulative_tallies[1], cumulative_tallies[2])
```

```python
import functools

import jax
import jax.numpy as jnp
from jax import lax
from jax.experimental import pallas as pl
from jax.experimental.pallas import tpu as pltpu
from jax.sharding import PartitionSpec as P

HEADS = 16
HEAD_DIM = 64
BLOCK = 512
WIDTH = 1024
OUTV = 128
BAND = 3

norm_epsilon = 1e-05
smooth_square = 0.0625

MESH = pl.DeviceIdType.MESH
VMEM_LIMIT = 56 * 1024 * 1024

PIECE = 64
PIECES = BLOCK // PIECE

HALF = 2176
PARTS = ((0, 384), (384, 384), (768, 384), (1152, 384), (1536, 384), (1920, 256))
TILE = 16
TILES = 64
CLASSES = 6


def layer_norm(values):
    average = jnp.mean(values, axis=-1, keepdims=True)
    centred = values - average
    spread = jnp.mean(centred * centred, axis=-1, keepdims=True)
    return centred * lax.rsqrt(spread + norm_epsilon)


def place():
    member = lax.axis_index("member")
    mp = lax.axis_index("mp")
    return {
        "z": member // 2,
        "y_hi": member % 2,
        "x": mp // 4,
        "y_lo": (mp // 2) % 2,
        "core": mp % 2,
    }


def device(at):
    return (at["z"] * 2 + at["y_hi"], at["x"] * 4 + at["y_lo"] * 2 + at["core"])


def moved(at, **changes):
    return device({**at, **changes})


def greet(partners):
    barrier = pltpu.get_barrier_semaphore()
    for partner in partners:
        pl.semaphore_signal(barrier, inc=1, device_id=partner, device_id_type=MESH)
    pl.semaphore_wait(barrier, len(partners))


def remote(source, target, send, receive, partner):
    return pltpu.make_async_remote_copy(
        src_ref=source,
        dst_ref=target,
        send_sem=send,
        recv_sem=receive,
        device_id=partner,
        device_id_type=MESH,
    )


def halo_kernel(own, out, y_send, y_recv, x_send, x_recv, c_send, c_recv, o_send, o_recv):
    at = place()
    other = moved(at, core=1 - at["core"])
    across = moved(at, y_lo=1 - at["y_lo"])
    forward = moved(at, x=(at["x"] + 1 + 2 * at["y_lo"]) % 4)
    backward = moved(at, x=(at["x"] + 3 - 2 * at["y_lo"]) % 4)
    greet((other, across, forward, backward))
    near_first = (at["core"] + at["y_lo"]) % 2 == 0

    def rows(piece):
        return pl.ds(piece * PIECE, PIECE)

    def to_across(piece):
        return remote(
            own.at[rows(piece)], out.at[1, rows(piece)], y_send.at[piece], y_recv.at[piece], across
        )

    def to_forward(piece):
        return remote(
            out.at[1, rows(piece)],
            out.at[2, rows(piece)],
            x_send.at[piece],
            x_recv.at[piece],
            forward,
        )

    def to_other(slot, piece):
        return remote(
            out.at[slot, rows(piece)],
            out.at[3, rows(piece)],
            c_send.at[piece],
            c_recv.at[piece],
            other,
        )

    for piece in range(PIECES):
        to_across(piece).start()
    swap = remote(own, out.at[0], o_send, o_recv, other)
    swap.start()
    for piece in range(PIECES):
        to_across(piece).wait_recv()
        to_forward(piece).start()

        @pl.when(near_first)
        def _():
            to_other(1, piece).start()

    for piece in range(PIECES):
        to_forward(piece).wait_recv()

        @pl.when(jnp.logical_not(near_first))
        def _():
            to_other(2, piece).start()

    for piece in range(PIECES):
        to_other(1, piece).wait_recv()
    swap.wait_recv()
    swap.wait_send()
    for piece in range(PIECES):
        to_across(piece).wait_send()
        to_forward(piece).wait_send()
        to_other(1, piece).wait_send()


def halo(own):
    dma = pltpu.SemaphoreType.DMA
    return pl.pallas_call(
        halo_kernel,
        out_shape=jax.ShapeDtypeStruct((4, BLOCK, WIDTH), jnp.bfloat16),
        in_specs=[pl.BlockSpec(memory_space=pltpu.VMEM)],
        out_specs=pl.BlockSpec(memory_space=pltpu.VMEM),
        scratch_shapes=[dma((PIECES,))] * 6 + [dma, dma],
        compiler_params=pltpu.CompilerParams(
            collective_id=0, has_side_effects=True, vmem_limit_bytes=VMEM_LIMIT
        ),
        name="halo",
    )(own)


def halo_back_kernel(
    terms,
    out,
    near,
    far,
    cross_in,
    far_in,
    near_in,
    other_in,
    y_send,
    y_recv,
    x_send,
    x_recv,
    c_send,
    c_recv,
    o_send,
    o_recv,
):
    at = place()
    other = moved(at, core=1 - at["core"])
    across = moved(at, y_lo=1 - at["y_lo"])
    forward = moved(at, x=(at["x"] + 1 + 2 * at["y_lo"]) % 4)
    backward = moved(at, x=(at["x"] + 3 - 2 * at["y_lo"]) % 4)
    greet((other, across, forward, backward))
    near_first = (at["core"] + at["y_lo"]) % 2 == 0

    def rows(piece):
        return pl.ds(piece * PIECE, PIECE)

    def wide(ref, *index):
        return ref[index].astype(jnp.float32)

    def to_other(piece):
        return remote(
            terms.at[3, rows(piece)],
            cross_in.at[rows(piece)],
            c_send.at[piece],
            c_recv.at[piece],
            other,
        )

    def to_backward(piece):
        return remote(
            far.at[rows(piece)], far_in.at[rows(piece)], x_send.at[piece], x_recv.at[piece], backward
        )

    def to_across(piece):
        return remote(
            near.at[rows(piece)], near_in.at[rows(piece)], y_send.at[piece], y_recv.at[piece], across
        )

    for piece in range(PIECES):
        to_other(piece).start()
    swap = remote(terms.at[0], other_in, o_send, o_recv, other)
    swap.start()
    for piece in range(PIECES):
        to_other(piece).wait_recv()
        cross = wide(cross_in, rows(piece))
        near_part = wide(terms, 1, rows(piece))
        far_part = wide(terms, 2, rows(piece))
        far[rows(piece)] = (far_part + jnp.where(near_first, 0.0, cross)).astype(jnp.bfloat16)
        near[rows(piece)] = (near_part + jnp.where(near_first, cross, 0.0)).astype(jnp.bfloat16)
        to_backward(piece).start()
    for piece in range(PIECES):
        to_backward(piece).wait_recv()
        near[rows(piece)] = (wide(near, rows(piece)) + wide(far_in, rows(piece))).astype(
            jnp.bfloat16
        )
        to_across(piece).start()
    swap.wait_recv()
    for piece in range(PIECES):
        to_across(piece).wait_recv()
        out[rows(piece)] = wide(other_in, rows(piece)) + wide(near_in, rows(piece))
    swap.wait_send()
    for piece in range(PIECES):
        to_other(piece).wait_send()
        to_backward(piece).wait_send()
        to_across(piece).wait_send()


def halo_back(terms):
    dma = pltpu.SemaphoreType.DMA
    block = pltpu.VMEM((BLOCK, WIDTH), jnp.bfloat16)
    return pl.pallas_call(
        halo_back_kernel,
        out_shape=jax.ShapeDtypeStruct((BLOCK, WIDTH), jnp.float32),
        in_specs=[pl.BlockSpec(memory_space=pltpu.VMEM)],
        out_specs=pl.BlockSpec(memory_space=pltpu.VMEM),
        scratch_shapes=[block] * 6 + [dma((PIECES,))] * 6 + [dma, dma],
        compiler_params=pltpu.CompilerParams(
            collective_id=1, has_side_effects=True, vmem_limit_bytes=VMEM_LIMIT
        ),
        name="halo_back",
    )(terms)


def members_kernel(own, out, send, receive):
    member = lax.axis_index("member")
    mp = lax.axis_index("mp")
    count = 8
    partners = [((member + step) % count, mp) for step in range(1, count)]
    greet(partners)
    copies = [
        remote(own, out.at[step], send.at[step], receive.at[step], partner)
        for step, partner in enumerate(partners)
    ]
    for copy in copies:
        copy.start()
    for copy in copies:
        copy.wait()


def other_members(own):
    dma = pltpu.SemaphoreType.DMA
    return pl.pallas_call(
        members_kernel,
        out_shape=jax.ShapeDtypeStruct((7,) + own.shape, own.dtype),
        in_specs=[pl.BlockSpec(memory_space=pltpu.VMEM)],
        out_specs=pl.BlockSpec(memory_space=pltpu.VMEM),
        scratch_shapes=[dma((7,)), dma((7,))],
        compiler_params=pltpu.CompilerParams(
            collective_id=2, has_side_effects=True, vmem_limit_bytes=VMEM_LIMIT
        ),
        name="other_members",
    )(own)


def flip(bit, value):
    return (bit + value) % 2


def sum_kernel(grads, out, *scratch):
    parts = len(PARTS)
    first_in = scratch[:parts]
    later_in = scratch[parts : 2 * parts]
    total = scratch[2 * parts : 3 * parts]
    last, last_in, send, receive, last_send, last_recv = scratch[3 * parts :]
    at = place()
    core = at["core"]
    x_bits = (at["x"] % 2, at["x"] // 2)
    z_bits = (at["z"] % 2, at["z"] // 2)
    y_bits = (at["y_lo"], at["y_hi"])
    other = moved(at, core=1 - core)

    def partner_of(link):
        low, high = 1, link // 3
        if link % 3 == 0:
            return moved(at, x=flip(x_bits[0], low) + 2 * flip(x_bits[1], high))
        if link % 3 == 1:
            return moved(at, y_lo=flip(y_bits[0], low), y_hi=flip(y_bits[1], high))
        return moved(at, z=flip(z_bits[0], low) + 2 * flip(z_bits[1], high))

    partners = [partner_of(link) for link in range(CLASSES)]
    greet([other] + partners)

    def link_at(part, step):
        return (part + step) % CLASSES

    def tile_of(part, position):
        bits = {}
        for step in range(CLASSES):
            bits[link_at(part, step)] = (position // (TILES >> (step + 1))) % 2

        def shifted(own, axis):
            low = (own[0] + bits[axis] + bits[axis + 3]) % 2
            high = (own[1] + bits[axis + 3]) % 2
            return low, high

        x_low, x_high = shifted(x_bits, 0)
        y_low, y_high = shifted(y_bits, 1)
        z_low, z_high = shifted(z_bits, 2)
        return (z_low + 2 * z_high) * 16 + y_high * 8 + (x_low + 2 * x_high) * 2 + y_low

    def first_copy(part):
        start, size = PARTS[part]
        return remote(
            grads.at[1 - core, :, pl.ds(start, size)],
            first_in[part],
            send.at[part, 0],
            receive.at[part, 0],
            other,
        )

    def kept(step):
        return (TILES >> step) * TILE

    def later_copy(part, step):
        count = kept(step)
        return remote(
            total[part].at[pl.ds(count, count)],
            later_in[part].at[pl.ds(count, count)],
            send.at[part, step],
            receive.at[part, step],
            partners[link_at(part, step - 1)],
        )

    for part in range(parts):
        first_copy(part).start()
    for part in range(parts):
        start, size = PARTS[part]
        first_copy(part).wait_recv()

        def merge(position, carry):
            source = pl.ds(pl.multiple_of(tile_of(part, position) * TILE, TILE), TILE)
            target = pl.ds(pl.multiple_of(position * TILE, TILE), TILE)
            summed = grads[core, source, pl.ds(start, size)].astype(jnp.float32) + first_in[part][
                source
            ].astype(jnp.float32)
            total[part][target] = summed.astype(jnp.bfloat16)
            return carry

        lax.fori_loop(TILES // 2, TILES, merge, 0, unroll=4)
        later_copy(part, 1).start()
        lax.fori_loop(0, TILES // 2, merge, 0, unroll=4)
    for step in range(1, CLASSES + 1):
        count = kept(step)
        for part in range(parts):
            start, size = PARTS[part]
            later_copy(part, step).wait_recv()
            if step < CLASSES:
                half = count // 2
                for begin in (half, 0):
                    here = pl.ds(begin, half)
                    arrived = later_in[part][pl.ds(count + begin, half)]
                    total[part][here] = (
                        total[part][here].astype(jnp.float32) + arrived.astype(jnp.float32)
                    ).astype(jnp.bfloat16)
                    if begin == half:
                        later_copy(part, step + 1).start()
            else:
                final = total[part][pl.ds(0, TILE)].astype(jnp.float32) + later_in[part][
                    pl.ds(TILE, TILE)
                ].astype(jnp.float32)
                last[:, :, pl.ds(start, size)] = final.reshape(2, 8, size)
    finish = remote(last.at[1 - core], last_in, last_send, last_recv, other)
    finish.start()
    out[core] = last[core]
    finish.wait()
    out[1 - core] = last_in[...]
    for part in range(parts):
        first_copy(part).wait_send()
        for step in range(1, CLASSES + 1):
            later_copy(part, step).wait_send()


def sum_grads(grads):
    dma = pltpu.SemaphoreType.DMA
    parts = len(PARTS)
    rows = TILES * TILE
    blocks = [pltpu.VMEM((rows, size), jnp.bfloat16) for _, size in PARTS]
    return pl.pallas_call(
        sum_kernel,
        out_shape=jax.ShapeDtypeStruct((2, 8, HALF), jnp.float32),
        in_specs=[pl.BlockSpec(memory_space=pltpu.VMEM)],
        out_specs=pl.BlockSpec(memory_space=pltpu.VMEM),
        scratch_shapes=blocks * 3
        + [
            pltpu.VMEM((2, 8, HALF), jnp.float32),
            pltpu.VMEM((8, HALF), jnp.float32),
            dma((parts, CLASSES + 1)),
            dma((parts, CLASSES + 1)),
            dma,
            dma,
        ],
        compiler_params=pltpu.CompilerParams(
            collective_id=3, has_side_effects=True, vmem_limit_bytes=VMEM_LIMIT
        ),
        name="sum_grads",
    )(grads)


NT = (((1,), (1,)), ((), ()))


def head_mask(shape, head):
    lane = lax.broadcasted_iota(jnp.int32, shape, 1)
    return (lane // HEAD_DIM) == head


def attend_kernel(q_ref, k_ref, v_ref, context_ref, stat_ref):
    queries = q_ref[...] * jnp.bfloat16(0.125)
    keys = k_ref[...]
    values_t = v_ref[...].T
    sides = []
    for head in range(2):
        picked = jnp.where(head_mask(queries.shape, head), queries, jnp.bfloat16(0))
        scores = lax.dot_general(keys, picked, NT, preferred_element_type=jnp.float32)
        top = jnp.max(scores, axis=0, keepdims=True)
        powers = jnp.exp(scores - top)
        total = jnp.sum(powers, axis=0, keepdims=True)
        mixed = jnp.dot(
            values_t[head * HEAD_DIM : (head + 1) * HEAD_DIM],
            powers.astype(jnp.bfloat16),
            preferred_element_type=jnp.float32,
        )
        sides.append(mixed / total)
        stat_ref[0, head : head + 1] = top + jnp.log(total)
    context_ref[...] = jnp.concatenate(sides, axis=0).T.astype(jnp.bfloat16)


def attend(q, k, v):
    rows, keys = q.shape[0], k.shape[0]
    pair = 2 * HEAD_DIM
    return pl.pallas_call(
        attend_kernel,
        grid=(HEADS // 2,),
        out_shape=(
            jax.ShapeDtypeStruct((rows, WIDTH), jnp.bfloat16),
            jax.ShapeDtypeStruct((HEADS // 2, 2, rows), jnp.float32),
        ),
        in_specs=[
            pl.BlockSpec((rows, pair), lambda i: (0, i)),
            pl.BlockSpec((keys, pair), lambda i: (0, i)),
            pl.BlockSpec((keys, pair), lambda i: (0, i)),
        ],
        out_specs=(
            pl.BlockSpec((rows, pair), lambda i: (0, i)),
            pl.BlockSpec((1, 2, rows), lambda i: (i, 0, 0)),
        ),
        compiler_params=pltpu.CompilerParams(vmem_limit_bytes=VMEM_LIMIT),
        cost_estimate=pl.CostEstimate(
            flops=4 * rows * keys * WIDTH,
            bytes_accessed=2 * WIDTH * (2 * rows + 2 * keys),
            transcendentals=rows * keys * HEADS,
        ),
        name="attend",
    )(q, k, v)


def attend_back_kernel(q_ref, k_ref, v_ref, context_ref, grad_ref, stat_ref, dq_ref, dk_ref, dv_ref):
    queries = q_ref[...] * jnp.bfloat16(0.125)
    keys = k_ref[...]
    keys_t = keys.T
    values = v_ref[...]
    grads = grad_ref[...]
    products = (grads.astype(jnp.float32) * context_ref[...].astype(jnp.float32)).T
    sides = []
    grad_keys = jnp.zeros(keys.shape, jnp.float32)
    grad_values = jnp.zeros(keys.shape, jnp.float32)
    for head in range(2):
        mask = head_mask(queries.shape, head)
        picked = jnp.where(mask, queries, jnp.bfloat16(0))
        grad_here = jnp.where(mask, grads, jnp.bfloat16(0))
        inner = jnp.sum(products[head * HEAD_DIM : (head + 1) * HEAD_DIM], axis=0, keepdims=True)
        scores = lax.dot_general(keys, picked, NT, preferred_element_type=jnp.float32)
        probs = jnp.exp(scores - stat_ref[0, head : head + 1])
        grad_probs = lax.dot_general(values, grad_here, NT, preferred_element_type=jnp.float32)
        grad_scores = (probs * (grad_probs - inner)).astype(jnp.bfloat16)
        grad_values += jnp.dot(
            probs.astype(jnp.bfloat16), grad_here, preferred_element_type=jnp.float32
        )
        grad_keys += jnp.dot(grad_scores, picked, preferred_element_type=jnp.float32)
        sides.append(
            jnp.dot(
                keys_t[head * HEAD_DIM : (head + 1) * HEAD_DIM],
                grad_scores,
                preferred_element_type=jnp.float32,
            )
        )
    dq_ref[...] = (jnp.concatenate(sides, axis=0) * 0.125).T.astype(jnp.bfloat16)
    dk_ref[...] = grad_keys.astype(jnp.bfloat16)
    dv_ref[...] = grad_values.astype(jnp.bfloat16)


def attend_back(q, k, v, context, grad_context, stats):
    rows, keys = q.shape[0], k.shape[0]
    pair = 2 * HEAD_DIM
    row_block = pl.BlockSpec((rows, pair), lambda i: (0, i))
    key_block = pl.BlockSpec((keys, pair), lambda i: (0, i))
    return pl.pallas_call(
        attend_back_kernel,
        grid=(HEADS // 2,),
        out_shape=(
            jax.ShapeDtypeStruct((rows, WIDTH), jnp.bfloat16),
            jax.ShapeDtypeStruct((keys, WIDTH), jnp.bfloat16),
            jax.ShapeDtypeStruct((keys, WIDTH), jnp.bfloat16),
        ),
        in_specs=[
            row_block,
            key_block,
            key_block,
            row_block,
            row_block,
            pl.BlockSpec((1, 2, rows), lambda i: (i, 0, 0)),
        ],
        out_specs=(row_block, key_block, key_block),
        compiler_params=pltpu.CompilerParams(vmem_limit_bytes=VMEM_LIMIT),
        cost_estimate=pl.CostEstimate(
            flops=10 * rows * keys * WIDTH,
            bytes_accessed=2 * WIDTH * (4 * rows + 4 * keys),
            transcendentals=rows * keys * HEADS,
        ),
        name="attend_back",
    )(q, k, v, context, grad_context, stats)


def softened_derivative(difference):
    return difference * lax.rsqrt(difference * difference + smooth_square)


def dot(left, right):
    return jnp.dot(left, right, preferred_element_type=jnp.float32)


def per_device(
    grid_point_features,
    projection_weights_qkv,
    merging_projection,
    readout_weights_table,
    observed,
    cell_surface_share,
    band_offsets,
    latitude_order,
):
    members = lax.axis_size("member")
    own_rows = grid_point_features[0]
    at = place()
    block = lax.axis_index("mp")
    normed_in = layer_norm(own_rows.astype(jnp.float32)).astype(jnp.bfloat16)

    near, far = jnp.int32(1), jnp.int32(2)
    above = jnp.where(at["y_lo"] == 0, near, far)
    below = jnp.where(at["y_lo"] == 0, far, near)
    minus = jnp.where(at["core"] == 0, 3, 0)
    plus = jnp.where(at["core"] == 0, 0, 3)
    offsets = lax.dynamic_slice(band_offsets, (block, 1), (1, 2))[0]
    slots = jnp.where(
        offsets == -2, below, jnp.where(offsets == -1, minus, jnp.where(offsets == 1, plus, above))
    ).astype(jnp.int32)

    neighbours = halo(normed_in)
    chosen = [
        lax.dynamic_index_in_dim(neighbours, slots[i], 0, keepdims=False) for i in range(BAND - 1)
    ]
    entries = jnp.concatenate([normed_in] + chosen, axis=0)
    weights_q = projection_weights_qkv[:, :WIDTH]
    weights_k = projection_weights_qkv[:, WIDTH : 2 * WIDTH]
    weights_v = projection_weights_qkv[:, 2 * WIDTH :]
    q = dot(normed_in, weights_q).astype(jnp.bfloat16)
    k = dot(entries, weights_k).astype(jnp.bfloat16)
    v = dot(entries, weights_v).astype(jnp.bfloat16)
    context, stats = attend(q, k, v)

    hidden = (own_rows.astype(jnp.float32) + dot(context, merging_projection)).astype(jnp.bfloat16)
    normed_mid = layer_norm(hidden.astype(jnp.float32)).astype(jnp.bfloat16)
    predictions = dot(normed_mid, readout_weights_table)
    others = other_members(predictions.astype(jnp.bfloat16))
    target = observed[latitude_order[0]]
    spread = jnp.sum(
        softened_derivative(predictions[None] - others.astype(jnp.float32)), axis=0
    ) / (members * (members - 1))
    single = softened_derivative(predictions - target) / members
    grad_forecast = (cell_surface_share[:, None] * (single - spread)).astype(jnp.bfloat16)

    grad_decoder = dot(normed_mid.T, grad_forecast)
    grad_mid = dot(grad_forecast, readout_weights_table.T)
    grad_hidden = jax.vjp(layer_norm, hidden.astype(jnp.float32))[1](grad_mid)[0]
    hidden_half = grad_hidden.astype(jnp.bfloat16)
    grad_output = dot(context.T, hidden_half)
    grad_context = dot(hidden_half, merging_projection.T).astype(jnp.bfloat16)
    dq, dk, dv = attend_back(q, k, v, context, grad_context, stats)

    grad_q_weight = dot(normed_in.T, dq)
    grad_k_weight = dot(entries.T, dk)
    grad_v_weight = dot(entries.T, dv)
    grad_entries = dot(dk, weights_k.T) + dot(dv, weights_v.T)
    grad_own = grad_entries[:BLOCK] + dot(dq, weights_q.T)
    first = grad_entries[BLOCK : 2 * BLOCK].astype(jnp.bfloat16)
    second = grad_entries[2 * BLOCK :].astype(jnp.bfloat16)
    terms = jnp.stack(
        [
            jnp.where(slots[0] == slot, first, jnp.where(slots[1] == slot, second, jnp.bfloat16(0)))
            for slot in range(4)
        ]
    )
    grad_normed = grad_own + halo_back(terms)
    feature_derivative = (
        grad_hidden + jax.vjp(layer_norm, own_rows.astype(jnp.float32))[1](grad_normed)[0]
    )

    grads = jnp.concatenate(
        [
            grad_q_weight.astype(jnp.bfloat16),
            grad_k_weight.astype(jnp.bfloat16),
            grad_v_weight.astype(jnp.bfloat16),
            grad_output.astype(jnp.bfloat16),
            grad_decoder.astype(jnp.bfloat16),
            jnp.zeros((WIDTH, 2 * HALF - 4 * WIDTH - OUTV), jnp.bfloat16),
        ],
        axis=1,
    )
    summed = sum_grads(jnp.stack([grads[:, :HALF], grads[:, HALF:]]))
    summed = jnp.concatenate([summed[0], summed[1]], axis=1)
    return (
        predictions[None],
        feature_derivative[None],
        summed[:, : 3 * WIDTH],
        summed[:, 3 * WIDTH : 4 * WIDTH],
        summed[:, 4 * WIDTH : 4 * WIDTH + OUTV],
    )


def solution(mesh):
    placed = (P("member", "mp", None), P(), P(), P(), P("mp", None), P("mp"), P(), P("mp", None))
    return jax.shard_map(
        per_device,
        mesh=mesh,
        in_specs=placed,
        out_specs=(
            P("member", "mp", None),
            P("member", "mp", None),
            P(("member", "mp"), None),
            P(("member", "mp"), None),
            P(("member", "mp"), None),
        ),
        check_vma=False,
    )
```

```python
import functools

import jax
import jax.numpy as jnp
from jax import lax
from jax.experimental import pallas as pl
from jax.experimental.pallas import tpu as pltpu
from jax.sharding import PartitionSpec as P

HEADS = 16
HEAD_DIM = 64
BLOCK = 512
WIDTH = 1024
OUTV = 128
BAND = 3

norm_epsilon = 1e-05
smooth_square = 0.0625

MESH = pl.DeviceIdType.MESH
VMEM_LIMIT = 56 * 1024 * 1024

PIECE = 64
PIECES = BLOCK // PIECE

HALF = 2176
PARTS = ((0, 384), (384, 384), (768, 384), (1152, 384), (1536, 384), (1920, 256))
TILE = 16
TILES = 64
CLASSES = 6
ORDER = (1, 3, 2, 4, 0, 5)
TAIL_VMEM = 60 * 1024 * 1024


def layer_norm(values):
    average = jnp.mean(values, axis=-1, keepdims=True)
    centred = values - average
    spread = jnp.mean(centred * centred, axis=-1, keepdims=True)
    return centred * lax.rsqrt(spread + norm_epsilon)


def place():
    member = lax.axis_index("member")
    mp = lax.axis_index("mp")
    return {
        "z": member // 2,
        "y_hi": member % 2,
        "x": mp // 4,
        "y_lo": (mp // 2) % 2,
        "core": mp % 2,
    }


def device(at):
    return (at["z"] * 2 + at["y_hi"], at["x"] * 4 + at["y_lo"] * 2 + at["core"])


def moved(at, **changes):
    return device({**at, **changes})


def greet(partners):
    barrier = pltpu.get_barrier_semaphore()
    for partner in partners:
        pl.semaphore_signal(barrier, inc=1, device_id=partner, device_id_type=MESH)
    pl.semaphore_wait(barrier, len(partners))


def remote(source, target, send, receive, partner):
    return pltpu.make_async_remote_copy(
        src_ref=source,
        dst_ref=target,
        send_sem=send,
        recv_sem=receive,
        device_id=partner,
        device_id_type=MESH,
    )


def halo_kernel(own, out, y_send, y_recv, x_send, x_recv, c_send, c_recv, o_send, o_recv):
    at = place()
    other = moved(at, core=1 - at["core"])
    across = moved(at, y_lo=1 - at["y_lo"])
    forward = moved(at, x=(at["x"] + 1 + 2 * at["y_lo"]) % 4)
    backward = moved(at, x=(at["x"] + 3 - 2 * at["y_lo"]) % 4)
    greet((other, across, forward, backward))
    near_first = (at["core"] + at["y_lo"]) % 2 == 0

    def rows(piece):
        return pl.ds(piece * PIECE, PIECE)

    def to_across(piece):
        return remote(
            own.at[rows(piece)], out.at[1, rows(piece)], y_send.at[piece], y_recv.at[piece], across
        )

    def to_forward(piece):
        return remote(
            out.at[1, rows(piece)],
            out.at[2, rows(piece)],
            x_send.at[piece],
            x_recv.at[piece],
            forward,
        )

    def to_other(slot, piece):
        return remote(
            out.at[slot, rows(piece)],
            out.at[3, rows(piece)],
            c_send.at[piece],
            c_recv.at[piece],
            other,
        )

    for piece in range(PIECES):
        to_across(piece).start()
    swap = remote(own, out.at[0], o_send, o_recv, other)
    swap.start()
    for piece in range(PIECES):
        to_across(piece).wait_recv()
        to_forward(piece).start()

        @pl.when(near_first)
        def _():
            to_other(1, piece).start()

    for piece in range(PIECES):
        to_forward(piece).wait_recv()

        @pl.when(jnp.logical_not(near_first))
        def _():
            to_other(2, piece).start()

    for piece in range(PIECES):
        to_other(1, piece).wait_recv()
    swap.wait_recv()
    swap.wait_send()
    for piece in range(PIECES):
        to_across(piece).wait_send()
        to_forward(piece).wait_send()
        to_other(1, piece).wait_send()


def halo(own):
    dma = pltpu.SemaphoreType.DMA
    return pl.pallas_call(
        halo_kernel,
        out_shape=jax.ShapeDtypeStruct((4, BLOCK, WIDTH), jnp.bfloat16),
        in_specs=[pl.BlockSpec(memory_space=pltpu.VMEM)],
        out_specs=pl.BlockSpec(memory_space=pltpu.VMEM),
        scratch_shapes=[dma((PIECES,))] * 6 + [dma, dma],
        compiler_params=pltpu.CompilerParams(
            collective_id=0, has_side_effects=True, vmem_limit_bytes=VMEM_LIMIT
        ),
        name="halo",
    )(own)


def members_kernel(own, out, send, receive):
    member = lax.axis_index("member")
    mp = lax.axis_index("mp")
    count = 8
    partners = [((member + step) % count, mp) for step in range(1, count)]
    greet(partners)
    copies = [
        remote(own, out.at[step], send.at[step], receive.at[step], partner)
        for step, partner in enumerate(partners)
    ]
    for copy in copies:
        copy.start()
    for copy in copies:
        copy.wait()


def other_members(own):
    dma = pltpu.SemaphoreType.DMA
    return pl.pallas_call(
        members_kernel,
        out_shape=jax.ShapeDtypeStruct((7,) + own.shape, own.dtype),
        in_specs=[pl.BlockSpec(memory_space=pltpu.VMEM)],
        out_specs=pl.BlockSpec(memory_space=pltpu.VMEM),
        scratch_shapes=[dma((7,)), dma((7,))],
        compiler_params=pltpu.CompilerParams(
            collective_id=2, has_side_effects=True, vmem_limit_bytes=VMEM_LIMIT
        ),
        name="other_members",
    )(own)


def flip(bit, value):
    return (bit + value) % 2


def tail_kernel(
    terms_hbm,
    entries_hbm,
    dq_hbm,
    dk_hbm,
    dv_hbm,
    context_hbm,
    hidden_hbm,
    mid_hbm,
    forecast_hbm,
    out,
    halo_out,
    *scratch,
):
    parts = len(PARTS)
    first_in = scratch[:parts]
    later_in = scratch[parts : 2 * parts]
    total = scratch[2 * parts : 3 * parts]
    (
        last,
        last_in,
        grads,
        terms,
        entries,
        dq,
        dk,
        dv,
        context,
        hidden,
        mid,
        forecast,
        entries_t,
        narrow_t,
        near,
        far,
        cross_in,
        far_in,
        near_in,
        other_in,
        send,
        receive,
        last_send,
        last_recv,
        y_send,
        y_recv,
        x_send,
        x_recv,
        c_send,
        c_recv,
        o_send,
        o_recv,
        fetched,
    ) = scratch[3 * parts :]
    at = place()
    core = at["core"]
    x_bits = (at["x"] % 2, at["x"] // 2)
    z_bits = (at["z"] % 2, at["z"] // 2)
    y_bits = (at["y_lo"], at["y_hi"])
    other = moved(at, core=1 - core)

    fetches = [
        pltpu.make_async_copy(source, target, fetched.at[i])
        for i, (source, target) in enumerate(
            (
                (terms_hbm, terms),
                (context_hbm, context),
                (hidden_hbm, hidden),
                (entries_hbm, entries),
                (dq_hbm, dq),
                (mid_hbm, mid),
                (forecast_hbm, forecast),
                (dk_hbm, dk),
                (dv_hbm, dv),
            )
        )
    ]
    for fetch in fetches:
        fetch.start()

    def partner_of(link):
        low, high = 1, link // 3
        if link % 3 == 0:
            return moved(at, x=flip(x_bits[0], low) + 2 * flip(x_bits[1], high))
        if link % 3 == 1:
            return moved(at, y_lo=flip(y_bits[0], low), y_hi=flip(y_bits[1], high))
        return moved(at, z=flip(z_bits[0], low) + 2 * flip(z_bits[1], high))

    partners = [partner_of(link) for link in range(CLASSES)]
    greet([other] + partners)

    across = partners[1]
    backward = moved(at, x=(at["x"] + 3 - 2 * at["y_lo"]) % 4)
    near_first = (at["core"] + at["y_lo"]) % 2 == 0

    def rows(piece):
        return pl.ds(piece * PIECE, PIECE)

    def wide(ref, *index):
        return ref[index].astype(jnp.float32)

    def to_other(piece):
        return remote(
            terms.at[3, rows(piece)],
            cross_in.at[rows(piece)],
            c_send.at[piece],
            c_recv.at[piece],
            other,
        )

    def to_backward(piece):
        return remote(
            far.at[rows(piece)], far_in.at[rows(piece)], x_send.at[piece], x_recv.at[piece], backward
        )

    def to_across(piece):
        return remote(
            near.at[rows(piece)], near_in.at[rows(piece)], y_send.at[piece], y_recv.at[piece], across
        )

    swap = remote(terms.at[0], other_in, o_send, o_recv, other)

    def halo_start():
        fetches[0].wait()
        for piece in range(PIECES):
            to_other(piece).start()
        swap.start()

    def halo_first(pieces):
        for piece in pieces:
            to_other(piece).wait_recv()
            cross = wide(cross_in, rows(piece))
            far[rows(piece)] = (
                wide(terms, 2, rows(piece)) + jnp.where(near_first, 0.0, cross)
            ).astype(jnp.bfloat16)
            to_backward(piece).start()
            near[rows(piece)] = (
                wide(terms, 1, rows(piece)) + jnp.where(near_first, cross, 0.0)
            ).astype(jnp.bfloat16)

    def halo_second(pieces):
        for piece in pieces:
            to_backward(piece).wait_recv()
            near[rows(piece)] = (wide(near, rows(piece)) + wide(far_in, rows(piece))).astype(
                jnp.bfloat16
            )
            to_across(piece).start()

    def halo_end(pieces):
        for piece in pieces:
            to_across(piece).wait_recv()
            halo_out[rows(piece)] = wide(other_in, rows(piece)) + wide(near_in, rows(piece))

    def link_at(part, step):
        return ORDER[(part + step) % CLASSES]

    def tile_of(part, position):
        bits = {}
        for step in range(CLASSES):
            bits[link_at(part, step)] = (position // (TILES >> (step + 1))) % 2

        def shifted(own, axis):
            low = (own[0] + bits[axis] + bits[axis + 3]) % 2
            high = (own[1] + bits[axis + 3]) % 2
            return low, high

        x_low, x_high = shifted(x_bits, 0)
        y_low, y_high = shifted(y_bits, 1)
        z_low, z_high = shifted(z_bits, 2)
        return (z_low + 2 * z_high) * 16 + y_high * 8 + (x_low + 2 * x_high) * 2 + y_low

    def first_copy(part):
        start, size = PARTS[part]
        return remote(
            grads.at[1 - core, :, pl.ds(start, size)],
            first_in[part],
            send.at[part, 0],
            receive.at[part, 0],
            other,
        )

    def kept(step):
        return (TILES >> step) * TILE

    def later_copy(part, step):
        count = kept(step)
        return remote(
            total[part].at[pl.ds(count, count)],
            later_in[part].at[pl.ds(count, count)],
            send.at[part, step],
            receive.at[part, step],
            partners[link_at(part, step - 1)],
        )

    def product(left, right, begin, width, column, half):
        def tile(i, carry):
            here = pl.ds(pl.multiple_of(i * 256, 256), 256)
            grads[half, here, pl.ds(column, width)] = jnp.dot(
                left[here], right[:, pl.ds(begin, width)], preferred_element_type=jnp.float32
            ).astype(jnp.bfloat16)
            return carry

        lax.fori_loop(0, WIDTH // 256, tile, 0)

    def both_halves(left, right, column):
        for half in range(2):
            product(left, right, half * 512, 512, column, half)

    def merge_first(part):
        start, size = PARTS[part]
        first_copy(part).wait_recv()

        def merge(position, carry):
            source = pl.ds(pl.multiple_of(tile_of(part, position) * TILE, TILE), TILE)
            target = pl.ds(pl.multiple_of(position * TILE, TILE), TILE)
            summed = grads[core, source, pl.ds(start, size)].astype(jnp.float32) + first_in[part][
                source
            ].astype(jnp.float32)
            total[part][target] = summed.astype(jnp.bfloat16)
            return carry

        lax.fori_loop(TILES // 2, TILES, merge, 0, unroll=8)
        later_copy(part, 1).start()
        lax.fori_loop(0, TILES // 2, merge, 0, unroll=8)

    def merge_later(part, step):
        start, size = PARTS[part]
        count = kept(step)
        later_copy(part, step).wait_recv()
        if step < CLASSES:
            half = count // 2
            for begin in (half, 0):
                here = pl.ds(begin, half)
                arrived = later_in[part][pl.ds(count + begin, half)]
                total[part][here] = (
                    total[part][here].astype(jnp.float32) + arrived.astype(jnp.float32)
                ).astype(jnp.bfloat16)
                if begin == half:
                    later_copy(part, step + 1).start()
        else:
            final = wide(total[part], pl.ds(0, TILE)) + wide(later_in[part], pl.ds(TILE, TILE))
            last[:, :, pl.ds(start, size)] = final.reshape(2, 8, size)

    halo_start()
    fetches[1].wait()
    narrow_t[...] = context[...].T
    fetches[2].wait()
    both_halves(narrow_t, hidden, 0)
    first_copy(0).start()
    halo_first(range(PIECES))
    fetches[3].wait()
    for block in range(BAND):
        here = pl.ds(block * BLOCK, BLOCK)
        entries_t[:, here] = entries[here].T
    fetches[4].wait()
    both_halves(entries_t.at[:, pl.ds(0, BLOCK)], dq, 512)
    first_copy(1).start()
    merge_first(0)
    fetches[5].wait()
    narrow_t[...] = mid[...].T
    fetches[6].wait()
    product(narrow_t, forecast, 0, OUTV, 2048, 0)
    grads[1, :, pl.ds(2048, OUTV)] = jnp.zeros((WIDTH, OUTV), jnp.bfloat16)
    halo_second(range(0, 2))
    merge_first(1)
    fetches[7].wait()
    both_halves(entries_t, dk, 1024)
    first_copy(2).start()
    first_copy(3).start()
    halo_second(range(2, 4))
    merge_first(2)
    merge_first(3)
    fetches[8].wait()
    both_halves(entries_t, dv, 1536)
    first_copy(4).start()
    first_copy(5).start()
    merge_later(0, 1)
    merge_first(4)
    merge_first(5)
    halo_second(range(4, 6))
    merge_later(1, 1)
    merge_later(0, 2)
    halo_second(range(6, 8))
    merge_later(2, 1)
    merge_later(3, 1)
    merge_later(1, 2)
    merge_later(0, 3)
    merge_later(2, 2)
    merge_later(3, 2)
    merge_later(4, 1)
    merge_later(5, 1)
    for part, step in ((1, 3), (0, 4), (2, 3), (3, 3), (4, 2), (5, 2)):
        merge_later(part, step)
    swap.wait_recv()
    halo_end(range(0, 4))
    for part, step in ((1, 4), (0, 5), (2, 4), (3, 4), (4, 3), (5, 3)):
        merge_later(part, step)
    halo_end(range(4, 8))
    for part, step in ((1, 5), (0, 6), (2, 5), (3, 5), (4, 4), (5, 4)):
        merge_later(part, step)
    for part, step in ((1, 6), (2, 6), (3, 6), (4, 5), (5, 5), (4, 6), (5, 6)):
        merge_later(part, step)
    finish = remote(last.at[1 - core], last_in, last_send, last_recv, other)
    finish.start()
    out[core] = last[core]
    finish.wait()
    out[1 - core] = last_in[...]
    swap.wait_send()
    for piece in range(PIECES):
        to_other(piece).wait_send()
        to_backward(piece).wait_send()
        to_across(piece).wait_send()
    for part in range(parts):
        first_copy(part).wait_send()
        for step in range(1, CLASSES + 1):
            later_copy(part, step).wait_send()


def tail(terms, entries, dq, dk, dv, context, hidden, mid, forecast):
    dma = pltpu.SemaphoreType.DMA
    parts = len(PARTS)
    rows = TILES * TILE
    operands = (terms, entries, dq, dk, dv, context, hidden, mid, forecast)
    blocks = [pltpu.VMEM((rows, size), jnp.bfloat16) for _, size in PARTS]
    block = pltpu.VMEM((BLOCK, WIDTH), jnp.bfloat16)
    return pl.pallas_call(
        tail_kernel,
        out_shape=(
            jax.ShapeDtypeStruct((2, 8, HALF), jnp.float32),
            jax.ShapeDtypeStruct((BLOCK, WIDTH), jnp.float32),
        ),
        in_specs=[pl.BlockSpec(memory_space=pl.ANY)] * len(operands),
        out_specs=(
            pl.BlockSpec(memory_space=pltpu.VMEM),
            pl.BlockSpec(memory_space=pltpu.VMEM),
        ),
        scratch_shapes=blocks * 3
        + [
            pltpu.VMEM((2, 8, HALF), jnp.float32),
            pltpu.VMEM((8, HALF), jnp.float32),
            pltpu.VMEM((2, WIDTH, HALF), jnp.bfloat16),
        ]
        + [pltpu.VMEM(operand.shape, operand.dtype) for operand in operands]
        + [
            pltpu.VMEM((WIDTH, BAND * BLOCK), jnp.bfloat16),
            pltpu.VMEM((WIDTH, BLOCK), jnp.bfloat16),
        ]
        + [block] * 6
        + [dma((parts, CLASSES + 1)), dma((parts, CLASSES + 1)), dma, dma]
        + [dma((PIECES,))] * 6
        + [dma, dma, dma((len(operands),))],
        compiler_params=pltpu.CompilerParams(
            collective_id=1, has_side_effects=True, vmem_limit_bytes=TAIL_VMEM
        ),
        name="tail",
    )(*operands)


NT = (((1,), (1,)), ((), ()))


def head_mask(shape, head):
    lane = lax.broadcasted_iota(jnp.int32, shape, 1)
    return (lane // HEAD_DIM) == head


def attend_kernel(q_ref, k_ref, v_ref, context_ref, stat_ref):
    queries = q_ref[...] * jnp.bfloat16(0.125)
    keys = k_ref[...]
    values_t = v_ref[...].T
    sides = []
    for head in range(2):
        picked = jnp.where(head_mask(queries.shape, head), queries, jnp.bfloat16(0))
        scores = lax.dot_general(keys, picked, NT, preferred_element_type=jnp.float32)
        top = jnp.max(scores, axis=0, keepdims=True)
        powers = jnp.exp(scores - top)
        total = jnp.sum(powers, axis=0, keepdims=True)
        mixed = jnp.dot(
            values_t[head * HEAD_DIM : (head + 1) * HEAD_DIM],
            powers.astype(jnp.bfloat16),
            preferred_element_type=jnp.float32,
        )
        sides.append(mixed / total)
        stat_ref[0, head : head + 1] = top + jnp.log(total)
    context_ref[...] = jnp.concatenate(sides, axis=0).T.astype(jnp.bfloat16)


def attend(q, k, v):
    rows, keys = q.shape[0], k.shape[0]
    pair = 2 * HEAD_DIM
    return pl.pallas_call(
        attend_kernel,
        grid=(HEADS // 2,),
        out_shape=(
            jax.ShapeDtypeStruct((rows, WIDTH), jnp.bfloat16),
            jax.ShapeDtypeStruct((HEADS // 2, 2, rows), jnp.float32),
        ),
        in_specs=[
            pl.BlockSpec((rows, pair), lambda i: (0, i)),
            pl.BlockSpec((keys, pair), lambda i: (0, i)),
            pl.BlockSpec((keys, pair), lambda i: (0, i)),
        ],
        out_specs=(
            pl.BlockSpec((rows, pair), lambda i: (0, i)),
            pl.BlockSpec((1, 2, rows), lambda i: (i, 0, 0)),
        ),
        compiler_params=pltpu.CompilerParams(vmem_limit_bytes=VMEM_LIMIT),
        cost_estimate=pl.CostEstimate(
            flops=4 * rows * keys * WIDTH,
            bytes_accessed=2 * WIDTH * (2 * rows + 2 * keys),
            transcendentals=rows * keys * HEADS,
        ),
        name="attend",
    )(q, k, v)


def attend_back_kernel(q_ref, k_ref, v_ref, context_ref, grad_ref, stat_ref, dq_ref, dk_ref, dv_ref):
    queries = q_ref[...] * jnp.bfloat16(0.125)
    keys = k_ref[...]
    keys_t = keys.T
    values = v_ref[...]
    grads = grad_ref[...]
    products = (grads.astype(jnp.float32) * context_ref[...].astype(jnp.float32)).T
    sides = []
    grad_keys = jnp.zeros(keys.shape, jnp.float32)
    grad_values = jnp.zeros(keys.shape, jnp.float32)
    for head in range(2):
        mask = head_mask(queries.shape, head)
        picked = jnp.where(mask, queries, jnp.bfloat16(0))
        grad_here = jnp.where(mask, grads, jnp.bfloat16(0))
        inner = jnp.sum(products[head * HEAD_DIM : (head + 1) * HEAD_DIM], axis=0, keepdims=True)
        scores = lax.dot_general(keys, picked, NT, preferred_element_type=jnp.float32)
        probs = jnp.exp(scores - stat_ref[0, head : head + 1])
        grad_probs = lax.dot_general(values, grad_here, NT, preferred_element_type=jnp.float32)
        grad_scores = (probs * (grad_probs - inner)).astype(jnp.bfloat16)
        grad_values += jnp.dot(
            probs.astype(jnp.bfloat16), grad_here, preferred_element_type=jnp.float32
        )
        grad_keys += jnp.dot(grad_scores, picked, preferred_element_type=jnp.float32)
        sides.append(
            jnp.dot(
                keys_t[head * HEAD_DIM : (head + 1) * HEAD_DIM],
                grad_scores,
                preferred_element_type=jnp.float32,
            )
        )
    dq_ref[...] = (jnp.concatenate(sides, axis=0) * 0.125).T.astype(jnp.bfloat16)
    dk_ref[...] = grad_keys.astype(jnp.bfloat16)
    dv_ref[...] = grad_values.astype(jnp.bfloat16)


def attend_back(q, k, v, context, grad_context, stats):
    rows, keys = q.shape[0], k.shape[0]
    pair = 2 * HEAD_DIM
    row_block = pl.BlockSpec((rows, pair), lambda i: (0, i))
    key_block = pl.BlockSpec((keys, pair), lambda i: (0, i))
    return pl.pallas_call(
        attend_back_kernel,
        grid=(HEADS // 2,),
        out_shape=(
            jax.ShapeDtypeStruct((rows, WIDTH), jnp.bfloat16),
            jax.ShapeDtypeStruct((keys, WIDTH), jnp.bfloat16),
            jax.ShapeDtypeStruct((keys, WIDTH), jnp.bfloat16),
        ),
        in_specs=[
            row_block,
            key_block,
            key_block,
            row_block,
            row_block,
            pl.BlockSpec((1, 2, rows), lambda i: (i, 0, 0)),
        ],
        out_specs=(row_block, key_block, key_block),
        compiler_params=pltpu.CompilerParams(vmem_limit_bytes=VMEM_LIMIT),
        cost_estimate=pl.CostEstimate(
            flops=10 * rows * keys * WIDTH,
            bytes_accessed=2 * WIDTH * (4 * rows + 4 * keys),
            transcendentals=rows * keys * HEADS,
        ),
        name="attend_back",
    )(q, k, v, context, grad_context, stats)


def softened_derivative(difference):
    return difference * lax.rsqrt(difference * difference + smooth_square)


def dot(left, right):
    return jnp.dot(left, right, preferred_element_type=jnp.float32)


def per_device(
    grid_point_features,
    projection_weights_qkv,
    merging_projection,
    readout_weights_table,
    observed,
    cell_surface_share,
    band_offsets,
    latitude_order,
):
    members = lax.axis_size("member")
    own_rows = grid_point_features[0]
    at = place()
    block = lax.axis_index("mp")
    normed_in = layer_norm(own_rows.astype(jnp.float32)).astype(jnp.bfloat16)

    near, far = jnp.int32(1), jnp.int32(2)
    above = jnp.where(at["y_lo"] == 0, near, far)
    below = jnp.where(at["y_lo"] == 0, far, near)
    minus = jnp.where(at["core"] == 0, 3, 0)
    plus = jnp.where(at["core"] == 0, 0, 3)
    offsets = lax.dynamic_slice(band_offsets, (block, 1), (1, 2))[0]
    slots = jnp.where(
        offsets == -2, below, jnp.where(offsets == -1, minus, jnp.where(offsets == 1, plus, above))
    ).astype(jnp.int32)

    neighbours = halo(normed_in)
    chosen = [
        lax.dynamic_index_in_dim(neighbours, slots[i], 0, keepdims=False) for i in range(BAND - 1)
    ]
    entries = jnp.concatenate([normed_in] + chosen, axis=0)
    weights_q = projection_weights_qkv[:, :WIDTH]
    weights_k = projection_weights_qkv[:, WIDTH : 2 * WIDTH]
    weights_v = projection_weights_qkv[:, 2 * WIDTH :]
    q = dot(normed_in, weights_q).astype(jnp.bfloat16)
    k = dot(entries, weights_k).astype(jnp.bfloat16)
    v = dot(entries, weights_v).astype(jnp.bfloat16)
    context, stats = attend(q, k, v)

    hidden = (own_rows.astype(jnp.float32) + dot(context, merging_projection)).astype(jnp.bfloat16)
    normed_mid = layer_norm(hidden.astype(jnp.float32)).astype(jnp.bfloat16)
    predictions = dot(normed_mid, readout_weights_table)
    others = other_members(predictions.astype(jnp.bfloat16))
    target = observed[latitude_order[0]]
    spread = jnp.sum(
        softened_derivative(predictions[None] - others.astype(jnp.float32)), axis=0
    ) / (members * (members - 1))
    single = softened_derivative(predictions - target) / members
    grad_forecast = (cell_surface_share[:, None] * (single - spread)).astype(jnp.bfloat16)

    grad_mid = dot(grad_forecast, readout_weights_table.T)
    grad_hidden = jax.vjp(layer_norm, hidden.astype(jnp.float32))[1](grad_mid)[0]
    hidden_half = grad_hidden.astype(jnp.bfloat16)
    grad_context = dot(hidden_half, merging_projection.T).astype(jnp.bfloat16)
    dq, dk, dv = attend_back(q, k, v, context, grad_context, stats)

    grad_entries = dot(dk, weights_k.T) + dot(dv, weights_v.T)
    grad_own = grad_entries[:BLOCK] + dot(dq, weights_q.T)
    first = grad_entries[BLOCK : 2 * BLOCK].astype(jnp.bfloat16)
    second = grad_entries[2 * BLOCK :].astype(jnp.bfloat16)
    terms = jnp.stack(
        [
            jnp.where(slots[0] == slot, first, jnp.where(slots[1] == slot, second, jnp.bfloat16(0)))
            for slot in range(4)
        ]
    )
    summed, from_others = tail(
        terms, entries, dq, dk, dv, context, hidden_half, normed_mid, grad_forecast
    )
    grad_normed = grad_own + from_others
    feature_derivative = (
        grad_hidden + jax.vjp(layer_norm, own_rows.astype(jnp.float32))[1](grad_normed)[0]
    )

    both = [
        jnp.concatenate([summed[0, :, i * 512 : i * 512 + 512], summed[1, :, i * 512 : i * 512 + 512]], axis=1)
        for i in range(4)
    ]
    return (
        predictions[None],
        feature_derivative[None],
        jnp.concatenate(both[1:], axis=1),
        both[0],
        summed[0, :, 2048 : 2048 + OUTV],
    )


def solution(mesh):
    placed = (P("member", "mp", None), P(), P(), P(), P("mp", None), P("mp"), P(), P("mp", None))
    return jax.shard_map(
        per_device,
        mesh=mesh,
        in_specs=placed,
        out_specs=(
            P("member", "mp", None),
            P("member", "mp", None),
            P(("member", "mp"), None),
            P(("member", "mp"), None),
            P(("member", "mp"), None),
        ),
        check_vma=False,
    )
```

```python
import functools

import jax
import jax.numpy as jnp
from jax import lax
from jax.experimental import pallas as pl
from jax.experimental.pallas import tpu as pltpu
from jax.sharding import PartitionSpec as P

HEADS = 16
HEAD_DIM = 64
BLOCK = 512
WIDTH = 1024
OUTV = 128
BAND = 3

norm_epsilon = 1e-05
smooth_square = 0.0625

MESH = pl.DeviceIdType.MESH
VMEM_LIMIT = 56 * 1024 * 1024

PIECE = 64
PIECES = BLOCK // PIECE

HALF = 2176
PARTS = ((0, 384), (384, 384), (768, 384), (1152, 384), (1536, 384), (1920, 256))
TILE = 16
TILES = 64
CLASSES = 6
ORDER = (1, 3, 2, 4, 0, 5)
TAIL_VMEM = 60 * 1024 * 1024


def layer_norm(values):
    average = jnp.mean(values, axis=-1, keepdims=True)
    centred = values - average
    spread = jnp.mean(centred * centred, axis=-1, keepdims=True)
    return centred * lax.rsqrt(spread + norm_epsilon)


def softened_derivative(difference):
    return difference * lax.rsqrt(difference * difference + smooth_square)


def place():
    member = lax.axis_index("member")
    mp = lax.axis_index("mp")
    return {
        "z": member // 2,
        "y_hi": member % 2,
        "x": mp // 4,
        "y_lo": (mp // 2) % 2,
        "core": mp % 2,
    }


def device(at):
    return (at["z"] * 2 + at["y_hi"], at["x"] * 4 + at["y_lo"] * 2 + at["core"])


def moved(at, **changes):
    return device({**at, **changes})


def greet(partners):
    barrier = pltpu.get_barrier_semaphore()
    for partner in partners:
        pl.semaphore_signal(barrier, inc=1, device_id=partner, device_id_type=MESH)
    pl.semaphore_wait(barrier, len(partners))


def remote(source, target, send, receive, partner):
    return pltpu.make_async_remote_copy(
        src_ref=source,
        dst_ref=target,
        send_sem=send,
        recv_sem=receive,
        device_id=partner,
        device_id_type=MESH,
    )


def halo_kernel(own, out, y_send, y_recv, x_send, x_recv, c_send, c_recv, o_send, o_recv):
    at = place()
    other = moved(at, core=1 - at["core"])
    across = moved(at, y_lo=1 - at["y_lo"])
    forward = moved(at, x=(at["x"] + 1 + 2 * at["y_lo"]) % 4)
    backward = moved(at, x=(at["x"] + 3 - 2 * at["y_lo"]) % 4)
    greet((other, across, forward, backward))
    near_first = (at["core"] + at["y_lo"]) % 2 == 0

    def rows(piece):
        return pl.ds(piece * PIECE, PIECE)

    def to_across(piece):
        return remote(
            own.at[rows(piece)], out.at[1, rows(piece)], y_send.at[piece], y_recv.at[piece], across
        )

    def to_forward(piece):
        return remote(
            out.at[1, rows(piece)],
            out.at[2, rows(piece)],
            x_send.at[piece],
            x_recv.at[piece],
            forward,
        )

    def to_other(slot, piece):
        return remote(
            out.at[slot, rows(piece)],
            out.at[3, rows(piece)],
            c_send.at[piece],
            c_recv.at[piece],
            other,
        )

    for piece in range(PIECES):
        to_across(piece).start()
    swap = remote(own, out.at[0], o_send, o_recv, other)
    swap.start()
    for piece in range(PIECES):
        to_across(piece).wait_recv()
        to_forward(piece).start()

        @pl.when(near_first)
        def _():
            to_other(1, piece).start()

    for piece in range(PIECES):
        to_forward(piece).wait_recv()

        @pl.when(jnp.logical_not(near_first))
        def _():
            to_other(2, piece).start()

    for piece in range(PIECES):
        to_other(1, piece).wait_recv()
    swap.wait_recv()
    swap.wait_send()
    for piece in range(PIECES):
        to_across(piece).wait_send()
        to_forward(piece).wait_send()
        to_other(1, piece).wait_send()


def halo(own):
    dma = pltpu.SemaphoreType.DMA
    return pl.pallas_call(
        halo_kernel,
        out_shape=jax.ShapeDtypeStruct((4, BLOCK, WIDTH), jnp.bfloat16),
        in_specs=[pl.BlockSpec(memory_space=pltpu.VMEM)],
        out_specs=pl.BlockSpec(memory_space=pltpu.VMEM),
        scratch_shapes=[dma((PIECES,))] * 6 + [dma, dma],
        compiler_params=pltpu.CompilerParams(
            collective_id=0, has_side_effects=True, vmem_limit_bytes=VMEM_LIMIT
        ),
        name="halo",
    )(own)


def crps_kernel(predictions, target, share, out, halves, gathered, grads, send, receive, back_send, back_recv):
    member = lax.axis_index("member")
    mp = lax.axis_index("mp")
    count = 8
    size = BLOCK // count
    greet([((member + step) % count, mp) for step in range(1, count)])

    def slice_of(index):
        return pl.ds(pl.multiple_of(index * size, size), size)

    def outward(step):
        to = (member + step) % count
        return remote(
            halves.at[slice_of(to)], gathered.at[step], send.at[step], receive.at[step], (to, mp)
        )

    def homeward(step):
        to = (member + count - step) % count
        return remote(
            grads.at[step],
            out.at[slice_of(member)],
            back_send.at[step],
            back_recv.at[step],
            (to, mp),
        )

    halves[...] = predictions[...].astype(jnp.bfloat16)
    for step in range(1, count):
        outward(step).start()
    own = slice_of(member)
    truth = target[own]
    weight = share[own]
    gathered[0] = halves[own]
    for step in range(1, count):
        outward(step).wait_recv()
    each = [gathered[step].astype(jnp.float32) for step in range(count)]
    spread = [0.0] * count
    for one in range(count):
        for two in range(one + 1, count):
            slope = softened_derivative(each[one] - each[two])
            spread[one] = spread[one] + slope
            spread[two] = spread[two] - slope
    for step in range(count):
        single = softened_derivative(each[step] - truth) / count
        paired = spread[step] / (count * (count - 1))
        grads[step] = (weight * (single - paired)).astype(jnp.bfloat16)
        if step:
            homeward(step).start()
    out[own] = grads[0]
    for step in range(1, count):
        homeward(step).wait_recv()
    for step in range(1, count):
        outward(step).wait_send()
        homeward(step).wait_send()


def crps_grad(predictions, target, share):
    dma = pltpu.SemaphoreType.DMA
    size = BLOCK // 8
    return pl.pallas_call(
        crps_kernel,
        out_shape=jax.ShapeDtypeStruct(predictions.shape, jnp.bfloat16),
        in_specs=[pl.BlockSpec(memory_space=pltpu.VMEM)] * 3,
        out_specs=pl.BlockSpec(memory_space=pltpu.VMEM),
        scratch_shapes=[
            pltpu.VMEM((BLOCK, OUTV), jnp.bfloat16),
            pltpu.VMEM((8, size, OUTV), jnp.bfloat16),
            pltpu.VMEM((8, size, OUTV), jnp.bfloat16),
        ]
        + [dma((8,))] * 4,
        compiler_params=pltpu.CompilerParams(
            collective_id=2, has_side_effects=True, vmem_limit_bytes=VMEM_LIMIT
        ),
        name="crps_grad",
    )(predictions, target, share)


def flip(bit, value):
    return (bit + value) % 2


def tail_kernel(
    terms_hbm,
    entries_hbm,
    dq_hbm,
    dk_hbm,
    dv_hbm,
    context_hbm,
    hidden_hbm,
    mid_hbm,
    forecast_hbm,
    out,
    halo_out,
    *scratch,
):
    parts = len(PARTS)
    first_in = scratch[:parts]
    later_in = scratch[parts : 2 * parts]
    total = scratch[2 * parts : 3 * parts]
    (
        last,
        last_in,
        grads,
        terms,
        entries,
        dq,
        dk,
        dv,
        context,
        hidden,
        mid,
        forecast,
        entries_t,
        narrow_t,
        near,
        far,
        cross_in,
        far_in,
        near_in,
        other_in,
        send,
        receive,
        last_send,
        last_recv,
        y_send,
        y_recv,
        x_send,
        x_recv,
        c_send,
        c_recv,
        o_send,
        o_recv,
        fetched,
    ) = scratch[3 * parts :]
    at = place()
    core = at["core"]
    x_bits = (at["x"] % 2, at["x"] // 2)
    z_bits = (at["z"] % 2, at["z"] // 2)
    y_bits = (at["y_lo"], at["y_hi"])
    other = moved(at, core=1 - core)

    fetches = [
        pltpu.make_async_copy(source, target, fetched.at[i])
        for i, (source, target) in enumerate(
            (
                (terms_hbm, terms),
                (context_hbm, context),
                (hidden_hbm, hidden),
                (entries_hbm, entries),
                (dq_hbm, dq),
                (mid_hbm, mid),
                (forecast_hbm, forecast),
                (dk_hbm, dk),
                (dv_hbm, dv),
            )
        )
    ]
    for fetch in fetches:
        fetch.start()

    def partner_of(link):
        low, high = 1, link // 3
        if link % 3 == 0:
            return moved(at, x=flip(x_bits[0], low) + 2 * flip(x_bits[1], high))
        if link % 3 == 1:
            return moved(at, y_lo=flip(y_bits[0], low), y_hi=flip(y_bits[1], high))
        return moved(at, z=flip(z_bits[0], low) + 2 * flip(z_bits[1], high))

    partners = [partner_of(link) for link in range(CLASSES)]
    greet([other] + partners)

    across = partners[1]
    backward = moved(at, x=(at["x"] + 3 - 2 * at["y_lo"]) % 4)
    near_first = (at["core"] + at["y_lo"]) % 2 == 0

    def rows(piece):
        return pl.ds(piece * PIECE, PIECE)

    def wide(ref, *index):
        return ref[index].astype(jnp.float32)

    def to_other(piece):
        return remote(
            terms.at[3, rows(piece)],
            cross_in.at[rows(piece)],
            c_send.at[piece],
            c_recv.at[piece],
            other,
        )

    def to_backward(piece):
        return remote(
            far.at[rows(piece)], far_in.at[rows(piece)], x_send.at[piece], x_recv.at[piece], backward
        )

    def to_across(piece):
        return remote(
            near.at[rows(piece)], near_in.at[rows(piece)], y_send.at[piece], y_recv.at[piece], across
        )

    swap = remote(terms.at[0], other_in, o_send, o_recv, other)

    def halo_start():
        fetches[0].wait()
        for piece in range(PIECES):
            to_other(piece).start()
        swap.start()

    def over_tiles(piece, work):
        def tile(i, carry):
            work(pl.ds(pl.multiple_of(piece * PIECE + i * TILE, TILE), TILE))
            return carry

        lax.fori_loop(0, PIECE // TILE, tile, 0)

    def halo_first(pieces):
        for piece in pieces:
            to_other(piece).wait_recv()

            def add(here):
                cross = wide(cross_in, here)
                far[here] = (wide(terms, 2, here) + jnp.where(near_first, 0.0, cross)).astype(
                    jnp.bfloat16
                )
                near[here] = (wide(terms, 1, here) + jnp.where(near_first, cross, 0.0)).astype(
                    jnp.bfloat16
                )

            over_tiles(piece, add)
            to_backward(piece).start()

    def halo_second(pieces):
        for piece in pieces:
            to_backward(piece).wait_recv()

            def add(here):
                near[here] = (wide(near, here) + wide(far_in, here)).astype(jnp.bfloat16)

            over_tiles(piece, add)
            to_across(piece).start()

    def halo_end(pieces):
        for piece in pieces:
            to_across(piece).wait_recv()

            def add(here):
                halo_out[here] = wide(other_in, here) + wide(near_in, here)

            over_tiles(piece, add)

    def link_at(part, step):
        return ORDER[(part + step) % CLASSES]

    def tile_of(part, position):
        bits = {}
        for step in range(CLASSES):
            bits[link_at(part, step)] = (position // (TILES >> (step + 1))) % 2

        def shifted(own, axis):
            low = (own[0] + bits[axis] + bits[axis + 3]) % 2
            high = (own[1] + bits[axis + 3]) % 2
            return low, high

        x_low, x_high = shifted(x_bits, 0)
        y_low, y_high = shifted(y_bits, 1)
        z_low, z_high = shifted(z_bits, 2)
        return (z_low + 2 * z_high) * 16 + y_high * 8 + (x_low + 2 * x_high) * 2 + y_low

    def first_copy(part):
        start, size = PARTS[part]
        return remote(
            grads.at[1 - core, :, pl.ds(start, size)],
            first_in[part],
            send.at[part, 0],
            receive.at[part, 0],
            other,
        )

    def kept(step):
        return (TILES >> step) * TILE

    def later_copy(part, step):
        count = kept(step)
        return remote(
            total[part].at[pl.ds(count, count)],
            later_in[part].at[pl.ds(count, count)],
            send.at[part, step],
            receive.at[part, step],
            partners[link_at(part, step - 1)],
        )

    def product(left, right, begin, width, column, half):
        def tile(i, carry):
            here = pl.ds(pl.multiple_of(i * 256, 256), 256)
            grads[half, here, pl.ds(column, width)] = jnp.dot(
                left[here], right[:, pl.ds(begin, width)], preferred_element_type=jnp.float32
            ).astype(jnp.bfloat16)
            return carry

        lax.fori_loop(0, WIDTH // 256, tile, 0)

    def both_halves(left, right, column):
        for half in range(2):
            product(left, right, half * 512, 512, column, half)

    def merge_first(part):
        start, size = PARTS[part]
        first_copy(part).wait_recv()

        def merge(position, carry):
            source = pl.ds(pl.multiple_of(tile_of(part, position) * TILE, TILE), TILE)
            target = pl.ds(pl.multiple_of(position * TILE, TILE), TILE)
            summed = grads[core, source, pl.ds(start, size)].astype(jnp.float32) + first_in[part][
                source
            ].astype(jnp.float32)
            total[part][target] = summed.astype(jnp.bfloat16)
            return carry

        lax.fori_loop(TILES // 2, TILES, merge, 0, unroll=8)
        later_copy(part, 1).start()
        lax.fori_loop(0, TILES // 2, merge, 0, unroll=8)

    def merge_later(part, step):
        start, size = PARTS[part]
        count = kept(step)
        later_copy(part, step).wait_recv()
        if step < CLASSES:
            half = count // 2
            tiles = half // TILE

            def merge(position, carry):
                here = pl.ds(pl.multiple_of(position * TILE, TILE), TILE)
                there = pl.ds(pl.multiple_of(position * TILE + count, TILE), TILE)
                total[part][here] = (
                    wide(total[part], here) + wide(later_in[part], there)
                ).astype(jnp.bfloat16)
                return carry

            lax.fori_loop(tiles, 2 * tiles, merge, 0, unroll=min(tiles, 8))
            later_copy(part, step + 1).start()
            lax.fori_loop(0, tiles, merge, 0, unroll=min(tiles, 8))
        else:
            final = wide(total[part], pl.ds(0, TILE)) + wide(later_in[part], pl.ds(TILE, TILE))
            last[:, :, pl.ds(start, size)] = final.reshape(2, 8, size)

    halo_start()
    fetches[1].wait()
    narrow_t[...] = context[...].T
    fetches[2].wait()
    both_halves(narrow_t, hidden, 0)
    first_copy(0).start()
    halo_first(range(PIECES))
    fetches[3].wait()
    for block in range(BAND):
        here = pl.ds(block * BLOCK, BLOCK)
        entries_t[:, here] = entries[here].T
    fetches[4].wait()
    both_halves(entries_t.at[:, pl.ds(0, BLOCK)], dq, 512)
    first_copy(1).start()
    merge_first(0)
    fetches[5].wait()
    narrow_t[...] = mid[...].T
    fetches[6].wait()
    product(narrow_t, forecast, 0, OUTV, 2048, 0)
    grads[1, :, pl.ds(2048, OUTV)] = jnp.zeros((WIDTH, OUTV), jnp.bfloat16)
    halo_second(range(0, 2))
    merge_first(1)
    fetches[7].wait()
    both_halves(entries_t, dk, 1024)
    first_copy(2).start()
    first_copy(3).start()
    halo_second(range(2, 4))
    merge_first(2)
    merge_first(3)
    fetches[8].wait()
    both_halves(entries_t, dv, 1536)
    first_copy(4).start()
    first_copy(5).start()
    merge_later(0, 1)
    merge_first(4)
    merge_first(5)
    halo_second(range(4, 6))
    merge_later(1, 1)
    merge_later(0, 2)
    halo_second(range(6, 8))
    merge_later(2, 1)
    merge_later(3, 1)
    merge_later(1, 2)
    merge_later(0, 3)
    merge_later(2, 2)
    merge_later(3, 2)
    merge_later(4, 1)
    merge_later(5, 1)
    for part, step in ((1, 3), (0, 4), (2, 3), (3, 3), (4, 2), (5, 2)):
        merge_later(part, step)
    swap.wait_recv()
    halo_end(range(0, 4))
    for part, step in ((1, 4), (0, 5), (2, 4), (3, 4), (4, 3), (5, 3)):
        merge_later(part, step)
    halo_end(range(4, 8))
    for part, step in ((1, 5), (0, 6), (2, 5), (3, 5), (4, 4), (5, 4)):
        merge_later(part, step)
    for part, step in ((1, 6), (2, 6), (3, 6), (4, 5), (5, 5), (4, 6), (5, 6)):
        merge_later(part, step)
    finish = remote(last.at[1 - core], last_in, last_send, last_recv, other)
    finish.start()
    out[core] = last[core]
    finish.wait()
    out[1 - core] = last_in[...]
    swap.wait_send()
    for piece in range(PIECES):
        to_other(piece).wait_send()
        to_backward(piece).wait_send()
        to_across(piece).wait_send()
    for part in range(parts):
        first_copy(part).wait_send()
        for step in range(1, CLASSES + 1):
            later_copy(part, step).wait_send()


def tail(terms, entries, dq, dk, dv, context, hidden, mid, forecast):
    dma = pltpu.SemaphoreType.DMA
    parts = len(PARTS)
    rows = TILES * TILE
    operands = (terms, entries, dq, dk, dv, context, hidden, mid, forecast)
    blocks = [pltpu.VMEM((rows, size), jnp.bfloat16) for _, size in PARTS]
    block = pltpu.VMEM((BLOCK, WIDTH), jnp.bfloat16)
    return pl.pallas_call(
        tail_kernel,
        out_shape=(
            jax.ShapeDtypeStruct((2, 8, HALF), jnp.float32),
            jax.ShapeDtypeStruct((BLOCK, WIDTH), jnp.float32),
        ),
        in_specs=[pl.BlockSpec(memory_space=pl.ANY)] * len(operands),
        out_specs=(
            pl.BlockSpec(memory_space=pltpu.VMEM),
            pl.BlockSpec(memory_space=pltpu.VMEM),
        ),
        scratch_shapes=blocks * 3
        + [
            pltpu.VMEM((2, 8, HALF), jnp.float32),
            pltpu.VMEM((8, HALF), jnp.float32),
            pltpu.VMEM((2, WIDTH, HALF), jnp.bfloat16),
        ]
        + [pltpu.VMEM(operand.shape, operand.dtype) for operand in operands]
        + [
            pltpu.VMEM((WIDTH, BAND * BLOCK), jnp.bfloat16),
            pltpu.VMEM((WIDTH, BLOCK), jnp.bfloat16),
        ]
        + [block] * 6
        + [dma((parts, CLASSES + 1)), dma((parts, CLASSES + 1)), dma, dma]
        + [dma((PIECES,))] * 6
        + [dma, dma, dma((len(operands),))],
        compiler_params=pltpu.CompilerParams(
            collective_id=1, has_side_effects=True, vmem_limit_bytes=TAIL_VMEM
        ),
        name="tail",
    )(*operands)


NT = (((1,), (1,)), ((), ()))


def head_mask(shape, head):
    lane = lax.broadcasted_iota(jnp.int32, shape, 1)
    return (lane // HEAD_DIM) == head


def attend_kernel(q_ref, k_ref, v_ref, context_ref, stat_ref):
    queries = q_ref[...] * jnp.bfloat16(0.125)
    keys = k_ref[...]
    values_t = v_ref[...].T
    sides = []
    for head in range(2):
        picked = jnp.where(head_mask(queries.shape, head), queries, jnp.bfloat16(0))
        scores = lax.dot_general(keys, picked, NT, preferred_element_type=jnp.float32)
        top = jnp.max(scores, axis=0, keepdims=True)
        powers = jnp.exp(scores - top)
        total = jnp.sum(powers, axis=0, keepdims=True)
        mixed = jnp.dot(
            values_t[head * HEAD_DIM : (head + 1) * HEAD_DIM],
            powers.astype(jnp.bfloat16),
            preferred_element_type=jnp.float32,
        )
        sides.append(mixed / total)
        stat_ref[0, head : head + 1] = top + jnp.log(total)
    context_ref[...] = jnp.concatenate(sides, axis=0).T.astype(jnp.bfloat16)


def attend(q, k, v):
    rows, keys = q.shape[0], k.shape[0]
    pair = 2 * HEAD_DIM
    return pl.pallas_call(
        attend_kernel,
        grid=(HEADS // 2,),
        out_shape=(
            jax.ShapeDtypeStruct((rows, WIDTH), jnp.bfloat16),
            jax.ShapeDtypeStruct((HEADS // 2, 2, rows), jnp.float32),
        ),
        in_specs=[
            pl.BlockSpec((rows, pair), lambda i: (0, i)),
            pl.BlockSpec((keys, pair), lambda i: (0, i)),
            pl.BlockSpec((keys, pair), lambda i: (0, i)),
        ],
        out_specs=(
            pl.BlockSpec((rows, pair), lambda i: (0, i)),
            pl.BlockSpec((1, 2, rows), lambda i: (i, 0, 0)),
        ),
        compiler_params=pltpu.CompilerParams(vmem_limit_bytes=VMEM_LIMIT),
        cost_estimate=pl.CostEstimate(
            flops=4 * rows * keys * WIDTH,
            bytes_accessed=2 * WIDTH * (2 * rows + 2 * keys),
            transcendentals=rows * keys * HEADS,
        ),
        name="attend",
    )(q, k, v)


def attend_back_kernel(q_ref, k_ref, v_ref, context_ref, grad_ref, stat_ref, dq_ref, dk_ref, dv_ref):
    queries = q_ref[...] * jnp.bfloat16(0.125)
    keys = k_ref[...]
    keys_t = keys.T
    values = v_ref[...]
    grads = grad_ref[...]
    products = (grads.astype(jnp.float32) * context_ref[...].astype(jnp.float32)).T
    sides = []
    grad_keys = jnp.zeros(keys.shape, jnp.float32)
    grad_values = jnp.zeros(keys.shape, jnp.float32)
    for head in range(2):
        mask = head_mask(queries.shape, head)
        picked = jnp.where(mask, queries, jnp.bfloat16(0))
        grad_here = jnp.where(mask, grads, jnp.bfloat16(0))
        inner = jnp.sum(products[head * HEAD_DIM : (head + 1) * HEAD_DIM], axis=0, keepdims=True)
        scores = lax.dot_general(keys, picked, NT, preferred_element_type=jnp.float32)
        probs = jnp.exp(scores - stat_ref[0, head : head + 1])
        grad_probs = lax.dot_general(values, grad_here, NT, preferred_element_type=jnp.float32)
        grad_scores = (probs * (grad_probs - inner)).astype(jnp.bfloat16)
        grad_values += jnp.dot(
            probs.astype(jnp.bfloat16), grad_here, preferred_element_type=jnp.float32
        )
        grad_keys += jnp.dot(grad_scores, picked, preferred_element_type=jnp.float32)
        sides.append(
            jnp.dot(
                keys_t[head * HEAD_DIM : (head + 1) * HEAD_DIM],
                grad_scores,
                preferred_element_type=jnp.float32,
            )
        )
    dq_ref[...] = (jnp.concatenate(sides, axis=0) * 0.125).T.astype(jnp.bfloat16)
    dk_ref[...] = grad_keys.astype(jnp.bfloat16)
    dv_ref[...] = grad_values.astype(jnp.bfloat16)


def attend_back(q, k, v, context, grad_context, stats):
    rows, keys = q.shape[0], k.shape[0]
    pair = 2 * HEAD_DIM
    row_block = pl.BlockSpec((rows, pair), lambda i: (0, i))
    key_block = pl.BlockSpec((keys, pair), lambda i: (0, i))
    return pl.pallas_call(
        attend_back_kernel,
        grid=(HEADS // 2,),
        out_shape=(
            jax.ShapeDtypeStruct((rows, WIDTH), jnp.bfloat16),
            jax.ShapeDtypeStruct((keys, WIDTH), jnp.bfloat16),
            jax.ShapeDtypeStruct((keys, WIDTH), jnp.bfloat16),
        ),
        in_specs=[
            row_block,
            key_block,
            key_block,
            row_block,
            row_block,
            pl.BlockSpec((1, 2, rows), lambda i: (i, 0, 0)),
        ],
        out_specs=(row_block, key_block, key_block),
        compiler_params=pltpu.CompilerParams(vmem_limit_bytes=VMEM_LIMIT),
        cost_estimate=pl.CostEstimate(
            flops=10 * rows * keys * WIDTH,
            bytes_accessed=2 * WIDTH * (4 * rows + 4 * keys),
            transcendentals=rows * keys * HEADS,
        ),
        name="attend_back",
    )(q, k, v, context, grad_context, stats)


def dot(left, right):
    return jnp.dot(left, right, preferred_element_type=jnp.float32)


def per_device(
    grid_point_features,
    projection_weights_qkv,
    merging_projection,
    readout_weights_table,
    observed,
    cell_surface_share,
    band_offsets,
    latitude_order,
):
    own_rows = grid_point_features[0]
    at = place()
    block = lax.axis_index("mp")
    normed_in = layer_norm(own_rows.astype(jnp.float32)).astype(jnp.bfloat16)

    near, far = jnp.int32(1), jnp.int32(2)
    above = jnp.where(at["y_lo"] == 0, near, far)
    below = jnp.where(at["y_lo"] == 0, far, near)
    minus = jnp.where(at["core"] == 0, 3, 0)
    plus = jnp.where(at["core"] == 0, 0, 3)
    offsets = lax.dynamic_slice(band_offsets, (block, 1), (1, 2))[0]
    slots = jnp.where(
        offsets == -2, below, jnp.where(offsets == -1, minus, jnp.where(offsets == 1, plus, above))
    ).astype(jnp.int32)

    neighbours = halo(normed_in)
    chosen = [
        lax.dynamic_index_in_dim(neighbours, slots[i], 0, keepdims=False) for i in range(BAND - 1)
    ]
    entries = jnp.concatenate([normed_in] + chosen, axis=0)
    weights_q = projection_weights_qkv[:, :WIDTH]
    weights_k = projection_weights_qkv[:, WIDTH : 2 * WIDTH]
    weights_v = projection_weights_qkv[:, 2 * WIDTH :]
    q = dot(normed_in, weights_q).astype(jnp.bfloat16)
    k = dot(entries, weights_k).astype(jnp.bfloat16)
    v = dot(entries, weights_v).astype(jnp.bfloat16)
    context, stats = attend(q, k, v)

    hidden = (own_rows.astype(jnp.float32) + dot(context, merging_projection)).astype(jnp.bfloat16)
    normed_mid = layer_norm(hidden.astype(jnp.float32)).astype(jnp.bfloat16)
    predictions = dot(normed_mid, readout_weights_table)
    target = observed[latitude_order[0]]
    grad_forecast = crps_grad(predictions, target, cell_surface_share[:, None])

    grad_mid = dot(grad_forecast, readout_weights_table.T)
    grad_hidden = jax.vjp(layer_norm, hidden.astype(jnp.float32))[1](grad_mid)[0]
    hidden_half = grad_hidden.astype(jnp.bfloat16)
    grad_context = dot(hidden_half, merging_projection.T).astype(jnp.bfloat16)
    dq, dk, dv = attend_back(q, k, v, context, grad_context, stats)

    grad_entries = dot(dk, weights_k.T) + dot(dv, weights_v.T)
    grad_own = grad_entries[:BLOCK] + dot(dq, weights_q.T)
    first = grad_entries[BLOCK : 2 * BLOCK].astype(jnp.bfloat16)
    second = grad_entries[2 * BLOCK :].astype(jnp.bfloat16)
    terms = jnp.stack(
        [
            jnp.where(slots[0] == slot, first, jnp.where(slots[1] == slot, second, jnp.bfloat16(0)))
            for slot in range(4)
        ]
    )
    summed, from_others = tail(
        terms, entries, dq, dk, dv, context, hidden_half, normed_mid, grad_forecast
    )
    grad_normed = grad_own + from_others
    feature_derivative = (
        grad_hidden + jax.vjp(layer_norm, own_rows.astype(jnp.float32))[1](grad_normed)[0]
    )

    both = [
        jnp.concatenate([summed[0, :, i * 512 : i * 512 + 512], summed[1, :, i * 512 : i * 512 + 512]], axis=1)
        for i in range(4)
    ]
    return (
        predictions[None],
        feature_derivative[None],
        jnp.concatenate(both[1:], axis=1),
        both[0],
        summed[0, :, 2048 : 2048 + OUTV],
    )


def solution(mesh):
    placed = (P("member", "mp", None), P(), P(), P(), P("mp", None), P("mp"), P(), P("mp", None))
    return jax.shard_map(
        per_device,
        mesh=mesh,
        in_specs=placed,
        out_specs=(
            P("member", "mp", None),
            P("member", "mp", None),
            P(("member", "mp"), None),
            P(("member", "mp"), None),
            P(("member", "mp"), None),
        ),
        check_vma=False,
    )
```

```python
import functools

import jax
import jax.numpy as jnp
from jax import lax
from jax.experimental import pallas as pl
from jax.experimental.pallas import tpu as pltpu
from jax.sharding import PartitionSpec as P

HEADS = 16
HEAD_DIM = 64
BLOCK = 512
WIDTH = 1024
OUTV = 128
BAND = 3

norm_epsilon = 1e-05
smooth_square = 0.0625

MESH = pl.DeviceIdType.MESH
VMEM_LIMIT = 56 * 1024 * 1024

PIECE = 64
PIECES = BLOCK // PIECE

HALF = 2176
PARTS = ((0, 384), (384, 256), (640, 256), (896, 256), (1152, 256)) + tuple(
    (1408 + 128 * i, 128) for i in range(6)
)
TILE = 16
TILES = 64
CLASSES = 6
ORDER = (1, 3, 2, 4, 0, 5)
FIRST_LINK = (2, 5, 1, 3, 4, 0, 1, 2, 3, 4, 5)
TAIL_VMEM = 60 * 1024 * 1024


def layer_norm(values):
    average = jnp.mean(values, axis=-1, keepdims=True)
    centred = values - average
    spread = jnp.mean(centred * centred, axis=-1, keepdims=True)
    return centred * lax.rsqrt(spread + norm_epsilon)


def softened_derivative(difference):
    return difference * lax.rsqrt(difference * difference + smooth_square)


NT = (((1,), (1,)), ((), ()))


def head_mask(shape, head):
    lane = lax.broadcasted_iota(jnp.int32, shape, 1)
    return (lane // HEAD_DIM) == head


def place():
    member = lax.axis_index("member")
    mp = lax.axis_index("mp")
    return {
        "z": member // 2,
        "y_hi": member % 2,
        "x": mp // 4,
        "y_lo": (mp // 2) % 2,
        "core": mp % 2,
    }


def device(at):
    return (at["z"] * 2 + at["y_hi"], at["x"] * 4 + at["y_lo"] * 2 + at["core"])


def moved(at, **changes):
    return device({**at, **changes})


def greet(partners):
    barrier = pltpu.get_barrier_semaphore()
    for partner in partners:
        pl.semaphore_signal(barrier, inc=1, device_id=partner, device_id_type=MESH)
    pl.semaphore_wait(barrier, len(partners))


def remote(source, target, send, receive, partner):
    return pltpu.make_async_remote_copy(
        src_ref=source,
        dst_ref=target,
        send_sem=send,
        recv_sem=receive,
        device_id=partner,
        device_id_type=MESH,
    )


def halo_kernel(own, out, y_send, y_recv, x_send, x_recv, c_send, c_recv, o_send, o_recv):
    at = place()
    other = moved(at, core=1 - at["core"])
    across = moved(at, y_lo=1 - at["y_lo"])
    forward = moved(at, x=(at["x"] + 1 + 2 * at["y_lo"]) % 4)
    backward = moved(at, x=(at["x"] + 3 - 2 * at["y_lo"]) % 4)
    greet((other, across, forward, backward))
    near_first = (at["core"] + at["y_lo"]) % 2 == 0

    def rows(piece):
        return pl.ds(piece * PIECE, PIECE)

    def to_across(piece):
        return remote(
            own.at[rows(piece)], out.at[1, rows(piece)], y_send.at[piece], y_recv.at[piece], across
        )

    def to_forward(piece):
        return remote(
            out.at[1, rows(piece)],
            out.at[2, rows(piece)],
            x_send.at[piece],
            x_recv.at[piece],
            forward,
        )

    def to_other(slot, piece):
        return remote(
            out.at[slot, rows(piece)],
            out.at[3, rows(piece)],
            c_send.at[piece],
            c_recv.at[piece],
            other,
        )

    for piece in range(PIECES):
        to_across(piece).start()
    swap = remote(own, out.at[0], o_send, o_recv, other)
    swap.start()
    for piece in range(PIECES):
        to_across(piece).wait_recv()
        to_forward(piece).start()

        @pl.when(near_first)
        def _():
            to_other(1, piece).start()

    for piece in range(PIECES):
        to_forward(piece).wait_recv()

        @pl.when(jnp.logical_not(near_first))
        def _():
            to_other(2, piece).start()

    for piece in range(PIECES):
        to_other(1, piece).wait_recv()
    swap.wait_recv()
    swap.wait_send()
    for piece in range(PIECES):
        to_across(piece).wait_send()
        to_forward(piece).wait_send()
        to_other(1, piece).wait_send()


def halo(own):
    dma = pltpu.SemaphoreType.DMA
    return pl.pallas_call(
        halo_kernel,
        out_shape=jax.ShapeDtypeStruct((4, BLOCK, WIDTH), jnp.bfloat16),
        in_specs=[pl.BlockSpec(memory_space=pltpu.VMEM)],
        out_specs=pl.BlockSpec(memory_space=pltpu.VMEM),
        scratch_shapes=[dma((PIECES,))] * 6 + [dma, dma],
        compiler_params=pltpu.CompilerParams(
            collective_id=0, has_side_effects=True, vmem_limit_bytes=VMEM_LIMIT
        ),
        name="halo",
    )(own)


def crps_kernel(predictions, target, share, out, halves, gathered, grads, send, receive, back_send, back_recv):
    member = lax.axis_index("member")
    mp = lax.axis_index("mp")
    count = 8
    size = BLOCK // count
    greet([((member + step) % count, mp) for step in range(1, count)])

    def slice_of(index):
        return pl.ds(pl.multiple_of(index * size, size), size)

    def outward(step):
        to = (member + step) % count
        return remote(
            halves.at[slice_of(to)], gathered.at[step], send.at[step], receive.at[step], (to, mp)
        )

    def homeward(step):
        to = (member + count - step) % count
        return remote(
            grads.at[step],
            out.at[slice_of(member)],
            back_send.at[step],
            back_recv.at[step],
            (to, mp),
        )

    halves[...] = predictions[...].astype(jnp.bfloat16)
    for step in range(1, count):
        outward(step).start()
    own = slice_of(member)
    truth = target[own]
    weight = share[own]
    gathered[0] = halves[own]
    for step in range(1, count):
        outward(step).wait_recv()
    each = [gathered[step].astype(jnp.float32) for step in range(count)]
    spread = [0.0] * count
    for one in range(count):
        for two in range(one + 1, count):
            slope = softened_derivative(each[one] - each[two])
            spread[one] = spread[one] + slope
            spread[two] = spread[two] - slope
    for step in range(count):
        single = softened_derivative(each[step] - truth) / count
        paired = spread[step] / (count * (count - 1))
        grads[step] = (weight * (single - paired)).astype(jnp.bfloat16)
        if step:
            homeward(step).start()
    out[own] = grads[0]
    for step in range(1, count):
        homeward(step).wait_recv()
    for step in range(1, count):
        outward(step).wait_send()
        homeward(step).wait_send()


def crps_grad(predictions, target, share):
    dma = pltpu.SemaphoreType.DMA
    size = BLOCK // 8
    return pl.pallas_call(
        crps_kernel,
        out_shape=jax.ShapeDtypeStruct(predictions.shape, jnp.bfloat16),
        in_specs=[pl.BlockSpec(memory_space=pltpu.VMEM)] * 3,
        out_specs=pl.BlockSpec(memory_space=pltpu.VMEM),
        scratch_shapes=[
            pltpu.VMEM((BLOCK, OUTV), jnp.bfloat16),
            pltpu.VMEM((8, size, OUTV), jnp.bfloat16),
            pltpu.VMEM((8, size, OUTV), jnp.bfloat16),
        ]
        + [dma((8,))] * 4,
        compiler_params=pltpu.CompilerParams(
            collective_id=2, has_side_effects=True, vmem_limit_bytes=VMEM_LIMIT
        ),
        name="crps_grad",
    )(predictions, target, share)


def flip(bit, value):
    return (bit + value) % 2


def tail_kernel(
    terms_hbm,
    entries_hbm,
    context_hbm,
    hidden_hbm,
    mid_hbm,
    forecast_hbm,
    q_hbm,
    k_hbm,
    v_hbm,
    grad_context_hbm,
    stats_hbm,
    dq_hbm,
    dk_hbm,
    dv_hbm,
    out,
    halo_out,
    dq_own,
    dk_own,
    dv_own,
    *scratch,
):
    parts = len(PARTS)
    first_in = scratch[:parts]
    later_in = scratch[parts : 2 * parts]
    total = scratch[2 * parts : 3 * parts]
    (
        last,
        last_in,
        grads,
        terms,
        context,
        hidden,
        mid,
        forecast,
        q,
        k,
        v,
        grad_context,
        stats,
        dq,
        dk,
        dv,
        entries_t,
        narrow_t,
        cross_in,
        far_in,
        near_in,
        other_in,
        send,
        receive,
        last_send,
        last_recv,
        y_send,
        y_recv,
        x_send,
        x_recv,
        c_send,
        c_recv,
        o_send,
        o_recv,
        fetched,
    ) = scratch[3 * parts :]
    at = place()
    core = at["core"]
    x_bits = (at["x"] % 2, at["x"] // 2)
    z_bits = (at["z"] % 2, at["z"] // 2)
    y_bits = (at["y_lo"], at["y_hi"])
    other = moved(at, core=1 - core)

    landing = (
        grads.at[0, pl.ds(0, BLOCK), pl.ds(1024, WIDTH)],
        grads.at[1, pl.ds(0, 2 * BLOCK), pl.ds(1024, WIDTH)],
    )
    fetches = [
        pltpu.make_async_copy(source, target, fetched.at[i])
        for i, (source, target) in enumerate(
            (
                (terms_hbm, terms),
                (context_hbm, context),
                (hidden_hbm, hidden),
                (mid_hbm, mid),
                (forecast_hbm, forecast),
                (entries_hbm.at[pl.ds(0, BLOCK)], landing[0]),
                (entries_hbm.at[pl.ds(BLOCK, 2 * BLOCK)], landing[1]),
                (q_hbm, q),
                (k_hbm, k),
                (v_hbm, v),
                (grad_context_hbm, grad_context),
                (stats_hbm, stats),
                (dq_hbm, dq),
                (dk_hbm, dk),
                (dv_hbm, dv),
            )
        )
    ]
    for fetch in fetches:
        fetch.start()

    def partner_of(link):
        low, high = 1, link // 3
        if link % 3 == 0:
            return moved(at, x=flip(x_bits[0], low) + 2 * flip(x_bits[1], high))
        if link % 3 == 1:
            return moved(at, y_lo=flip(y_bits[0], low), y_hi=flip(y_bits[1], high))
        return moved(at, z=flip(z_bits[0], low) + 2 * flip(z_bits[1], high))

    partners = [partner_of(link) for link in range(CLASSES)]
    greet([other] + partners)

    across = partners[1]
    backward = moved(at, x=(at["x"] + 3 - 2 * at["y_lo"]) % 4)
    near_first = (at["core"] + at["y_lo"]) % 2 == 0

    def rows(piece):
        return pl.ds(piece * PIECE, PIECE)

    def wide(ref, *index):
        return ref[index].astype(jnp.float32)

    def to_other(piece):
        return remote(
            terms.at[3, rows(piece)],
            cross_in.at[rows(piece)],
            c_send.at[piece],
            c_recv.at[piece],
            other,
        )

    def to_backward(piece):
        return remote(
            terms.at[2, rows(piece)], far_in.at[rows(piece)], x_send.at[piece], x_recv.at[piece], backward
        )

    def to_across(piece):
        return remote(
            terms.at[1, rows(piece)], near_in.at[rows(piece)], y_send.at[piece], y_recv.at[piece], across
        )

    swap = remote(terms.at[0], other_in, o_send, o_recv, other)

    def halo_start():
        fetches[0].wait()
        for piece in range(PIECES):
            to_other(piece).start()
        swap.start()

    def over_tiles(piece, work):
        def tile(i, carry):
            work(pl.ds(pl.multiple_of(piece * PIECE + i * TILE, TILE), TILE))
            return carry

        lax.fori_loop(0, PIECE // TILE, tile, 0)

    def halo_first(pieces):
        for piece in pieces:
            to_other(piece).wait_recv()

            def add(here):
                cross = wide(cross_in, here)
                terms[2, here] = (wide(terms, 2, here) + jnp.where(near_first, 0.0, cross)).astype(
                    jnp.bfloat16
                )
                terms[1, here] = (wide(terms, 1, here) + jnp.where(near_first, cross, 0.0)).astype(
                    jnp.bfloat16
                )

            over_tiles(piece, add)
            to_backward(piece).start()

    def halo_second(pieces):
        for piece in pieces:
            to_backward(piece).wait_recv()

            def add(here):
                terms[1, here] = (wide(terms, 1, here) + wide(far_in, here)).astype(jnp.bfloat16)

            over_tiles(piece, add)
            to_across(piece).start()

    def halo_end(pieces):
        for piece in pieces:
            to_across(piece).wait_recv()

            def add(here):
                halo_out[here] = wide(other_in, here) + wide(near_in, here)

            over_tiles(piece, add)

    def link_at(part, step):
        return ORDER[(FIRST_LINK[part] + step) % CLASSES]

    def tile_of(part, position):
        bits = {}
        for step in range(CLASSES):
            bits[link_at(part, step)] = (position // (TILES >> (step + 1))) % 2

        def shifted(own, axis):
            low = (own[0] + bits[axis] + bits[axis + 3]) % 2
            high = (own[1] + bits[axis + 3]) % 2
            return low, high

        x_low, x_high = shifted(x_bits, 0)
        y_low, y_high = shifted(y_bits, 1)
        z_low, z_high = shifted(z_bits, 2)
        return (z_low + 2 * z_high) * 16 + y_high * 8 + (x_low + 2 * x_high) * 2 + y_low

    def first_copy(part):
        start, size = PARTS[part]
        return remote(
            grads.at[1 - core, :, pl.ds(start, size)],
            first_in[part],
            send.at[part, 0],
            receive.at[part, 0],
            other,
        )

    def kept(step):
        return (TILES >> step) * TILE

    def later_copy(part, step):
        count = kept(step)
        return remote(
            total[part].at[pl.ds(count, count)],
            later_in[part].at[pl.ds(count, count)],
            send.at[part, step],
            receive.at[part, step],
            partners[link_at(part, step - 1)],
        )

    def product(terms_of, width, column, half):
        def tile(i, carry):
            here = pl.ds(pl.multiple_of(i * 256, 256), 256)
            summed = 0.0
            for left, right, begin in terms_of:
                summed = summed + jnp.dot(
                    left[here], right[:, pl.ds(begin, width)], preferred_element_type=jnp.float32
                )
            grads[half, here, pl.ds(column, width)] = summed.astype(jnp.bfloat16)
            return carry

        lax.fori_loop(0, WIDTH // 256, tile, 0)

    own_t = entries_t.at[:, pl.ds(0, BLOCK)]
    chosen_t = entries_t.at[:, pl.ds(BLOCK, 2 * BLOCK)]

    def products_of(group):
        column = 640 + 768 * group
        for half in range(2):
            begin = 512 * group + 256 * half
            product([(own_t, dq_own, begin)], 256, column, half)
            product([(own_t, dk_own, begin), (chosen_t, dk, begin)], 256, column + 256, half)
            product([(own_t, dv_own, begin), (chosen_t, dv, begin)], 256, column + 512, half)

    def own_pair(pair, carry):
        here = pl.ds(pl.multiple_of(pair * 2 * HEAD_DIM, 2 * HEAD_DIM), 2 * HEAD_DIM)
        queries, grad_keys, grad_values = back_of_pair(
            q[:, here],
            k[:, here],
            v[:, here],
            context[:, here],
            grad_context[:, here],
            [stats[pair, head : head + 1] for head in range(2)],
        )
        dq_own[:, here] = (queries + dq[:, here]).astype(jnp.bfloat16)
        dk_own[:, here] = grad_keys
        dv_own[:, here] = grad_values
        return carry

    def merge_first(part):
        start, size = PARTS[part]
        first_copy(part).wait_recv()

        def merge(position, carry):
            source = pl.ds(pl.multiple_of(tile_of(part, position) * TILE, TILE), TILE)
            target = pl.ds(pl.multiple_of(position * TILE, TILE), TILE)
            summed = grads[core, source, pl.ds(start, size)].astype(jnp.float32) + first_in[part][
                source
            ].astype(jnp.float32)
            total[part][target] = summed.astype(jnp.bfloat16)
            return carry

        lax.fori_loop(TILES // 2, TILES, merge, 0, unroll=8)
        later_copy(part, 1).start()
        lax.fori_loop(0, TILES // 2, merge, 0, unroll=8)

    def merge_later(part, step):
        start, size = PARTS[part]
        count = kept(step)
        later_copy(part, step).wait_recv()
        if step < CLASSES:
            half = count // 2
            tiles = half // TILE

            def merge(position, carry):
                here = pl.ds(pl.multiple_of(position * TILE, TILE), TILE)
                there = pl.ds(pl.multiple_of(position * TILE + count, TILE), TILE)
                total[part][here] = (
                    wide(total[part], here) + wide(later_in[part], there)
                ).astype(jnp.bfloat16)
                return carry

            lax.fori_loop(tiles, 2 * tiles, merge, 0, unroll=min(tiles, 8))
            later_copy(part, step + 1).start()
            lax.fori_loop(0, tiles, merge, 0, unroll=min(tiles, 8))
        else:
            final = wide(total[part], pl.ds(0, TILE)) + wide(later_in[part], pl.ds(TILE, TILE))
            last[:, :, pl.ds(start, size)] = final.reshape(2, 8, size)

    halo_start()
    fetches[1].wait()
    narrow_t[...] = context[...].T
    fetches[2].wait()
    for half in range(2):
        product([(narrow_t, hidden, 512 * half)], 512, 0, half)
    first_copy(0).start()
    halo_first(range(PIECES))
    fetches[3].wait()
    narrow_t[...] = mid[...].T
    fetches[4].wait()
    product([(narrow_t, forecast, 0)], OUTV, 512, 0)
    grads[1, :, pl.ds(512, OUTV)] = jnp.zeros((WIDTH, OUTV), jnp.bfloat16)
    first_copy(1).start()
    fetches[5].wait()
    entries_t[:, pl.ds(0, BLOCK)] = grads[0, pl.ds(0, BLOCK), pl.ds(1024, WIDTH)].T
    fetches[6].wait()
    for block in range(2):
        entries_t[:, pl.ds((block + 1) * BLOCK, BLOCK)] = grads[
            1, pl.ds(block * BLOCK, BLOCK), pl.ds(1024, WIDTH)
        ].T
    merge_first(0)
    merge_first(1)
    for i in range(7, 13):
        fetches[i].wait()
    lax.fori_loop(0, 4, own_pair, 0)
    halo_second(range(0, 2))
    fetches[13].wait()
    fetches[14].wait()
    products_of(0)
    for part in (2, 3, 4):
        first_copy(part).start()
    merge_later(0, 1)
    merge_later(1, 1)
    halo_second(range(2, 4))
    for part in (2, 3, 4):
        merge_first(part)
    lax.fori_loop(4, 8, own_pair, 0)
    merge_later(0, 2)
    merge_later(1, 2)
    halo_second(range(4, 6))
    for part in (2, 3, 4):
        merge_later(part, 1)
    products_of(1)
    for part in range(5, 11):
        first_copy(part).start()
    merge_later(0, 3)
    merge_later(1, 3)
    for part in (2, 3, 4):
        merge_later(part, 2)
    halo_second(range(6, 8))
    for part in range(5, 11):
        merge_first(part)
    for step in range(1, CLASSES + 1):
        for part, ahead in ((0, 3), (1, 3), (2, 2), (3, 2), (4, 2)):
            if step + ahead <= CLASSES:
                merge_later(part, step + ahead)
        if step == 2:
            swap.wait_recv()
        if step >= 3:
            halo_end(range(2 * step - 6, 2 * step - 4))
        for part in range(5, 11):
            merge_later(part, step)
    finish = remote(last.at[1 - core], last_in, last_send, last_recv, other)
    finish.start()
    out[core] = last[core]
    finish.wait()
    out[1 - core] = last_in[...]
    swap.wait_send()
    for piece in range(PIECES):
        to_other(piece).wait_send()
        to_backward(piece).wait_send()
        to_across(piece).wait_send()
    for part in range(parts):
        first_copy(part).wait_send()
        for step in range(1, CLASSES + 1):
            later_copy(part, step).wait_send()


def tail(terms, entries, *others):
    dma = pltpu.SemaphoreType.DMA
    parts = len(PARTS)
    rows = TILES * TILE
    operands = (terms, entries) + others
    blocks = [pltpu.VMEM((rows, size), jnp.bfloat16) for _, size in PARTS]
    block = pltpu.VMEM((BLOCK, WIDTH), jnp.bfloat16)
    result = jax.ShapeDtypeStruct((BLOCK, WIDTH), jnp.bfloat16)
    return pl.pallas_call(
        tail_kernel,
        out_shape=(
            jax.ShapeDtypeStruct((2, 8, HALF), jnp.float32),
            jax.ShapeDtypeStruct((BLOCK, WIDTH), jnp.float32),
            result,
            result,
            result,
        ),
        in_specs=[pl.BlockSpec(memory_space=pl.ANY)] * len(operands),
        out_specs=(pl.BlockSpec(memory_space=pltpu.VMEM),) * 5,
        scratch_shapes=blocks * 3
        + [
            pltpu.VMEM((2, 8, HALF), jnp.float32),
            pltpu.VMEM((8, HALF), jnp.float32),
            pltpu.VMEM((2, WIDTH, HALF), jnp.bfloat16),
            pltpu.VMEM(terms.shape, terms.dtype),
        ]
        + [pltpu.VMEM(operand.shape, operand.dtype) for operand in others]
        + [
            pltpu.VMEM((WIDTH, BAND * BLOCK), jnp.bfloat16),
            pltpu.VMEM((WIDTH, BLOCK), jnp.bfloat16),
        ]
        + [block] * 4
        + [dma((parts, CLASSES + 1)), dma((parts, CLASSES + 1)), dma, dma]
        + [dma((PIECES,))] * 6
        + [dma, dma, dma((len(operands) + 1,))],
        compiler_params=pltpu.CompilerParams(
            collective_id=1, has_side_effects=True, vmem_limit_bytes=TAIL_VMEM
        ),
        name="tail",
    )(*operands)


def attend_kernel(q_ref, k_own_ref, k_ref, v_own_ref, v_ref, context_ref, stat_ref):
    queries = q_ref[...] * jnp.bfloat16(0.125)
    keys = jnp.concatenate([k_own_ref[...], k_ref[...]], axis=0)
    values_t = jnp.concatenate([v_own_ref[...], v_ref[...]], axis=0).T
    sides = []
    for head in range(2):
        picked = jnp.where(head_mask(queries.shape, head), queries, jnp.bfloat16(0))
        scores = lax.dot_general(keys, picked, NT, preferred_element_type=jnp.float32)
        top = jnp.max(scores, axis=0, keepdims=True)
        powers = jnp.exp(scores - top)
        total = jnp.sum(powers, axis=0, keepdims=True)
        mixed = jnp.dot(
            values_t[head * HEAD_DIM : (head + 1) * HEAD_DIM],
            powers.astype(jnp.bfloat16),
            preferred_element_type=jnp.float32,
        )
        sides.append(mixed / total)
        stat_ref[0, head : head + 1] = top + jnp.log(total)
    context_ref[...] = jnp.concatenate(sides, axis=0).T.astype(jnp.bfloat16)


PAIR = 2 * HEAD_DIM


def column_block(rows):
    return pl.BlockSpec((rows, PAIR), lambda i: (0, i))


STAT_BLOCK = pl.BlockSpec((1, 2, BLOCK), lambda i: (i, 0, 0))


def attend(q, k_own, k, v_own, v):
    keys = BAND * BLOCK
    return pl.pallas_call(
        attend_kernel,
        grid=(HEADS // 2,),
        out_shape=(
            jax.ShapeDtypeStruct((BLOCK, WIDTH), jnp.bfloat16),
            jax.ShapeDtypeStruct((HEADS // 2, 2, BLOCK), jnp.float32),
        ),
        in_specs=[column_block(array.shape[0]) for array in (q, k_own, k, v_own, v)],
        out_specs=(column_block(BLOCK), STAT_BLOCK),
        compiler_params=pltpu.CompilerParams(vmem_limit_bytes=VMEM_LIMIT),
        cost_estimate=pl.CostEstimate(
            flops=4 * BLOCK * keys * WIDTH,
            bytes_accessed=2 * WIDTH * (2 * BLOCK + 2 * keys),
            transcendentals=BLOCK * keys * HEADS,
        ),
        name="attend",
    )(q, k_own, k, v_own, v)


def back_of_pair(queries, keys, values, context, grads, stats):
    queries = queries * jnp.bfloat16(0.125)
    keys_t = keys.T
    products = (grads.astype(jnp.float32) * context.astype(jnp.float32)).T
    sides = []
    grad_keys = jnp.zeros(keys.shape, jnp.float32)
    grad_values = jnp.zeros(keys.shape, jnp.float32)
    for head in range(2):
        mask = head_mask(queries.shape, head)
        picked = jnp.where(mask, queries, jnp.bfloat16(0))
        grad_here = jnp.where(mask, grads, jnp.bfloat16(0))
        inner = jnp.sum(products[head * HEAD_DIM : (head + 1) * HEAD_DIM], axis=0, keepdims=True)
        scores = lax.dot_general(keys, picked, NT, preferred_element_type=jnp.float32)
        probs = jnp.exp(scores - stats[head])
        grad_probs = lax.dot_general(values, grad_here, NT, preferred_element_type=jnp.float32)
        grad_scores = (probs * (grad_probs - inner)).astype(jnp.bfloat16)
        grad_values += jnp.dot(
            probs.astype(jnp.bfloat16), grad_here, preferred_element_type=jnp.float32
        )
        grad_keys += jnp.dot(grad_scores, picked, preferred_element_type=jnp.float32)
        sides.append(
            jnp.dot(
                keys_t[head * HEAD_DIM : (head + 1) * HEAD_DIM],
                grad_scores,
                preferred_element_type=jnp.float32,
            )
        )
    grad_queries = (jnp.concatenate(sides, axis=0) * 0.125).T
    return grad_queries, grad_keys.astype(jnp.bfloat16), grad_values.astype(jnp.bfloat16)


def attend_back_kernel(q_ref, k_ref, v_ref, context_ref, grad_ref, stat_ref, dq_ref, dk_ref, dv_ref):
    dq_ref[...], dk_ref[...], dv_ref[...] = back_of_pair(
        q_ref[...],
        k_ref[...],
        v_ref[...],
        context_ref[...],
        grad_ref[...],
        [stat_ref[0, head : head + 1] for head in range(2)],
    )


def attend_back(q, k, v, context, grad_context, stats):
    rows, keys = q.shape[0], k.shape[0]
    return pl.pallas_call(
        attend_back_kernel,
        grid=(HEADS // 2,),
        out_shape=(
            jax.ShapeDtypeStruct((rows, WIDTH), jnp.float32),
            jax.ShapeDtypeStruct((keys, WIDTH), jnp.bfloat16),
            jax.ShapeDtypeStruct((keys, WIDTH), jnp.bfloat16),
        ),
        in_specs=[column_block(array.shape[0]) for array in (q, k, v, context, grad_context)]
        + [STAT_BLOCK],
        out_specs=(column_block(rows), column_block(keys), column_block(keys)),
        compiler_params=pltpu.CompilerParams(vmem_limit_bytes=VMEM_LIMIT),
        cost_estimate=pl.CostEstimate(
            flops=10 * rows * keys * WIDTH,
            bytes_accessed=2 * WIDTH * (4 * rows + 4 * keys),
            transcendentals=rows * keys * HEADS,
        ),
        name="attend_back",
    )(q, k, v, context, grad_context, stats)


def dot(left, right):
    return jnp.dot(left, right, preferred_element_type=jnp.float32)


def per_device(
    grid_point_features,
    projection_weights_qkv,
    merging_projection,
    readout_weights_table,
    observed,
    cell_surface_share,
    band_offsets,
    latitude_order,
):
    own_rows = grid_point_features[0]
    at = place()
    block = lax.axis_index("mp")
    normed_in = layer_norm(own_rows.astype(jnp.float32)).astype(jnp.bfloat16)

    near, far = jnp.int32(1), jnp.int32(2)
    above = jnp.where(at["y_lo"] == 0, near, far)
    below = jnp.where(at["y_lo"] == 0, far, near)
    minus = jnp.where(at["core"] == 0, 3, 0)
    plus = jnp.where(at["core"] == 0, 0, 3)
    offsets = lax.dynamic_slice(band_offsets, (block, 1), (1, 2))[0]
    slots = jnp.where(
        offsets == -2, below, jnp.where(offsets == -1, minus, jnp.where(offsets == 1, plus, above))
    ).astype(jnp.int32)

    neighbours = halo(normed_in)
    chosen = [
        lax.dynamic_index_in_dim(neighbours, slots[i], 0, keepdims=False) for i in range(BAND - 1)
    ]
    chosen = jnp.concatenate(chosen, axis=0)
    weights_q = projection_weights_qkv[:, :WIDTH]
    weights_k = projection_weights_qkv[:, WIDTH : 2 * WIDTH]
    weights_v = projection_weights_qkv[:, 2 * WIDTH :]
    q = dot(normed_in, weights_q).astype(jnp.bfloat16)
    k_own = dot(normed_in, weights_k).astype(jnp.bfloat16)
    v_own = dot(normed_in, weights_v).astype(jnp.bfloat16)
    k = dot(chosen, weights_k).astype(jnp.bfloat16)
    v = dot(chosen, weights_v).astype(jnp.bfloat16)
    context, stats = attend(q, k_own, k, v_own, v)

    hidden = (own_rows.astype(jnp.float32) + dot(context, merging_projection)).astype(jnp.bfloat16)
    normed_mid = layer_norm(hidden.astype(jnp.float32)).astype(jnp.bfloat16)
    predictions = dot(normed_mid, readout_weights_table)
    target = observed[latitude_order[0]]
    grad_forecast = crps_grad(predictions, target, cell_surface_share[:, None])

    grad_mid = dot(grad_forecast, readout_weights_table.T)
    grad_hidden = jax.vjp(layer_norm, hidden.astype(jnp.float32))[1](grad_mid)[0]
    hidden_half = grad_hidden.astype(jnp.bfloat16)
    grad_context = dot(hidden_half, merging_projection.T).astype(jnp.bfloat16)
    dq, dk, dv = attend_back(q, k, v, context, grad_context, stats)

    grad_entries = (dot(dk, weights_k.T) + dot(dv, weights_v.T)).astype(jnp.bfloat16)
    first = grad_entries[:BLOCK]
    second = grad_entries[BLOCK:]
    terms = jnp.stack(
        [
            jnp.where(slots[0] == slot, first, jnp.where(slots[1] == slot, second, jnp.bfloat16(0)))
            for slot in range(4)
        ]
    )
    summed, from_others, dq_own, dk_own, dv_own = tail(
        terms,
        jnp.concatenate([normed_in, chosen], axis=0),
        context,
        hidden_half,
        normed_mid,
        grad_forecast,
        q,
        k_own,
        v_own,
        grad_context,
        stats,
        dq,
        dk,
        dv,
    )
    grad_normed = (
        dot(dq_own, weights_q.T) + dot(dk_own, weights_k.T) + dot(dv_own, weights_v.T) + from_others
    )
    feature_derivative = (
        grad_hidden + jax.vjp(layer_norm, own_rows.astype(jnp.float32))[1](grad_normed)[0]
    )

    pieces = [
        summed[half, :, 640 + 768 * group + 256 * kind : 896 + 768 * group + 256 * kind]
        for kind in range(3)
        for group in range(2)
        for half in range(2)
    ]
    return (
        predictions[None],
        feature_derivative[None],
        jnp.concatenate(pieces, axis=1),
        jnp.concatenate([summed[0, :, :512], summed[1, :, :512]], axis=1),
        summed[0, :, 512 : 512 + OUTV],
    )


def solution(mesh):
    placed = (P("member", "mp", None), P(), P(), P(), P("mp", None), P("mp"), P(), P("mp", None))
    return jax.shard_map(
        per_device,
        mesh=mesh,
        in_specs=placed,
        out_specs=(
            P("member", "mp", None),
            P("member", "mp", None),
            P(("member", "mp"), None),
            P(("member", "mp"), None),
            P(("member", "mp"), None),
        ),
        check_vma=False,
    )
```

```python
import functools

import jax
import jax.numpy as jnp
from jax import lax
from jax.experimental import pallas as pl
from jax.experimental.pallas import tpu as pltpu
from jax.sharding import PartitionSpec as P

HEADS = 16
HEAD_DIM = 64
BLOCK = 512
WIDTH = 1024
OUTV = 128
BAND = 3

norm_epsilon = 1e-05
smooth_square = 0.0625

MESH = pl.DeviceIdType.MESH
VMEM_LIMIT = 56 * 1024 * 1024

PIECE = 64
PIECES = BLOCK // PIECE

HALF = 2176
PARTS = ((0, 384), (384, 256), (640, 256), (896, 256), (1152, 256)) + tuple(
    (1408 + 128 * i, 128) for i in range(6)
)
TILE = 16
TILES = 64
CLASSES = 6
ORDER = (1, 3, 2, 4, 0, 5)
FIRST_LINK = (2, 5, 1, 3, 4, 0, 1, 2, 3, 4, 5)
TAIL_VMEM = 60 * 1024 * 1024


def layer_norm(values):
    average = jnp.mean(values, axis=-1, keepdims=True)
    centred = values - average
    spread = jnp.mean(centred * centred, axis=-1, keepdims=True)
    return centred * lax.rsqrt(spread + norm_epsilon)


def softened_derivative(difference):
    return difference * lax.rsqrt(difference * difference + smooth_square)


NT = (((1,), (1,)), ((), ()))


def head_mask(shape, head):
    lane = lax.broadcasted_iota(jnp.int32, shape, 1)
    return (lane // HEAD_DIM) == head


def place():
    member = lax.axis_index("member")
    mp = lax.axis_index("mp")
    return {
        "z": member // 2,
        "y_hi": member % 2,
        "x": mp // 4,
        "y_lo": (mp // 2) % 2,
        "core": mp % 2,
    }


def device(at):
    return (at["z"] * 2 + at["y_hi"], at["x"] * 4 + at["y_lo"] * 2 + at["core"])


def moved(at, **changes):
    return device({**at, **changes})


def greet(partners):
    barrier = pltpu.get_barrier_semaphore()
    for partner in partners:
        pl.semaphore_signal(barrier, inc=1, device_id=partner, device_id_type=MESH)
    pl.semaphore_wait(barrier, len(partners))


def remote(source, target, send, receive, partner):
    return pltpu.make_async_remote_copy(
        src_ref=source,
        dst_ref=target,
        send_sem=send,
        recv_sem=receive,
        device_id=partner,
        device_id_type=MESH,
    )


def halo_kernel(own, out, y_send, y_recv, x_send, x_recv, c_send, c_recv, o_send, o_recv):
    at = place()
    other = moved(at, core=1 - at["core"])
    across = moved(at, y_lo=1 - at["y_lo"])
    forward = moved(at, x=(at["x"] + 1 + 2 * at["y_lo"]) % 4)
    backward = moved(at, x=(at["x"] + 3 - 2 * at["y_lo"]) % 4)
    greet((other, across, forward, backward))
    near_first = (at["core"] + at["y_lo"]) % 2 == 0

    def rows(piece):
        return pl.ds(piece * PIECE, PIECE)

    def to_across(piece):
        return remote(
            own.at[rows(piece)], out.at[1, rows(piece)], y_send.at[piece], y_recv.at[piece], across
        )

    def to_forward(piece):
        return remote(
            out.at[1, rows(piece)],
            out.at[2, rows(piece)],
            x_send.at[piece],
            x_recv.at[piece],
            forward,
        )

    def to_other(slot, piece):
        return remote(
            out.at[slot, rows(piece)],
            out.at[3, rows(piece)],
            c_send.at[piece],
            c_recv.at[piece],
            other,
        )

    for piece in range(PIECES):
        to_across(piece).start()
    swap = remote(own, out.at[0], o_send, o_recv, other)
    swap.start()
    for piece in range(PIECES):
        to_across(piece).wait_recv()
        to_forward(piece).start()

        @pl.when(near_first)
        def _():
            to_other(1, piece).start()

    for piece in range(PIECES):
        to_forward(piece).wait_recv()

        @pl.when(jnp.logical_not(near_first))
        def _():
            to_other(2, piece).start()

    for piece in range(PIECES):
        to_other(1, piece).wait_recv()
    swap.wait_recv()
    swap.wait_send()
    for piece in range(PIECES):
        to_across(piece).wait_send()
        to_forward(piece).wait_send()
        to_other(1, piece).wait_send()


def halo(own):
    dma = pltpu.SemaphoreType.DMA
    return pl.pallas_call(
        halo_kernel,
        out_shape=jax.ShapeDtypeStruct((4, BLOCK, WIDTH), jnp.bfloat16),
        in_specs=[pl.BlockSpec(memory_space=pltpu.VMEM)],
        out_specs=pl.BlockSpec(memory_space=pltpu.VMEM),
        scratch_shapes=[dma((PIECES,))] * 6 + [dma, dma],
        compiler_params=pltpu.CompilerParams(
            collective_id=0, has_side_effects=True, vmem_limit_bytes=VMEM_LIMIT
        ),
        name="halo",
    )(own)


def crps_kernel(predictions, target, share, out, halves, gathered, grads, send, receive, back_send, back_recv):
    member = lax.axis_index("member")
    mp = lax.axis_index("mp")
    count = 8
    size = BLOCK // count
    greet([((member + step) % count, mp) for step in range(1, count)])

    def slice_of(index):
        return pl.ds(pl.multiple_of(index * size, size), size)

    def outward(step):
        to = (member + step) % count
        return remote(
            halves.at[slice_of(to)], gathered.at[step], send.at[step], receive.at[step], (to, mp)
        )

    def homeward(step):
        to = (member + count - step) % count
        return remote(
            grads.at[step],
            out.at[slice_of(member)],
            back_send.at[step],
            back_recv.at[step],
            (to, mp),
        )

    halves[...] = predictions[...].astype(jnp.bfloat16)
    for step in range(1, count):
        outward(step).start()
    own = slice_of(member)
    truth = target[own]
    weight = share[own]
    gathered[0] = halves[own]
    for step in range(1, count):
        outward(step).wait_recv()
    each = [gathered[step].astype(jnp.float32) for step in range(count)]
    spread = [0.0] * count
    for one in range(count):
        for two in range(one + 1, count):
            slope = softened_derivative(each[one] - each[two])
            spread[one] = spread[one] + slope
            spread[two] = spread[two] - slope
    for step in range(count):
        single = softened_derivative(each[step] - truth) / count
        paired = spread[step] / (count * (count - 1))
        grads[step] = (weight * (single - paired)).astype(jnp.bfloat16)
        if step:
            homeward(step).start()
    out[own] = grads[0]
    for step in range(1, count):
        homeward(step).wait_recv()
    for step in range(1, count):
        outward(step).wait_send()
        homeward(step).wait_send()


def crps_grad(predictions, target, share):
    dma = pltpu.SemaphoreType.DMA
    size = BLOCK // 8
    return pl.pallas_call(
        crps_kernel,
        out_shape=jax.ShapeDtypeStruct(predictions.shape, jnp.bfloat16),
        in_specs=[pl.BlockSpec(memory_space=pltpu.VMEM)] * 3,
        out_specs=pl.BlockSpec(memory_space=pltpu.VMEM),
        scratch_shapes=[
            pltpu.VMEM((BLOCK, OUTV), jnp.bfloat16),
            pltpu.VMEM((8, size, OUTV), jnp.bfloat16),
            pltpu.VMEM((8, size, OUTV), jnp.bfloat16),
        ]
        + [dma((8,))] * 4,
        compiler_params=pltpu.CompilerParams(
            collective_id=2, has_side_effects=True, vmem_limit_bytes=VMEM_LIMIT
        ),
        name="crps_grad",
    )(predictions, target, share)


def flip(bit, value):
    return (bit + value) % 2


def tail_kernel(
    terms_hbm,
    entries_hbm,
    context_hbm,
    hidden_hbm,
    mid_hbm,
    forecast_hbm,
    q_hbm,
    k_hbm,
    v_hbm,
    grad_context_hbm,
    stats_hbm,
    dq_hbm,
    dk_hbm,
    dv_hbm,
    input_out,
    output_out,
    decoder_out,
    halo_out,
    dq_own,
    dk_own,
    dv_own,
    *scratch,
):
    parts = len(PARTS)
    first_in = scratch[:parts]
    later_in = scratch[parts : 2 * parts]
    total = scratch[2 * parts : 3 * parts]
    other_total = scratch[3 * parts : 4 * parts]
    (
        last,
        last_in,
        grads,
        terms,
        context,
        hidden,
        mid,
        forecast,
        q,
        k,
        v,
        grad_context,
        stats,
        dq,
        dk,
        dv,
        entries_t,
        narrow_t,
        cross_in,
        far_in,
        near_in,
        other_in,
        send,
        receive,
        last_send,
        last_recv,
        y_send,
        y_recv,
        x_send,
        x_recv,
        c_send,
        c_recv,
        o_send,
        o_recv,
        fetched,
    ) = scratch[4 * parts :]
    at = place()
    core = at["core"]
    x_bits = (at["x"] % 2, at["x"] // 2)
    z_bits = (at["z"] % 2, at["z"] // 2)
    y_bits = (at["y_lo"], at["y_hi"])
    other = moved(at, core=1 - core)

    landing = (
        grads.at[0, pl.ds(0, BLOCK), pl.ds(1024, WIDTH)],
        grads.at[1, pl.ds(0, 2 * BLOCK), pl.ds(1024, WIDTH)],
    )
    fetches = [
        pltpu.make_async_copy(source, target, fetched.at[i])
        for i, (source, target) in enumerate(
            (
                (terms_hbm, terms),
                (context_hbm, context),
                (hidden_hbm, hidden),
                (mid_hbm, mid),
                (forecast_hbm, forecast),
                (entries_hbm.at[pl.ds(0, BLOCK)], landing[0]),
                (entries_hbm.at[pl.ds(BLOCK, 2 * BLOCK)], landing[1]),
                (q_hbm, q),
                (k_hbm, k),
                (v_hbm, v),
                (grad_context_hbm, grad_context),
                (stats_hbm, stats),
                (dq_hbm, dq),
                (dk_hbm, dk),
                (dv_hbm, dv),
            )
        )
    ]
    for fetch in fetches:
        fetch.start()

    def partner_of(link):
        low, high = 1, link // 3
        if link % 3 == 0:
            return moved(at, x=flip(x_bits[0], low) + 2 * flip(x_bits[1], high))
        if link % 3 == 1:
            return moved(at, y_lo=flip(y_bits[0], low), y_hi=flip(y_bits[1], high))
        return moved(at, z=flip(z_bits[0], low) + 2 * flip(z_bits[1], high))

    partners = [partner_of(link) for link in range(CLASSES)]
    greet([other] + partners)

    across = partners[1]
    backward = moved(at, x=(at["x"] + 3 - 2 * at["y_lo"]) % 4)
    near_first = (at["core"] + at["y_lo"]) % 2 == 0

    def rows(piece):
        return pl.ds(piece * PIECE, PIECE)

    def wide(ref, *index):
        return ref[index].astype(jnp.float32)

    def to_other(piece):
        return remote(
            terms.at[3, rows(piece)],
            cross_in.at[rows(piece)],
            c_send.at[piece],
            c_recv.at[piece],
            other,
        )

    def to_backward(piece):
        return remote(
            terms.at[2, rows(piece)], far_in.at[rows(piece)], x_send.at[piece], x_recv.at[piece], backward
        )

    def to_across(piece):
        return remote(
            terms.at[1, rows(piece)], near_in.at[rows(piece)], y_send.at[piece], y_recv.at[piece], across
        )

    swap = remote(terms.at[0], other_in, o_send, o_recv, other)

    def halo_start():
        fetches[0].wait()
        for piece in range(PIECES):
            to_other(piece).start()
        swap.start()

    def over_tiles(piece, work):
        def tile(i, carry):
            work(pl.ds(pl.multiple_of(piece * PIECE + i * TILE, TILE), TILE))
            return carry

        lax.fori_loop(0, PIECE // TILE, tile, 0)

    def halo_first(pieces):
        for piece in pieces:
            to_other(piece).wait_recv()

            def add(here):
                cross = wide(cross_in, here)
                terms[2, here] = (wide(terms, 2, here) + jnp.where(near_first, 0.0, cross)).astype(
                    jnp.bfloat16
                )
                terms[1, here] = (wide(terms, 1, here) + jnp.where(near_first, cross, 0.0)).astype(
                    jnp.bfloat16
                )

            over_tiles(piece, add)
            to_backward(piece).start()

    def halo_second(pieces):
        for piece in pieces:
            to_backward(piece).wait_recv()

            def add(here):
                terms[1, here] = (wide(terms, 1, here) + wide(far_in, here)).astype(jnp.bfloat16)

            over_tiles(piece, add)
            to_across(piece).start()

    def halo_end(pieces):
        for piece in pieces:
            to_across(piece).wait_recv()

            def add(here):
                halo_out[here] = wide(other_in, here) + wide(near_in, here)

            over_tiles(piece, add)

    def link_at(part, step):
        return ORDER[(FIRST_LINK[part] + step) % CLASSES]

    def tile_of(part, position):
        bits = {}
        for step in range(CLASSES):
            bits[link_at(part, step)] = (position // (TILES >> (step + 1))) % 2

        def shifted(own, axis):
            low = (own[0] + bits[axis] + bits[axis + 3]) % 2
            high = (own[1] + bits[axis + 3]) % 2
            return low, high

        x_low, x_high = shifted(x_bits, 0)
        y_low, y_high = shifted(y_bits, 1)
        z_low, z_high = shifted(z_bits, 2)
        return (z_low + 2 * z_high) * 16 + y_high * 8 + (x_low + 2 * x_high) * 2 + y_low

    def first_copy(part):
        start, size = PARTS[part]
        return remote(
            grads.at[1 - core, :, pl.ds(start, size)],
            first_in[part],
            send.at[part, 0],
            receive.at[part, 0],
            other,
        )

    def kept(step):
        return (TILES >> step) * TILE

    def pair_of(part, step):
        pair = (total[part], other_total[part])
        return pair if step % 2 else pair[::-1]

    def later_copy(part, step):
        count = kept(step)
        return remote(
            pair_of(part, step)[0].at[pl.ds(count, count)],
            later_in[part].at[pl.ds(count, count)],
            send.at[part, step],
            receive.at[part, step],
            partners[link_at(part, step - 1)],
        )

    def product(terms_of, width, column, half):
        summed = 0.0
        for left, right, begin in terms_of:
            summed = summed + jnp.dot(
                left[...], right[:, pl.ds(begin, width)], preferred_element_type=jnp.float32
            )
        grads[half, :, pl.ds(column, width)] = summed.astype(jnp.bfloat16)

    own_t = entries_t.at[:, pl.ds(0, BLOCK)]
    chosen_t = entries_t.at[:, pl.ds(BLOCK, 2 * BLOCK)]

    def products_of(group):
        column = 640 + 768 * group
        for half in range(2):
            begin = 512 * group + 256 * half
            product([(own_t, dq_own, begin)], 256, column, half)
            product([(own_t, dk_own, begin), (chosen_t, dk, begin)], 256, column + 256, half)
            product([(own_t, dv_own, begin), (chosen_t, dv, begin)], 256, column + 512, half)

    def own_pair(pair, carry):
        here = pl.ds(pl.multiple_of(pair * 2 * HEAD_DIM, 2 * HEAD_DIM), 2 * HEAD_DIM)
        queries, grad_keys, grad_values = back_of_pair(
            q[:, here],
            k[:, here],
            v[:, here],
            context[:, here],
            grad_context[:, here],
            [stats[pair, head : head + 1] for head in range(2)],
        )
        dq_own[:, here] = (queries + dq[:, here]).astype(jnp.bfloat16)
        dk_own[:, here] = grad_keys
        dv_own[:, here] = grad_values
        return carry

    def merge_first(part):
        start, size = PARTS[part]
        first_copy(part).wait_recv()

        def merge(position, carry):
            source = pl.ds(pl.multiple_of(tile_of(part, position) * TILE, TILE), TILE)
            target = pl.ds(pl.multiple_of(position * TILE, TILE), TILE)
            summed = grads[core, source, pl.ds(start, size)].astype(jnp.float32) + first_in[part][
                source
            ].astype(jnp.float32)
            total[part][target] = summed.astype(jnp.bfloat16)
            return carry

        lax.fori_loop(TILES // 2, TILES, merge, 0, unroll=8)
        later_copy(part, 1).start()
        lax.fori_loop(0, TILES // 2, merge, 0, unroll=8)

    def merge_later(part, step):
        start, size = PARTS[part]
        count = kept(step)
        held, made = pair_of(part, step)
        later_copy(part, step).wait_recv()
        if step < CLASSES:
            half = count // 2
            for begin in (half, 0):
                made[pl.ds(begin, half)] = (
                    held[pl.ds(begin, half)] + later_in[part][pl.ds(count + begin, half)]
                )
                if begin == half:
                    later_copy(part, step + 1).start()
        else:
            final = wide(held, pl.ds(0, TILE)) + wide(later_in[part], pl.ds(TILE, TILE))
            last[:, :, pl.ds(start, size)] = final.reshape(2, 8, size)

    halo_start()
    fetches[1].wait()
    narrow_t[...] = context[...].T
    fetches[2].wait()
    for half in range(2):
        for part in range(2):
            product([(narrow_t, hidden, 512 * half + 256 * part)], 256, 256 * part, half)
    first_copy(0).start()
    halo_first(range(PIECES))
    fetches[3].wait()
    narrow_t[...] = mid[...].T
    fetches[4].wait()
    product([(narrow_t, forecast, 0)], OUTV, 512, 0)
    grads[1, :, pl.ds(512, OUTV)] = jnp.zeros((WIDTH, OUTV), jnp.bfloat16)
    first_copy(1).start()
    fetches[5].wait()
    entries_t[:, pl.ds(0, BLOCK)] = grads[0, pl.ds(0, BLOCK), pl.ds(1024, WIDTH)].T
    fetches[6].wait()
    for block in range(2):
        entries_t[:, pl.ds((block + 1) * BLOCK, BLOCK)] = grads[
            1, pl.ds(block * BLOCK, BLOCK), pl.ds(1024, WIDTH)
        ].T
    merge_first(0)
    merge_first(1)
    for i in range(7, 13):
        fetches[i].wait()
    lax.fori_loop(0, 4, own_pair, 0)
    halo_second(range(0, 2))
    fetches[13].wait()
    fetches[14].wait()
    products_of(0)
    for part in (2, 3, 4):
        first_copy(part).start()
    merge_later(0, 1)
    merge_later(1, 1)
    halo_second(range(2, 4))
    for part in (2, 3, 4):
        merge_first(part)
    lax.fori_loop(4, 8, own_pair, 0)
    merge_later(0, 2)
    merge_later(1, 2)
    halo_second(range(4, 6))
    for part in (2, 3, 4):
        merge_later(part, 1)
    products_of(1)
    for part in range(5, 11):
        first_copy(part).start()
    merge_later(0, 3)
    merge_later(1, 3)
    for part in (2, 3, 4):
        merge_later(part, 2)
    halo_second(range(6, 8))
    for part in range(5, 11):
        merge_first(part)
    for step in range(1, CLASSES + 1):
        for part, ahead in ((0, 3), (1, 3), (2, 2), (3, 2), (4, 2)):
            if step + ahead <= CLASSES:
                merge_later(part, step + ahead)
        if step == 2:
            swap.wait_recv()
        if step >= 3:
            halo_end(range(2 * step - 6, 2 * step - 4))
        for part in range(5, 11):
            merge_later(part, step)
    finish = remote(last.at[1 - core], last_in, last_send, last_recv, other)
    finish.start()

    def deliver(half, source):
        def columns(begin, size):
            return pl.ds(pl.multiple_of(begin, 128), size)

        output_out[:, columns(512 * half, 512)] = source[:, pl.ds(0, 512)]
        for group in range(2):
            for kind in range(3):
                input_out[:, columns(1024 * kind + 512 * group + 256 * half, 256)] = source[
                    :, pl.ds(640 + 768 * group + 256 * kind, 256)
                ]

    deliver(core, last.at[core])
    finish.wait()
    deliver(1 - core, last_in)
    decoder_out[...] = jnp.where(core == 0, last[0, :, pl.ds(512, OUTV)], last_in[:, pl.ds(512, OUTV)])
    swap.wait_send()
    for piece in range(PIECES):
        to_other(piece).wait_send()
        to_backward(piece).wait_send()
        to_across(piece).wait_send()
    for part in range(parts):
        first_copy(part).wait_send()
        for step in range(1, CLASSES + 1):
            later_copy(part, step).wait_send()


def tail(terms, entries, *others):
    dma = pltpu.SemaphoreType.DMA
    parts = len(PARTS)
    rows = TILES * TILE
    operands = (terms, entries) + others
    blocks = [pltpu.VMEM((rows, size), jnp.bfloat16) for _, size in PARTS]
    block = pltpu.VMEM((BLOCK, WIDTH), jnp.bfloat16)
    result = jax.ShapeDtypeStruct((BLOCK, WIDTH), jnp.bfloat16)
    return pl.pallas_call(
        tail_kernel,
        out_shape=(
            jax.ShapeDtypeStruct((8, 3 * WIDTH), jnp.float32),
            jax.ShapeDtypeStruct((8, WIDTH), jnp.float32),
            jax.ShapeDtypeStruct((8, OUTV), jnp.float32),
            jax.ShapeDtypeStruct((BLOCK, WIDTH), jnp.float32),
            result,
            result,
            result,
        ),
        in_specs=[pl.BlockSpec(memory_space=pl.ANY)] * len(operands),
        out_specs=(pl.BlockSpec(memory_space=pltpu.VMEM),) * 7,
        scratch_shapes=blocks * 3
        + [pltpu.VMEM((rows // 2, size), jnp.bfloat16) for _, size in PARTS]
        + [
            pltpu.VMEM((2, 8, HALF), jnp.float32),
            pltpu.VMEM((8, HALF), jnp.float32),
            pltpu.VMEM((2, WIDTH, HALF), jnp.bfloat16),
            pltpu.VMEM(terms.shape, terms.dtype),
        ]
        + [pltpu.VMEM(operand.shape, operand.dtype) for operand in others]
        + [
            pltpu.VMEM((WIDTH, BAND * BLOCK), jnp.bfloat16),
            pltpu.VMEM((WIDTH, BLOCK), jnp.bfloat16),
        ]
        + [block] * 4
        + [dma((parts, CLASSES + 1)), dma((parts, CLASSES + 1)), dma, dma]
        + [dma((PIECES,))] * 6
        + [dma, dma, dma((len(operands) + 1,))],
        compiler_params=pltpu.CompilerParams(
            collective_id=1, has_side_effects=True, vmem_limit_bytes=TAIL_VMEM
        ),
        name="tail",
    )(*operands)


def attend_kernel(q_ref, k_own_ref, k_ref, v_own_ref, v_ref, context_ref, stat_ref):
    queries = q_ref[...] * jnp.bfloat16(0.125)
    keys = jnp.concatenate([k_own_ref[...], k_ref[...]], axis=0)
    values_t = jnp.concatenate([v_own_ref[...], v_ref[...]], axis=0).T
    sides = []
    for head in range(2):
        picked = jnp.where(head_mask(queries.shape, head), queries, jnp.bfloat16(0))
        scores = lax.dot_general(keys, picked, NT, preferred_element_type=jnp.float32)
        top = jnp.max(scores, axis=0, keepdims=True)
        powers = jnp.exp(scores - top)
        total = jnp.sum(powers, axis=0, keepdims=True)
        mixed = jnp.dot(
            values_t[head * HEAD_DIM : (head + 1) * HEAD_DIM],
            powers.astype(jnp.bfloat16),
            preferred_element_type=jnp.float32,
        )
        sides.append(mixed / total)
        stat_ref[0, head : head + 1] = top + jnp.log(total)
    context_ref[...] = jnp.concatenate(sides, axis=0).T.astype(jnp.bfloat16)


PAIR = 2 * HEAD_DIM


def column_block(rows):
    return pl.BlockSpec((rows, PAIR), lambda i: (0, i))


STAT_BLOCK = pl.BlockSpec((1, 2, BLOCK), lambda i: (i, 0, 0))


def attend(q, k_own, k, v_own, v):
    keys = BAND * BLOCK
    return pl.pallas_call(
        attend_kernel,
        grid=(HEADS // 2,),
        out_shape=(
            jax.ShapeDtypeStruct((BLOCK, WIDTH), jnp.bfloat16),
            jax.ShapeDtypeStruct((HEADS // 2, 2, BLOCK), jnp.float32),
        ),
        in_specs=[column_block(array.shape[0]) for array in (q, k_own, k, v_own, v)],
        out_specs=(column_block(BLOCK), STAT_BLOCK),
        compiler_params=pltpu.CompilerParams(vmem_limit_bytes=VMEM_LIMIT),
        cost_estimate=pl.CostEstimate(
            flops=4 * BLOCK * keys * WIDTH,
            bytes_accessed=2 * WIDTH * (2 * BLOCK + 2 * keys),
            transcendentals=BLOCK * keys * HEADS,
        ),
        name="attend",
    )(q, k_own, k, v_own, v)


def back_of_pair(queries, keys, values, context, grads, stats):
    queries = queries * jnp.bfloat16(0.125)
    keys_t = keys.T
    products = (grads.astype(jnp.float32) * context.astype(jnp.float32)).T
    sides = []
    grad_keys = jnp.zeros(keys.shape, jnp.float32)
    grad_values = jnp.zeros(keys.shape, jnp.float32)
    for head in range(2):
        mask = head_mask(queries.shape, head)
        picked = jnp.where(mask, queries, jnp.bfloat16(0))
        grad_here = jnp.where(mask, grads, jnp.bfloat16(0))
        inner = jnp.sum(products[head * HEAD_DIM : (head + 1) * HEAD_DIM], axis=0, keepdims=True)
        scores = lax.dot_general(keys, picked, NT, preferred_element_type=jnp.float32)
        probs = jnp.exp(scores - stats[head])
        grad_probs = lax.dot_general(values, grad_here, NT, preferred_element_type=jnp.float32)
        grad_scores = (probs * (grad_probs - inner)).astype(jnp.bfloat16)
        grad_values += jnp.dot(
            probs.astype(jnp.bfloat16), grad_here, preferred_element_type=jnp.float32
        )
        grad_keys += jnp.dot(grad_scores, picked, preferred_element_type=jnp.float32)
        sides.append(
            jnp.dot(
                keys_t[head * HEAD_DIM : (head + 1) * HEAD_DIM],
                grad_scores,
                preferred_element_type=jnp.float32,
            )
        )
    grad_queries = (jnp.concatenate(sides, axis=0) * 0.125).T
    return grad_queries, grad_keys.astype(jnp.bfloat16), grad_values.astype(jnp.bfloat16)


def attend_back_kernel(q_ref, k_ref, v_ref, context_ref, grad_ref, stat_ref, dq_ref, dk_ref, dv_ref):
    dq_ref[...], dk_ref[...], dv_ref[...] = back_of_pair(
        q_ref[...],
        k_ref[...],
        v_ref[...],
        context_ref[...],
        grad_ref[...],
        [stat_ref[0, head : head + 1] for head in range(2)],
    )


def attend_back(q, k, v, context, grad_context, stats):
    rows, keys = q.shape[0], k.shape[0]
    return pl.pallas_call(
        attend_back_kernel,
        grid=(HEADS // 2,),
        out_shape=(
            jax.ShapeDtypeStruct((rows, WIDTH), jnp.float32),
            jax.ShapeDtypeStruct((keys, WIDTH), jnp.bfloat16),
            jax.ShapeDtypeStruct((keys, WIDTH), jnp.bfloat16),
        ),
        in_specs=[column_block(array.shape[0]) for array in (q, k, v, context, grad_context)]
        + [STAT_BLOCK],
        out_specs=(column_block(rows), column_block(keys), column_block(keys)),
        compiler_params=pltpu.CompilerParams(vmem_limit_bytes=VMEM_LIMIT),
        cost_estimate=pl.CostEstimate(
            flops=10 * rows * keys * WIDTH,
            bytes_accessed=2 * WIDTH * (4 * rows + 4 * keys),
            transcendentals=rows * keys * HEADS,
        ),
        name="attend_back",
    )(q, k, v, context, grad_context, stats)


def dot(left, right):
    return jnp.dot(left, right, preferred_element_type=jnp.float32)


def per_device(
    grid_point_features,
    projection_weights_qkv,
    merging_projection,
    readout_weights_table,
    observed,
    cell_surface_share,
    band_offsets,
    latitude_order,
):
    own_rows = grid_point_features[0]
    at = place()
    block = lax.axis_index("mp")
    normed_in = layer_norm(own_rows.astype(jnp.float32)).astype(jnp.bfloat16)

    near, far = jnp.int32(1), jnp.int32(2)
    above = jnp.where(at["y_lo"] == 0, near, far)
    below = jnp.where(at["y_lo"] == 0, far, near)
    minus = jnp.where(at["core"] == 0, 3, 0)
    plus = jnp.where(at["core"] == 0, 0, 3)
    offsets = lax.dynamic_slice(band_offsets, (block, 1), (1, 2))[0]
    slots = jnp.where(
        offsets == -2, below, jnp.where(offsets == -1, minus, jnp.where(offsets == 1, plus, above))
    ).astype(jnp.int32)

    neighbours = halo(normed_in)
    chosen = [
        lax.dynamic_index_in_dim(neighbours, slots[i], 0, keepdims=False) for i in range(BAND - 1)
    ]
    chosen = jnp.concatenate(chosen, axis=0)
    weights_q = projection_weights_qkv[:, :WIDTH]
    weights_k = projection_weights_qkv[:, WIDTH : 2 * WIDTH]
    weights_v = projection_weights_qkv[:, 2 * WIDTH :]
    q = dot(normed_in, weights_q).astype(jnp.bfloat16)
    k_own = dot(normed_in, weights_k).astype(jnp.bfloat16)
    v_own = dot(normed_in, weights_v).astype(jnp.bfloat16)
    k = dot(chosen, weights_k).astype(jnp.bfloat16)
    v = dot(chosen, weights_v).astype(jnp.bfloat16)
    context, stats = attend(q, k_own, k, v_own, v)

    hidden = (own_rows.astype(jnp.float32) + dot(context, merging_projection)).astype(jnp.bfloat16)
    normed_mid = layer_norm(hidden.astype(jnp.float32)).astype(jnp.bfloat16)
    predictions = dot(normed_mid, readout_weights_table)
    target = observed[latitude_order[0]]
    grad_forecast = crps_grad(predictions, target, cell_surface_share[:, None])

    grad_mid = dot(grad_forecast, readout_weights_table.T)
    grad_hidden = jax.vjp(layer_norm, hidden.astype(jnp.float32))[1](grad_mid)[0]
    hidden_half = grad_hidden.astype(jnp.bfloat16)
    grad_context = dot(hidden_half, merging_projection.T).astype(jnp.bfloat16)
    dq, dk, dv = attend_back(q, k, v, context, grad_context, stats)

    grad_entries = (dot(dk, weights_k.T) + dot(dv, weights_v.T)).astype(jnp.bfloat16)
    first = grad_entries[:BLOCK]
    second = grad_entries[BLOCK:]
    terms = jnp.stack(
        [
            jnp.where(slots[0] == slot, first, jnp.where(slots[1] == slot, second, jnp.bfloat16(0)))
            for slot in range(4)
        ]
    )
    grad_input, grad_output, grad_decoder, from_others, dq_own, dk_own, dv_own = tail(
        terms,
        jnp.concatenate([normed_in, chosen], axis=0),
        context,
        hidden_half,
        normed_mid,
        grad_forecast,
        q,
        k_own,
        v_own,
        grad_context,
        stats,
        dq,
        dk,
        dv,
    )
    grad_normed = (
        dot(dq_own, weights_q.T) + dot(dk_own, weights_k.T) + dot(dv_own, weights_v.T) + from_others
    )
    feature_derivative = (
        grad_hidden + jax.vjp(layer_norm, own_rows.astype(jnp.float32))[1](grad_normed)[0]
    )

    return (
        predictions[None],
        feature_derivative[None],
        grad_input,
        grad_output,
        grad_decoder,
    )


def solution(mesh):
    placed = (P("member", "mp", None), P(), P(), P(), P("mp", None), P("mp"), P(), P("mp", None))
    return jax.shard_map(
        per_device,
        mesh=mesh,
        in_specs=placed,
        out_specs=(
            P("member", "mp", None),
            P("member", "mp", None),
            P(("member", "mp"), None),
            P(("member", "mp"), None),
            P(("member", "mp"), None),
        ),
        check_vma=False,
    )
```

```python
import functools

import jax
import jax.numpy as jnp
from jax import lax
from jax.experimental import pallas as pl
from jax.experimental.pallas import tpu as pltpu
from jax.sharding import PartitionSpec as P

HEADS = 16
HEAD_DIM = 64
BLOCK = 512
WIDTH = 1024
OUTV = 128
BAND = 3

norm_epsilon = 1e-05
smooth_square = 0.0625

MESH = pl.DeviceIdType.MESH
VMEM_LIMIT = 56 * 1024 * 1024

PIECE = 64
PIECES = BLOCK // PIECE

HALF = 2176
PARTS = ((0, 384), (384, 256), (640, 256), (896, 256), (1152, 256)) + tuple(
    (1408 + 128 * i, 128) for i in range(6)
)
TILE = 16
TILES = 64
CLASSES = 6
ORDER = (1, 3, 2, 4, 0, 5)
FIRST_LINK = (2, 5, 1, 3, 4, 0, 1, 2, 3, 4, 5)
TAIL_VMEM = 60 * 1024 * 1024


def layer_norm(values):
    average = jnp.mean(values, axis=-1, keepdims=True)
    centred = values - average
    spread = jnp.mean(centred * centred, axis=-1, keepdims=True)
    return centred * lax.rsqrt(spread + norm_epsilon)


def softened_derivative(difference):
    return difference * lax.rsqrt(difference * difference + smooth_square)


NT = (((1,), (1,)), ((), ()))


def head_mask(shape, head):
    lane = lax.broadcasted_iota(jnp.int32, shape, 1)
    return (lane // HEAD_DIM) == head


def place():
    member = lax.axis_index("member")
    mp = lax.axis_index("mp")
    return {
        "z": member // 2,
        "y_hi": member % 2,
        "x": mp // 4,
        "y_lo": (mp // 2) % 2,
        "core": mp % 2,
    }


def device(at):
    return (at["z"] * 2 + at["y_hi"], at["x"] * 4 + at["y_lo"] * 2 + at["core"])


def moved(at, **changes):
    return device({**at, **changes})


def greet(partners):
    barrier = pltpu.get_barrier_semaphore()
    for partner in partners:
        pl.semaphore_signal(barrier, inc=1, device_id=partner, device_id_type=MESH)
    pl.semaphore_wait(barrier, len(partners))


def remote(source, target, send, receive, partner):
    return pltpu.make_async_remote_copy(
        src_ref=source,
        dst_ref=target,
        send_sem=send,
        recv_sem=receive,
        device_id=partner,
        device_id_type=MESH,
    )


def halo_kernel(own, out, y_send, y_recv, x_send, x_recv, c_send, c_recv, o_send, o_recv):
    at = place()
    other = moved(at, core=1 - at["core"])
    across = moved(at, y_lo=1 - at["y_lo"])
    forward = moved(at, x=(at["x"] + 1 + 2 * at["y_lo"]) % 4)
    backward = moved(at, x=(at["x"] + 3 - 2 * at["y_lo"]) % 4)
    greet((other, across, forward, backward))
    near_first = (at["core"] + at["y_lo"]) % 2 == 0

    def rows(piece):
        return pl.ds(piece * PIECE, PIECE)

    def to_across(piece):
        return remote(
            own.at[rows(piece)], out.at[1, rows(piece)], y_send.at[piece], y_recv.at[piece], across
        )

    def to_forward(piece):
        return remote(
            out.at[1, rows(piece)],
            out.at[2, rows(piece)],
            x_send.at[piece],
            x_recv.at[piece],
            forward,
        )

    def to_other(slot, piece):
        return remote(
            out.at[slot, rows(piece)],
            out.at[3, rows(piece)],
            c_send.at[piece],
            c_recv.at[piece],
            other,
        )

    for piece in range(PIECES):
        to_across(piece).start()
    swap = remote(own, out.at[0], o_send, o_recv, other)
    swap.start()
    for piece in range(PIECES):
        to_across(piece).wait_recv()
        to_forward(piece).start()

        @pl.when(near_first)
        def _():
            to_other(1, piece).start()

    for piece in range(PIECES):
        to_forward(piece).wait_recv()

        @pl.when(jnp.logical_not(near_first))
        def _():
            to_other(2, piece).start()

    for piece in range(PIECES):
        to_other(1, piece).wait_recv()
    swap.wait_recv()
    swap.wait_send()
    for piece in range(PIECES):
        to_across(piece).wait_send()
        to_forward(piece).wait_send()
        to_other(1, piece).wait_send()


def halo(own):
    dma = pltpu.SemaphoreType.DMA
    return pl.pallas_call(
        halo_kernel,
        out_shape=jax.ShapeDtypeStruct((4, BLOCK, WIDTH), jnp.bfloat16),
        in_specs=[pl.BlockSpec(memory_space=pltpu.VMEM)],
        out_specs=pl.BlockSpec(memory_space=pltpu.VMEM),
        scratch_shapes=[dma((PIECES,))] * 6 + [dma, dma],
        compiler_params=pltpu.CompilerParams(
            collective_id=0, has_side_effects=True, vmem_limit_bytes=VMEM_LIMIT
        ),
        name="halo",
    )(own)


def crps_kernel(predictions, target, share, out, halves, gathered, grads, send, receive, back_send, back_recv):
    member = lax.axis_index("member")
    mp = lax.axis_index("mp")
    count = 8
    size = BLOCK // count
    greet([((member + step) % count, mp) for step in range(1, count)])

    def slice_of(index):
        return pl.ds(pl.multiple_of(index * size, size), size)

    def outward(step):
        to = (member + step) % count
        return remote(
            halves.at[slice_of(to)], gathered.at[step], send.at[step], receive.at[step], (to, mp)
        )

    def homeward(step):
        to = (member + count - step) % count
        return remote(
            grads.at[step],
            out.at[slice_of(member)],
            back_send.at[step],
            back_recv.at[step],
            (to, mp),
        )

    halves[...] = predictions[...].astype(jnp.bfloat16)
    for step in range(1, count):
        outward(step).start()
    own = slice_of(member)
    truth = target[own]
    weight = share[own]
    gathered[0] = halves[own]
    for step in range(1, count):
        outward(step).wait_recv()
    each = [gathered[step].astype(jnp.float32) for step in range(count)]
    spread = [0.0] * count
    for one in range(count):
        for two in range(one + 1, count):
            slope = softened_derivative(each[one] - each[two])
            spread[one] = spread[one] + slope
            spread[two] = spread[two] - slope
    for step in range(count):
        single = softened_derivative(each[step] - truth) / count
        paired = spread[step] / (count * (count - 1))
        grads[step] = (weight * (single - paired)).astype(jnp.bfloat16)
        if step:
            homeward(step).start()
    out[own] = grads[0]
    for step in range(1, count):
        homeward(step).wait_recv()
    for step in range(1, count):
        outward(step).wait_send()
        homeward(step).wait_send()


def crps_grad(predictions, target, share):
    dma = pltpu.SemaphoreType.DMA
    size = BLOCK // 8
    return pl.pallas_call(
        crps_kernel,
        out_shape=jax.ShapeDtypeStruct(predictions.shape, jnp.bfloat16),
        in_specs=[pl.BlockSpec(memory_space=pltpu.VMEM)] * 3,
        out_specs=pl.BlockSpec(memory_space=pltpu.VMEM),
        scratch_shapes=[
            pltpu.VMEM((BLOCK, OUTV), jnp.bfloat16),
            pltpu.VMEM((8, size, OUTV), jnp.bfloat16),
            pltpu.VMEM((8, size, OUTV), jnp.bfloat16),
        ]
        + [dma((8,))] * 4,
        compiler_params=pltpu.CompilerParams(
            collective_id=2, has_side_effects=True, vmem_limit_bytes=VMEM_LIMIT
        ),
        name="crps_grad",
    )(predictions, target, share)


def flip(bit, value):
    return (bit + value) % 2


def tail_kernel(
    terms_hbm,
    entries_hbm,
    context_hbm,
    hidden_hbm,
    mid_hbm,
    forecast_hbm,
    q_hbm,
    k_hbm,
    v_hbm,
    grad_context_hbm,
    stats_hbm,
    dq_hbm,
    dk_hbm,
    dv_hbm,
    input_out,
    output_out,
    decoder_out,
    halo_out,
    dq_own,
    dk_own,
    dv_own,
    *scratch,
):
    parts = len(PARTS)
    first_in = scratch[:parts]
    later_in = scratch[parts : 2 * parts]
    total = scratch[2 * parts : 3 * parts]
    other_total = scratch[3 * parts : 4 * parts]
    (
        last,
        last_in,
        grads,
        terms,
        context,
        hidden,
        mid,
        forecast,
        q,
        k,
        v,
        grad_context,
        stats,
        dq,
        dk,
        dv,
        entries_t,
        narrow_t,
        cross_in,
        far_in,
        near_in,
        other_in,
        send,
        receive,
        last_send,
        last_recv,
        y_send,
        y_recv,
        x_send,
        x_recv,
        c_send,
        c_recv,
        o_send,
        o_recv,
        fetched,
    ) = scratch[4 * parts :]
    at = place()
    core = at["core"]
    x_bits = (at["x"] % 2, at["x"] // 2)
    z_bits = (at["z"] % 2, at["z"] // 2)
    y_bits = (at["y_lo"], at["y_hi"])
    other = moved(at, core=1 - core)

    landing = (
        grads.at[0, pl.ds(0, BLOCK), pl.ds(1024, WIDTH)],
        grads.at[1, pl.ds(0, 2 * BLOCK), pl.ds(1024, WIDTH)],
    )
    fetches = [
        pltpu.make_async_copy(source, target, fetched.at[i])
        for i, (source, target) in enumerate(
            (
                (terms_hbm, terms),
                (context_hbm, context),
                (hidden_hbm, hidden),
                (mid_hbm, mid),
                (forecast_hbm, forecast),
                (entries_hbm.at[pl.ds(0, BLOCK)], landing[0]),
                (entries_hbm.at[pl.ds(BLOCK, 2 * BLOCK)], landing[1]),
                (q_hbm, q),
                (k_hbm, k),
                (v_hbm, v),
                (grad_context_hbm, grad_context),
                (stats_hbm, stats),
                (dq_hbm, dq),
                (dk_hbm, dk),
                (dv_hbm, dv),
            )
        )
    ]
    for fetch in fetches:
        fetch.start()

    def partner_of(link):
        low, high = 1, link // 3
        if link % 3 == 0:
            return moved(at, x=flip(x_bits[0], low) + 2 * flip(x_bits[1], high))
        if link % 3 == 1:
            return moved(at, y_lo=flip(y_bits[0], low), y_hi=flip(y_bits[1], high))
        return moved(at, z=flip(z_bits[0], low) + 2 * flip(z_bits[1], high))

    partners = [partner_of(link) for link in range(CLASSES)]
    greet([other] + partners)

    across = partners[1]
    backward = moved(at, x=(at["x"] + 3 - 2 * at["y_lo"]) % 4)
    near_first = (at["core"] + at["y_lo"]) % 2 == 0

    def rows(piece):
        return pl.ds(piece * PIECE, PIECE)

    def wide(ref, *index):
        return ref[index].astype(jnp.float32)

    def to_other(piece):
        return remote(
            terms.at[3, rows(piece)],
            cross_in.at[rows(piece)],
            c_send.at[piece],
            c_recv.at[piece],
            other,
        )

    def to_backward(piece):
        return remote(
            terms.at[2, rows(piece)], far_in.at[rows(piece)], x_send.at[piece], x_recv.at[piece], backward
        )

    def to_across(piece):
        return remote(
            terms.at[1, rows(piece)], near_in.at[rows(piece)], y_send.at[piece], y_recv.at[piece], across
        )

    swap = remote(terms.at[0], other_in, o_send, o_recv, other)

    def halo_start():
        fetches[0].wait()
        for piece in range(PIECES):
            to_other(piece).start()
        swap.start()

    def over_tiles(piece, work):
        def tile(i, carry):
            work(pl.ds(pl.multiple_of(piece * PIECE + i * TILE, TILE), TILE))
            return carry

        lax.fori_loop(0, PIECE // TILE, tile, 0)

    def halo_first(pieces):
        for piece in pieces:
            to_other(piece).wait_recv()

            def add(here):
                cross = wide(cross_in, here)
                terms[2, here] = (wide(terms, 2, here) + jnp.where(near_first, 0.0, cross)).astype(
                    jnp.bfloat16
                )
                terms[1, here] = (wide(terms, 1, here) + jnp.where(near_first, cross, 0.0)).astype(
                    jnp.bfloat16
                )

            over_tiles(piece, add)
            to_backward(piece).start()

    def halo_second(pieces):
        for piece in pieces:
            to_backward(piece).wait_recv()

            def add(here):
                terms[1, here] = (wide(terms, 1, here) + wide(far_in, here)).astype(jnp.bfloat16)

            over_tiles(piece, add)
            to_across(piece).start()

    def halo_end(pieces):
        for piece in pieces:
            to_across(piece).wait_recv()

            def add(here):
                halo_out[here] = wide(other_in, here) + wide(near_in, here)

            over_tiles(piece, add)

    def link_at(part, step):
        return ORDER[(FIRST_LINK[part] + step) % CLASSES]

    weights = (2, 1, 16, 4, 8, 32)
    places = (x_bits[0], y_bits[0], z_bits[0], x_bits[1], y_bits[1], z_bits[1])
    turns = [TILE * weight * (1 - 2 * bit) for weight, bit in zip(weights, places)]
    tile_rows = [TILE * sum(weight * bit for weight, bit in zip(weights, places))]
    for turn in turns:
        tile_rows = tile_rows + [row + turn for row in tile_rows]

    def tile_row(part, position):
        mask = 0
        for step in range(CLASSES):
            if position & (TILES >> (step + 1)):
                link = link_at(part, step)
                mask ^= (1 << link) | (1 << (link % 3))
        return pl.multiple_of(tile_rows[mask], TILE)

    def first_copy(part):
        start, size = PARTS[part]
        return remote(
            grads.at[1 - core, :, pl.ds(start, size)],
            first_in[part],
            send.at[part, 0],
            receive.at[part, 0],
            other,
        )

    def kept(step):
        return (TILES >> step) * TILE

    def pair_of(part, step):
        pair = (total[part], other_total[part])
        return pair if step % 2 else pair[::-1]

    def later_copy(part, step):
        count = kept(step)
        return remote(
            pair_of(part, step)[0].at[pl.ds(count, count)],
            later_in[part].at[pl.ds(count, count)],
            send.at[part, step],
            receive.at[part, step],
            partners[link_at(part, step - 1)],
        )

    def product(terms_of, width, column, half):
        summed = 0.0
        for left, right, begin in terms_of:
            summed = summed + jnp.dot(
                left[...], right[:, pl.ds(begin, width)], preferred_element_type=jnp.float32
            )
        grads[half, :, pl.ds(column, width)] = summed.astype(jnp.bfloat16)

    own_t = entries_t.at[:, pl.ds(0, BLOCK)]
    chosen_t = entries_t.at[:, pl.ds(BLOCK, 2 * BLOCK)]

    def products_of(group):
        column = 640 + 768 * group
        for half in range(2):
            begin = 512 * group + 256 * half
            product([(own_t, dq_own, begin)], 256, column, half)
            product([(own_t, dk_own, begin), (chosen_t, dk, begin)], 256, column + 256, half)
            product([(own_t, dv_own, begin), (chosen_t, dv, begin)], 256, column + 512, half)

    def own_pair(pair, carry):
        here = pl.ds(pl.multiple_of(pair * 2 * HEAD_DIM, 2 * HEAD_DIM), 2 * HEAD_DIM)
        queries, grad_keys, grad_values = back_of_pair(
            q[:, here],
            k[:, here],
            v[:, here],
            context[:, here],
            grad_context[:, here],
            [stats[pair, head : head + 1] for head in range(2)],
        )
        dq_own[:, here] = (queries + dq[:, here]).astype(jnp.bfloat16)
        dk_own[:, here] = grad_keys
        dv_own[:, here] = grad_values
        return carry

    def merge_first(part):
        start, size = PARTS[part]
        first_copy(part).wait_recv()

        def merge(positions):
            for position in positions:
                source = pl.ds(tile_row(part, position), TILE)
                total[part][pl.ds(position * TILE, TILE)] = (
                    grads[core, source, pl.ds(start, size)] + first_in[part][source]
                )

        merge(range(TILES // 2, TILES))
        later_copy(part, 1).start()
        merge(range(TILES // 2))

    def merge_later(part, step):
        start, size = PARTS[part]
        count = kept(step)
        held, made = pair_of(part, step)
        later_copy(part, step).wait_recv()
        if step < CLASSES:
            half = count // 2
            for begin in (half, 0):
                made[pl.ds(begin, half)] = (
                    held[pl.ds(begin, half)] + later_in[part][pl.ds(count + begin, half)]
                )
                if begin == half:
                    later_copy(part, step + 1).start()
        else:
            final = wide(held, pl.ds(0, TILE)) + wide(later_in[part], pl.ds(TILE, TILE))
            last[:, :, pl.ds(start, size)] = final.reshape(2, 8, size)

    halo_start()
    fetches[1].wait()
    narrow_t[...] = context[...].T
    fetches[2].wait()
    for half in range(2):
        for part in range(2):
            product([(narrow_t, hidden, 512 * half + 256 * part)], 256, 256 * part, half)
    first_copy(0).start()
    halo_first(range(PIECES))
    fetches[3].wait()
    narrow_t[...] = mid[...].T
    fetches[4].wait()
    product([(narrow_t, forecast, 0)], OUTV, 512, 0)
    grads[1, :, pl.ds(512, OUTV)] = jnp.zeros((WIDTH, OUTV), jnp.bfloat16)
    first_copy(1).start()
    fetches[5].wait()
    entries_t[:, pl.ds(0, BLOCK)] = grads[0, pl.ds(0, BLOCK), pl.ds(1024, WIDTH)].T
    fetches[6].wait()
    for block in range(2):
        entries_t[:, pl.ds((block + 1) * BLOCK, BLOCK)] = grads[
            1, pl.ds(block * BLOCK, BLOCK), pl.ds(1024, WIDTH)
        ].T
    merge_first(0)
    merge_first(1)
    for i in range(7, 13):
        fetches[i].wait()
    lax.fori_loop(0, 4, own_pair, 0)
    halo_second(range(0, 2))
    fetches[13].wait()
    fetches[14].wait()
    products_of(0)
    for part in (2, 3, 4):
        first_copy(part).start()
    merge_later(0, 1)
    merge_later(1, 1)
    halo_second(range(2, 4))
    for part in (2, 3, 4):
        merge_first(part)
    lax.fori_loop(4, 8, own_pair, 0)
    merge_later(0, 2)
    merge_later(1, 2)
    halo_second(range(4, 6))
    for part in (2, 3, 4):
        merge_later(part, 1)
    products_of(1)
    for part in range(5, 11):
        first_copy(part).start()
    merge_later(0, 3)
    merge_later(1, 3)
    for part in (2, 3, 4):
        merge_later(part, 2)
    halo_second(range(6, 8))
    for part in range(5, 11):
        merge_first(part)
    for step in range(1, CLASSES + 1):
        for part, ahead in ((0, 3), (1, 3), (2, 2), (3, 2), (4, 2)):
            if step + ahead <= CLASSES:
                merge_later(part, step + ahead)
        if step == 2:
            swap.wait_recv()
        if step >= 3:
            halo_end(range(2 * step - 6, 2 * step - 4))
        for part in range(5, 11):
            merge_later(part, step)
    finish = remote(last.at[1 - core], last_in, last_send, last_recv, other)
    finish.start()

    def deliver(half, source):
        def columns(begin, size):
            return pl.ds(pl.multiple_of(begin, 128), size)

        output_out[:, columns(512 * half, 512)] = source[:, pl.ds(0, 512)]
        for group in range(2):
            for kind in range(3):
                input_out[:, columns(1024 * kind + 512 * group + 256 * half, 256)] = source[
                    :, pl.ds(640 + 768 * group + 256 * kind, 256)
                ]

    deliver(core, last.at[core])
    finish.wait()
    deliver(1 - core, last_in)
    decoder_out[...] = jnp.where(core == 0, last[0, :, pl.ds(512, OUTV)], last_in[:, pl.ds(512, OUTV)])
    swap.wait_send()
    for piece in range(PIECES):
        to_other(piece).wait_send()
        to_backward(piece).wait_send()
        to_across(piece).wait_send()
    for part in range(parts):
        first_copy(part).wait_send()
        for step in range(1, CLASSES + 1):
            later_copy(part, step).wait_send()


def tail(terms, entries, *others):
    dma = pltpu.SemaphoreType.DMA
    parts = len(PARTS)
    rows = TILES * TILE
    operands = (terms, entries) + others
    blocks = [pltpu.VMEM((rows, size), jnp.bfloat16) for _, size in PARTS]
    block = pltpu.VMEM((BLOCK, WIDTH), jnp.bfloat16)
    result = jax.ShapeDtypeStruct((BLOCK, WIDTH), jnp.bfloat16)
    return pl.pallas_call(
        tail_kernel,
        out_shape=(
            jax.ShapeDtypeStruct((8, 3 * WIDTH), jnp.float32),
            jax.ShapeDtypeStruct((8, WIDTH), jnp.float32),
            jax.ShapeDtypeStruct((8, OUTV), jnp.float32),
            jax.ShapeDtypeStruct((BLOCK, WIDTH), jnp.float32),
            result,
            result,
            result,
        ),
        in_specs=[pl.BlockSpec(memory_space=pl.ANY)] * len(operands),
        out_specs=(pl.BlockSpec(memory_space=pltpu.VMEM),) * 7,
        scratch_shapes=blocks * 3
        + [pltpu.VMEM((rows // 2, size), jnp.bfloat16) for _, size in PARTS]
        + [
            pltpu.VMEM((2, 8, HALF), jnp.float32),
            pltpu.VMEM((8, HALF), jnp.float32),
            pltpu.VMEM((2, WIDTH, HALF), jnp.bfloat16),
            pltpu.VMEM(terms.shape, terms.dtype),
        ]
        + [pltpu.VMEM(operand.shape, operand.dtype) for operand in others]
        + [
            pltpu.VMEM((WIDTH, BAND * BLOCK), jnp.bfloat16),
            pltpu.VMEM((WIDTH, BLOCK), jnp.bfloat16),
        ]
        + [block] * 4
        + [dma((parts, CLASSES + 1)), dma((parts, CLASSES + 1)), dma, dma]
        + [dma((PIECES,))] * 6
        + [dma, dma, dma((len(operands) + 1,))],
        compiler_params=pltpu.CompilerParams(
            collective_id=1, has_side_effects=True, vmem_limit_bytes=TAIL_VMEM
        ),
        name="tail",
    )(*operands)


def attend_kernel(q_ref, k_own_ref, k_ref, v_own_ref, v_ref, context_ref, stat_ref):
    queries = q_ref[...] * jnp.bfloat16(0.125)
    keys = jnp.concatenate([k_own_ref[...], k_ref[...]], axis=0)
    values_t = jnp.concatenate([v_own_ref[...], v_ref[...]], axis=0).T
    sides = []
    for head in range(2):
        picked = jnp.where(head_mask(queries.shape, head), queries, jnp.bfloat16(0))
        scores = lax.dot_general(keys, picked, NT, preferred_element_type=jnp.float32)
        top = jnp.max(scores, axis=0, keepdims=True)
        powers = jnp.exp(scores - top)
        total = jnp.sum(powers, axis=0, keepdims=True)
        mixed = jnp.dot(
            values_t[head * HEAD_DIM : (head + 1) * HEAD_DIM],
            powers.astype(jnp.bfloat16),
            preferred_element_type=jnp.float32,
        )
        sides.append(mixed / total)
        stat_ref[0, head : head + 1] = top + jnp.log(total)
    context_ref[...] = jnp.concatenate(sides, axis=0).T.astype(jnp.bfloat16)


PAIR = 2 * HEAD_DIM


def column_block(rows):
    return pl.BlockSpec((rows, PAIR), lambda i: (0, i))


STAT_BLOCK = pl.BlockSpec((1, 2, BLOCK), lambda i: (i, 0, 0))


def attend(q, k_own, k, v_own, v):
    keys = BAND * BLOCK
    return pl.pallas_call(
        attend_kernel,
        grid=(HEADS // 2,),
        out_shape=(
            jax.ShapeDtypeStruct((BLOCK, WIDTH), jnp.bfloat16),
            jax.ShapeDtypeStruct((HEADS // 2, 2, BLOCK), jnp.float32),
        ),
        in_specs=[column_block(array.shape[0]) for array in (q, k_own, k, v_own, v)],
        out_specs=(column_block(BLOCK), STAT_BLOCK),
        compiler_params=pltpu.CompilerParams(vmem_limit_bytes=VMEM_LIMIT),
        cost_estimate=pl.CostEstimate(
            flops=4 * BLOCK * keys * WIDTH,
            bytes_accessed=2 * WIDTH * (2 * BLOCK + 2 * keys),
            transcendentals=BLOCK * keys * HEADS,
        ),
        name="attend",
    )(q, k_own, k, v_own, v)


def back_of_pair(queries, keys, values, context, grads, stats):
    queries = queries * jnp.bfloat16(0.125)
    keys_t = keys.T
    products = (grads.astype(jnp.float32) * context.astype(jnp.float32)).T
    sides = []
    grad_keys = jnp.zeros(keys.shape, jnp.float32)
    grad_values = jnp.zeros(keys.shape, jnp.float32)
    for head in range(2):
        mask = head_mask(queries.shape, head)
        picked = jnp.where(mask, queries, jnp.bfloat16(0))
        grad_here = jnp.where(mask, grads, jnp.bfloat16(0))
        inner = jnp.sum(products[head * HEAD_DIM : (head + 1) * HEAD_DIM], axis=0, keepdims=True)
        scores = lax.dot_general(keys, picked, NT, preferred_element_type=jnp.float32)
        probs = jnp.exp(scores - stats[head])
        grad_probs = lax.dot_general(values, grad_here, NT, preferred_element_type=jnp.float32)
        grad_scores = (probs * (grad_probs - inner)).astype(jnp.bfloat16)
        grad_values += jnp.dot(
            probs.astype(jnp.bfloat16), grad_here, preferred_element_type=jnp.float32
        )
        grad_keys += jnp.dot(grad_scores, picked, preferred_element_type=jnp.float32)
        sides.append(
            jnp.dot(
                keys_t[head * HEAD_DIM : (head + 1) * HEAD_DIM],
                grad_scores,
                preferred_element_type=jnp.float32,
            )
        )
    grad_queries = (jnp.concatenate(sides, axis=0) * 0.125).T
    return grad_queries, grad_keys.astype(jnp.bfloat16), grad_values.astype(jnp.bfloat16)


def attend_back_kernel(q_ref, k_ref, v_ref, context_ref, grad_ref, stat_ref, dq_ref, dk_ref, dv_ref):
    dq_ref[...], dk_ref[...], dv_ref[...] = back_of_pair(
        q_ref[...],
        k_ref[...],
        v_ref[...],
        context_ref[...],
        grad_ref[...],
        [stat_ref[0, head : head + 1] for head in range(2)],
    )


def attend_back(q, k, v, context, grad_context, stats):
    rows, keys = q.shape[0], k.shape[0]
    return pl.pallas_call(
        attend_back_kernel,
        grid=(HEADS // 2,),
        out_shape=(
            jax.ShapeDtypeStruct((rows, WIDTH), jnp.float32),
            jax.ShapeDtypeStruct((keys, WIDTH), jnp.bfloat16),
            jax.ShapeDtypeStruct((keys, WIDTH), jnp.bfloat16),
        ),
        in_specs=[column_block(array.shape[0]) for array in (q, k, v, context, grad_context)]
        + [STAT_BLOCK],
        out_specs=(column_block(rows), column_block(keys), column_block(keys)),
        compiler_params=pltpu.CompilerParams(vmem_limit_bytes=VMEM_LIMIT),
        cost_estimate=pl.CostEstimate(
            flops=10 * rows * keys * WIDTH,
            bytes_accessed=2 * WIDTH * (4 * rows + 4 * keys),
            transcendentals=rows * keys * HEADS,
        ),
        name="attend_back",
    )(q, k, v, context, grad_context, stats)


def dot(left, right):
    return jnp.dot(left, right, preferred_element_type=jnp.float32)


def per_device(
    grid_point_features,
    projection_weights_qkv,
    merging_projection,
    readout_weights_table,
    observed,
    cell_surface_share,
    band_offsets,
    latitude_order,
):
    own_rows = grid_point_features[0]
    at = place()
    block = lax.axis_index("mp")
    normed_in = layer_norm(own_rows.astype(jnp.float32)).astype(jnp.bfloat16)

    near, far = jnp.int32(1), jnp.int32(2)
    above = jnp.where(at["y_lo"] == 0, near, far)
    below = jnp.where(at["y_lo"] == 0, far, near)
    minus = jnp.where(at["core"] == 0, 3, 0)
    plus = jnp.where(at["core"] == 0, 0, 3)
    offsets = lax.dynamic_slice(band_offsets, (block, 1), (1, 2))[0]
    slots = jnp.where(
        offsets == -2, below, jnp.where(offsets == -1, minus, jnp.where(offsets == 1, plus, above))
    ).astype(jnp.int32)

    neighbours = halo(normed_in)
    chosen = [
        lax.dynamic_index_in_dim(neighbours, slots[i], 0, keepdims=False) for i in range(BAND - 1)
    ]
    chosen = jnp.concatenate(chosen, axis=0)
    weights_q = projection_weights_qkv[:, :WIDTH]
    weights_k = projection_weights_qkv[:, WIDTH : 2 * WIDTH]
    weights_v = projection_weights_qkv[:, 2 * WIDTH :]
    q = dot(normed_in, weights_q).astype(jnp.bfloat16)
    k_own = dot(normed_in, weights_k).astype(jnp.bfloat16)
    v_own = dot(normed_in, weights_v).astype(jnp.bfloat16)
    k = dot(chosen, weights_k).astype(jnp.bfloat16)
    v = dot(chosen, weights_v).astype(jnp.bfloat16)
    context, stats = attend(q, k_own, k, v_own, v)

    hidden = (own_rows.astype(jnp.float32) + dot(context, merging_projection)).astype(jnp.bfloat16)
    normed_mid = layer_norm(hidden.astype(jnp.float32)).astype(jnp.bfloat16)
    predictions = dot(normed_mid, readout_weights_table)
    target = observed[latitude_order[0]]
    grad_forecast = crps_grad(predictions, target, cell_surface_share[:, None])

    grad_mid = dot(grad_forecast, readout_weights_table.T)
    grad_hidden = jax.vjp(layer_norm, hidden.astype(jnp.float32))[1](grad_mid)[0]
    hidden_half = grad_hidden.astype(jnp.bfloat16)
    grad_context = dot(hidden_half, merging_projection.T).astype(jnp.bfloat16)
    dq, dk, dv = attend_back(q, k, v, context, grad_context, stats)

    grad_entries = (dot(dk, weights_k.T) + dot(dv, weights_v.T)).astype(jnp.bfloat16)
    first = grad_entries[:BLOCK]
    second = grad_entries[BLOCK:]
    terms = jnp.stack(
        [
            jnp.where(slots[0] == slot, first, jnp.where(slots[1] == slot, second, jnp.bfloat16(0)))
            for slot in range(4)
        ]
    )
    grad_input, grad_output, grad_decoder, from_others, dq_own, dk_own, dv_own = tail(
        terms,
        jnp.concatenate([normed_in, chosen], axis=0),
        context,
        hidden_half,
        normed_mid,
        grad_forecast,
        q,
        k_own,
        v_own,
        grad_context,
        stats,
        dq,
        dk,
        dv,
    )
    grad_normed = (
        dot(dq_own, weights_q.T) + dot(dk_own, weights_k.T) + dot(dv_own, weights_v.T) + from_others
    )
    feature_derivative = (
        grad_hidden + jax.vjp(layer_norm, own_rows.astype(jnp.float32))[1](grad_normed)[0]
    )

    return (
        predictions[None],
        feature_derivative[None],
        grad_input,
        grad_output,
        grad_decoder,
    )


def solution(mesh):
    placed = (P("member", "mp", None), P(), P(), P(), P("mp", None), P("mp"), P(), P("mp", None))
    return jax.shard_map(
        per_device,
        mesh=mesh,
        in_specs=placed,
        out_specs=(
            P("member", "mp", None),
            P("member", "mp", None),
            P(("member", "mp"), None),
            P(("member", "mp"), None),
            P(("member", "mp"), None),
        ),
        check_vma=False,
    )
```

```python
import functools

import jax
import jax.numpy as jnp
from jax import lax
from jax.experimental import pallas as pl
from jax.experimental.pallas import tpu as pltpu
from jax.sharding import PartitionSpec as P

HEADS = 16
HEAD_DIM = 64
BLOCK = 512
WIDTH = 1024
OUTV = 128
BAND = 3

norm_epsilon = 1e-05
smooth_square = 0.0625

MESH = pl.DeviceIdType.MESH
VMEM_LIMIT = 56 * 1024 * 1024

PIECE = 64
PIECES = BLOCK // PIECE

HALF = 2176
PARTS = ((0, 384), (384, 256), (640, 256), (896, 256), (1152, 256)) + tuple(
    (1408 + 128 * i, 128) for i in range(6)
)
TILE = 16
TILES = 64
CLASSES = 6
ORDER = (1, 3, 2, 4, 0, 5)
FIRST_LINK = (2, 5, 1, 3, 4, 0, 1, 2, 3, 4, 5)
TAIL_VMEM = 60 * 1024 * 1024


def layer_norm(values):
    average = jnp.mean(values, axis=-1, keepdims=True)
    centred = values - average
    spread = jnp.mean(centred * centred, axis=-1, keepdims=True)
    return centred * lax.rsqrt(spread + norm_epsilon)


def softened_derivative(difference):
    return difference * lax.rsqrt(difference * difference + smooth_square)


NT = (((1,), (1,)), ((), ()))


def head_mask(shape, head):
    lane = lax.broadcasted_iota(jnp.int32, shape, 1)
    return (lane // HEAD_DIM) == head


def forward_of_pair(queries, keys, values):
    queries = queries * jnp.bfloat16(0.125)
    values_t = values.T
    sides, tops, totals = [], [], []
    for head in range(2):
        picked = jnp.where(head_mask(queries.shape, head), queries, jnp.bfloat16(0))
        scores = lax.dot_general(keys, picked, NT, preferred_element_type=jnp.float32)
        top = jnp.max(scores, axis=0, keepdims=True)
        powers = jnp.exp(scores - top)
        tops.append(top)
        totals.append(jnp.sum(powers, axis=0, keepdims=True))
        sides.append(
            jnp.dot(
                values_t[head * HEAD_DIM : (head + 1) * HEAD_DIM],
                powers.astype(jnp.bfloat16),
                preferred_element_type=jnp.float32,
            )
        )
    return sides, tops, totals


def place():
    member = lax.axis_index("member")
    mp = lax.axis_index("mp")
    return {
        "z": member // 2,
        "y_hi": member % 2,
        "x": mp // 4,
        "y_lo": (mp // 2) % 2,
        "core": mp % 2,
    }


def device(at):
    return (at["z"] * 2 + at["y_hi"], at["x"] * 4 + at["y_lo"] * 2 + at["core"])


def moved(at, **changes):
    return device({**at, **changes})


def greet(partners):
    barrier = pltpu.get_barrier_semaphore()
    for partner in partners:
        pl.semaphore_signal(barrier, inc=1, device_id=partner, device_id_type=MESH)
    pl.semaphore_wait(barrier, len(partners))


def remote(source, target, send, receive, partner):
    return pltpu.make_async_remote_copy(
        src_ref=source,
        dst_ref=target,
        send_sem=send,
        recv_sem=receive,
        device_id=partner,
        device_id_type=MESH,
    )


def entry_kernel(
    slots,
    own,
    weights_hbm,
    q,
    k_own,
    v_own,
    k,
    v,
    entries,
    mixed,
    tops,
    totals,
    weights,
    held,
    fetched,
    y_send,
    y_recv,
    x_send,
    x_recv,
    c_send,
    c_recv,
    o_send,
    o_recv,
):
    at = place()
    other = moved(at, core=1 - at["core"])
    across = moved(at, y_lo=1 - at["y_lo"])
    forward = moved(at, x=(at["x"] + 1 + 2 * at["y_lo"]) % 4)
    backward = moved(at, x=(at["x"] + 3 - 2 * at["y_lo"]) % 4)
    fetch = pltpu.make_async_copy(weights_hbm, weights, fetched)
    fetch.start()
    greet((other, across, forward, backward))
    near_first = (at["core"] + at["y_lo"]) % 2 == 0

    def rows(piece):
        return pl.ds(pl.multiple_of(piece * PIECE, PIECE), PIECE)

    def to_across(piece):
        return remote(
            own.at[rows(piece)], held.at[1, rows(piece)], y_send.at[piece], y_recv.at[piece], across
        )

    def to_forward(piece):
        return remote(
            held.at[1, rows(piece)],
            held.at[2, rows(piece)],
            x_send.at[piece],
            x_recv.at[piece],
            forward,
        )

    def to_other(slot, piece):
        return remote(
            held.at[slot, rows(piece)],
            held.at[3, rows(piece)],
            c_send.at[piece],
            c_recv.at[piece],
            other,
        )

    def pass_on(piece):
        to_across(piece).wait_recv()
        to_forward(piece).start()

        @pl.when(near_first)
        def _():
            to_other(1, piece).start()

    def project(target, here, source, column):
        def tile(i, carry):
            width = 256
            begin = pl.multiple_of(i * width, width)
            target[here, pl.ds(begin, width)] = jnp.dot(
                source,
                weights[:, pl.ds(pl.multiple_of(column + begin, width), width)],
                preferred_element_type=jnp.float32,
            ).astype(jnp.bfloat16)
            return carry

        lax.fori_loop(0, WIDTH // 256, tile, 0)

    def own_pair(pair, carry):
        here = pl.ds(pl.multiple_of(pair * 2 * HEAD_DIM, 2 * HEAD_DIM), 2 * HEAD_DIM)
        sides, top, total = forward_of_pair(q[:, here], k_own[:, here], v_own[:, here])
        for head in range(2):
            mixed[pair, pl.ds(head * HEAD_DIM, HEAD_DIM)] = sides[head]
            tops[pair, pl.ds(head, 1)] = top[head]
            totals[pair, pl.ds(head, 1)] = total[head]
        pass_on(pair)
        return carry

    for piece in range(PIECES):
        to_across(piece).start()
    swap = remote(own, held.at[0], o_send, o_recv, other)
    swap.start()
    everything = pl.ds(0, BLOCK)
    entries[everything] = own[...]
    fetch.wait()
    for i, target in enumerate((q, k_own, v_own)):
        project(target, everything, own[...], i * WIDTH)
    lax.fori_loop(0, PIECES, own_pair, 0)
    for piece in range(PIECES):
        to_forward(piece).wait_recv()

        @pl.when(jnp.logical_not(near_first))
        def _():
            to_other(2, piece).start()

    for piece in range(PIECES):
        to_other(1, piece).wait_recv()
    swap.wait_recv()
    for i in range(BAND - 1):
        here = pl.ds(i * BLOCK, BLOCK)
        chosen = held[slots[i]]
        entries[pl.ds((i + 1) * BLOCK, BLOCK)] = chosen
        project(k, here, chosen, WIDTH)
        project(v, here, chosen, 2 * WIDTH)
    swap.wait_send()
    for piece in range(PIECES):
        to_across(piece).wait_send()
        to_forward(piece).wait_send()
        to_other(1, piece).wait_send()


def entry(slots, own, weights):
    dma = pltpu.SemaphoreType.DMA
    pairs = HEADS // 2

    def half(rows):
        return jax.ShapeDtypeStruct((rows, WIDTH), jnp.bfloat16)

    stat = jax.ShapeDtypeStruct((pairs, 2, BLOCK), jnp.float32)
    return pl.pallas_call(
        entry_kernel,
        out_shape=(
            half(BLOCK),
            half(BLOCK),
            half(BLOCK),
            half(2 * BLOCK),
            half(2 * BLOCK),
            half(3 * BLOCK),
            jax.ShapeDtypeStruct((pairs, 2 * HEAD_DIM, BLOCK), jnp.float32),
            stat,
            stat,
        ),
        in_specs=[
            pl.BlockSpec(memory_space=pltpu.SMEM),
            pl.BlockSpec(memory_space=pltpu.VMEM),
            pl.BlockSpec(memory_space=pl.ANY),
        ],
        out_specs=(pl.BlockSpec(memory_space=pltpu.VMEM),) * 9,
        scratch_shapes=[
            pltpu.VMEM(weights.shape, jnp.bfloat16),
            pltpu.VMEM((4, BLOCK, WIDTH), jnp.bfloat16),
            dma,
        ]
        + [dma((PIECES,))] * 6
        + [dma, dma],
        compiler_params=pltpu.CompilerParams(
            collective_id=0, has_side_effects=True, vmem_limit_bytes=VMEM_LIMIT
        ),
        name="entry",
    )(slots, own, weights)


def crps_kernel(predictions, target, share, out, halves, gathered, grads, send, receive, back_send, back_recv):
    member = lax.axis_index("member")
    mp = lax.axis_index("mp")
    count = 8
    size = BLOCK // count
    greet([((member + step) % count, mp) for step in range(1, count)])

    def slice_of(index):
        return pl.ds(pl.multiple_of(index * size, size), size)

    def outward(step):
        to = (member + step) % count
        return remote(
            halves.at[slice_of(to)], gathered.at[step], send.at[step], receive.at[step], (to, mp)
        )

    def homeward(step):
        to = (member + count - step) % count
        return remote(
            grads.at[step],
            out.at[slice_of(member)],
            back_send.at[step],
            back_recv.at[step],
            (to, mp),
        )

    halves[...] = predictions[...].astype(jnp.bfloat16)
    for step in range(1, count):
        outward(step).start()
    own = slice_of(member)
    truth = target[own]
    weight = share[own]
    gathered[0] = halves[own]
    for step in range(1, count):
        outward(step).wait_recv()
    each = [gathered[step].astype(jnp.float32) for step in range(count)]
    spread = [0.0] * count
    for one in range(count):
        for two in range(one + 1, count):
            slope = softened_derivative(each[one] - each[two])
            spread[one] = spread[one] + slope
            spread[two] = spread[two] - slope
    for step in range(count):
        single = softened_derivative(each[step] - truth) / count
        paired = spread[step] / (count * (count - 1))
        grads[step] = (weight * (single - paired)).astype(jnp.bfloat16)
        if step:
            homeward(step).start()
    out[own] = grads[0]
    for step in range(1, count):
        homeward(step).wait_recv()
    for step in range(1, count):
        outward(step).wait_send()
        homeward(step).wait_send()


def crps_grad(predictions, target, share):
    dma = pltpu.SemaphoreType.DMA
    size = BLOCK // 8
    return pl.pallas_call(
        crps_kernel,
        out_shape=jax.ShapeDtypeStruct(predictions.shape, jnp.bfloat16),
        in_specs=[pl.BlockSpec(memory_space=pltpu.VMEM)] * 3,
        out_specs=pl.BlockSpec(memory_space=pltpu.VMEM),
        scratch_shapes=[
            pltpu.VMEM((BLOCK, OUTV), jnp.bfloat16),
            pltpu.VMEM((8, size, OUTV), jnp.bfloat16),
            pltpu.VMEM((8, size, OUTV), jnp.bfloat16),
        ]
        + [dma((8,))] * 4,
        compiler_params=pltpu.CompilerParams(
            collective_id=2, has_side_effects=True, vmem_limit_bytes=VMEM_LIMIT
        ),
        name="crps_grad",
    )(predictions, target, share)


def flip(bit, value):
    return (bit + value) % 2


def tail_kernel(
    terms_hbm,
    entries_hbm,
    weights_hbm,
    context_hbm,
    hidden_hbm,
    mid_hbm,
    forecast_hbm,
    q_hbm,
    k_hbm,
    v_hbm,
    grad_context_hbm,
    stats_hbm,
    dq_hbm,
    dk_hbm,
    dv_hbm,
    input_out,
    output_out,
    decoder_out,
    halo_out,
    *scratch,
):
    parts = len(PARTS)
    first_in = scratch[:parts]
    later_in = scratch[parts : 2 * parts]
    total = scratch[2 * parts : 3 * parts]
    other_total = scratch[3 * parts : 4 * parts]
    (
        last,
        last_in,
        grads,
        terms,
        context,
        hidden,
        mid,
        forecast,
        q,
        k,
        v,
        grad_context,
        stats,
        dq,
        dk,
        dv,
        entries_t,
        narrow_t,
        dq_own,
        dk_own,
        dv_own,
        cross_in,
        far_in,
        near_in,
        other_in,
        send,
        receive,
        last_send,
        last_recv,
        y_send,
        y_recv,
        x_send,
        x_recv,
        c_send,
        c_recv,
        o_send,
        o_recv,
        fetched,
    ) = scratch[4 * parts :]
    at = place()
    core = at["core"]
    x_bits = (at["x"] % 2, at["x"] // 2)
    z_bits = (at["z"] % 2, at["z"] // 2)
    y_bits = (at["y_lo"], at["y_hi"])
    other = moved(at, core=1 - core)

    landing = (
        grads.at[0, pl.ds(0, BLOCK), pl.ds(1024, WIDTH)],
        grads.at[1, pl.ds(0, 2 * BLOCK), pl.ds(1024, WIDTH)],
    )
    fetches = [
        pltpu.make_async_copy(source, target, fetched.at[i])
        for i, (source, target) in enumerate(
            (
                (terms_hbm, terms),
                (context_hbm, context),
                (hidden_hbm, hidden),
                (mid_hbm, mid),
                (forecast_hbm, forecast),
                (entries_hbm.at[pl.ds(0, BLOCK)], landing[0]),
                (entries_hbm.at[pl.ds(BLOCK, 2 * BLOCK)], landing[1]),
                (q_hbm, q),
                (k_hbm, k),
                (v_hbm, v),
                (grad_context_hbm, grad_context),
                (stats_hbm, stats),
                (dq_hbm, dq),
                (dk_hbm, dk),
                (dv_hbm, dv),
            )
        )
    ]
    fetches[0].start()

    def partner_of(link):
        low, high = 1, link // 3
        if link % 3 == 0:
            return moved(at, x=flip(x_bits[0], low) + 2 * flip(x_bits[1], high))
        if link % 3 == 1:
            return moved(at, y_lo=flip(y_bits[0], low), y_hi=flip(y_bits[1], high))
        return moved(at, z=flip(z_bits[0], low) + 2 * flip(z_bits[1], high))

    partners = [partner_of(link) for link in range(CLASSES)]
    greet([other] + partners)

    across = partners[1]
    backward = moved(at, x=(at["x"] + 3 - 2 * at["y_lo"]) % 4)
    near_first = (at["core"] + at["y_lo"]) % 2 == 0

    def rows(piece):
        return pl.ds(piece * PIECE, PIECE)

    def wide(ref, *index):
        return ref[index].astype(jnp.float32)

    def to_other(piece):
        return remote(
            terms.at[3, rows(piece)],
            cross_in.at[rows(piece)],
            c_send.at[piece],
            c_recv.at[piece],
            other,
        )

    def to_backward(piece):
        return remote(
            terms.at[2, rows(piece)], far_in.at[rows(piece)], x_send.at[piece], x_recv.at[piece], backward
        )

    def to_across(piece):
        return remote(
            terms.at[1, rows(piece)], near_in.at[rows(piece)], y_send.at[piece], y_recv.at[piece], across
        )

    swap = remote(terms.at[0], other_in, o_send, o_recv, other)

    def halo_start():
        fetches[0].wait()
        for piece in range(PIECES):
            to_other(piece).start()
        swap.start()
        for fetch in fetches[1:]:
            fetch.start()

    def over_tiles(piece, work):
        def tile(i, carry):
            work(pl.ds(pl.multiple_of(piece * PIECE + i * TILE, TILE), TILE))
            return carry

        lax.fori_loop(0, PIECE // TILE, tile, 0)

    def halo_first(pieces):
        for piece in pieces:
            to_other(piece).wait_recv()

            def add(here):
                cross = wide(cross_in, here)
                terms[2, here] = (wide(terms, 2, here) + jnp.where(near_first, 0.0, cross)).astype(
                    jnp.bfloat16
                )
                terms[1, here] = (wide(terms, 1, here) + jnp.where(near_first, cross, 0.0)).astype(
                    jnp.bfloat16
                )

            over_tiles(piece, add)
            to_backward(piece).start()

    def halo_second(pieces):
        for piece in pieces:
            to_backward(piece).wait_recv()

            def add(here):
                terms[1, here] = (wide(terms, 1, here) + wide(far_in, here)).astype(jnp.bfloat16)

            over_tiles(piece, add)
            to_across(piece).start()

    def halo_end(pieces):
        for piece in pieces:
            to_across(piece).wait_recv()

            def add(here):
                halo_out[here] = halo_out[here] + (wide(other_in, here) + wide(near_in, here))

            over_tiles(piece, add)

    def link_at(part, step):
        return ORDER[(FIRST_LINK[part] + step) % CLASSES]

    weights = (2, 1, 16, 4, 8, 32)
    places = (x_bits[0], y_bits[0], z_bits[0], x_bits[1], y_bits[1], z_bits[1])
    turns = [TILE * weight * (1 - 2 * bit) for weight, bit in zip(weights, places)]
    tile_rows = [TILE * sum(weight * bit for weight, bit in zip(weights, places))]
    for turn in turns:
        tile_rows = tile_rows + [row + turn for row in tile_rows]

    def tile_row(part, position):
        mask = 0
        for step in range(CLASSES):
            if position & (TILES >> (step + 1)):
                link = link_at(part, step)
                mask ^= (1 << link) | (1 << (link % 3))
        return pl.multiple_of(tile_rows[mask], TILE)

    def first_copy(part):
        start, size = PARTS[part]
        return remote(
            grads.at[1 - core, :, pl.ds(start, size)],
            first_in[part],
            send.at[part, 0],
            receive.at[part, 0],
            other,
        )

    def kept(step):
        return (TILES >> step) * TILE

    def pair_of(part, step):
        pair = (total[part], other_total[part])
        return pair if step % 2 else pair[::-1]

    def later_copy(part, step):
        count = kept(step)
        return remote(
            pair_of(part, step)[0].at[pl.ds(count, count)],
            later_in[part].at[pl.ds(count, count)],
            send.at[part, step],
            receive.at[part, step],
            partners[link_at(part, step - 1)],
        )

    def product(terms_of, width, column, half):
        summed = 0.0
        for left, right, begin in terms_of:
            summed = summed + jnp.dot(
                left[...], right[:, pl.ds(begin, width)], preferred_element_type=jnp.float32
            )
        grads[half, :, pl.ds(column, width)] = summed.astype(jnp.bfloat16)

    own_t = entries_t.at[:, pl.ds(0, BLOCK)]
    chosen_t = entries_t.at[:, pl.ds(BLOCK, 2 * BLOCK)]

    def products_of(group):
        column = 640 + 768 * group
        for half in range(2):
            begin = 512 * group + 256 * half
            product([(own_t, dq_own, begin)], 256, column, half)
            product([(own_t, dk_own, begin), (chosen_t, dk, begin)], 256, column + 256, half)
            product([(own_t, dv_own, begin), (chosen_t, dv, begin)], 256, column + 512, half)

    weights = (
        grads.at[0, :, pl.ds(0, WIDTH)],
        grads.at[0, :, pl.ds(WIDTH, WIDTH)],
        grads.at[1, :, pl.ds(0, WIDTH)],
    )
    weight_fetches = [
        pltpu.make_async_copy(
            weights_hbm.at[:, pl.ds(i * WIDTH, WIDTH)], weights[i], fetched.at[len(fetches) + i]
        )
        for i in range(3)
    ]

    def own_part(quarter):
        here = pl.ds(quarter * 256, 256)
        summed = 0.0
        for grad, weight in zip((dq_own, dk_own, dv_own), weights):
            summed = summed + lax.dot_general(
                grad[...], weight[here], NT, preferred_element_type=jnp.float32
            )
        halo_out[:, here] = summed

    def own_pair(pair, carry):
        here = pl.ds(pl.multiple_of(pair * 2 * HEAD_DIM, 2 * HEAD_DIM), 2 * HEAD_DIM)
        queries, grad_keys, grad_values = back_of_pair(
            q[:, here],
            k[:, here],
            v[:, here],
            context[:, here],
            grad_context[:, here],
            [stats[pair, head : head + 1] for head in range(2)],
        )
        dq_own[:, here] = (queries + dq[:, here]).astype(jnp.bfloat16)
        dk_own[:, here] = grad_keys
        dv_own[:, here] = grad_values
        return carry

    def merge_first(part):
        start, size = PARTS[part]
        first_copy(part).wait_recv()

        def merge(positions):
            for position in positions:
                source = pl.ds(tile_row(part, position), TILE)
                total[part][pl.ds(position * TILE, TILE)] = (
                    grads[core, source, pl.ds(start, size)] + first_in[part][source]
                )

        merge(range(TILES // 2, TILES))
        later_copy(part, 1).start()
        merge(range(TILES // 2))

    def merge_later(part, step):
        start, size = PARTS[part]
        count = kept(step)
        held, made = pair_of(part, step)
        later_copy(part, step).wait_recv()
        if step < CLASSES:
            half = count // 2
            for begin in (half, 0):
                made[pl.ds(begin, half)] = (
                    held[pl.ds(begin, half)] + later_in[part][pl.ds(count + begin, half)]
                )
                if begin == half:
                    later_copy(part, step + 1).start()
        else:
            final = wide(held, pl.ds(0, TILE)) + wide(later_in[part], pl.ds(TILE, TILE))
            last[:, :, pl.ds(start, size)] = final.reshape(2, 8, size)

    halo_start()
    fetches[1].wait()
    narrow_t[...] = context[...].T
    fetches[2].wait()
    for half in range(2):
        for part in range(2):
            product([(narrow_t, hidden, 512 * half + 256 * part)], 256, 256 * part, half)
    first_copy(0).start()
    halo_first(range(PIECES))
    fetches[3].wait()
    narrow_t[...] = mid[...].T
    fetches[4].wait()
    product([(narrow_t, forecast, 0)], OUTV, 512, 0)
    grads[1, :, pl.ds(512, OUTV)] = jnp.zeros((WIDTH, OUTV), jnp.bfloat16)
    first_copy(1).start()
    fetches[5].wait()
    entries_t[:, pl.ds(0, BLOCK)] = grads[0, pl.ds(0, BLOCK), pl.ds(1024, WIDTH)].T
    fetches[6].wait()
    for block in range(2):
        entries_t[:, pl.ds((block + 1) * BLOCK, BLOCK)] = grads[
            1, pl.ds(block * BLOCK, BLOCK), pl.ds(1024, WIDTH)
        ].T
    merge_first(0)
    merge_first(1)
    for i in range(7, 13):
        fetches[i].wait()
    lax.fori_loop(0, 4, own_pair, 0)
    halo_second(range(0, 2))
    fetches[13].wait()
    fetches[14].wait()
    products_of(0)
    for part in (2, 3, 4):
        first_copy(part).start()
    merge_later(0, 1)
    merge_later(1, 1)
    halo_second(range(2, 4))
    for part in (2, 3, 4):
        merge_first(part)
    lax.fori_loop(4, 8, own_pair, 0)
    merge_later(0, 2)
    merge_later(1, 2)
    halo_second(range(4, 6))
    for part in (2, 3, 4):
        merge_later(part, 1)
    products_of(1)
    for part in range(5, 11):
        first_copy(part).start()
    merge_later(0, 3)
    merge_later(1, 3)
    for part in (2, 3, 4):
        merge_later(part, 2)
    halo_second(range(6, 8))
    for part in range(5, 11):
        merge_first(part)
    for part in range(parts):
        first_copy(part).wait_send()
    for fetch in weight_fetches:
        fetch.start()
    for step in range(1, CLASSES + 1):
        for part, ahead in ((0, 3), (1, 3), (2, 2), (3, 2), (4, 2)):
            if step + ahead <= CLASSES:
                merge_later(part, step + ahead)
        if step == 1:
            for fetch in weight_fetches:
                fetch.wait()
            for quarter in range(2):
                own_part(quarter)
        if step == 2:
            for quarter in range(2, 4):
                own_part(quarter)
            swap.wait_recv()
        if step >= 3:
            halo_end(range(2 * step - 6, 2 * step - 4))
        for part in range(5, 11):
            merge_later(part, step)
    finish = remote(last.at[1 - core], last_in, last_send, last_recv, other)
    finish.start()

    def deliver(half, source):
        def columns(begin, size):
            return pl.ds(pl.multiple_of(begin, 128), size)

        output_out[:, columns(512 * half, 512)] = source[:, pl.ds(0, 512)]
        for group in range(2):
            for kind in range(3):
                input_out[:, columns(1024 * kind + 512 * group + 256 * half, 256)] = source[
                    :, pl.ds(640 + 768 * group + 256 * kind, 256)
                ]

    deliver(core, last.at[core])
    finish.wait()
    deliver(1 - core, last_in)
    decoder_out[...] = jnp.where(core == 0, last[0, :, pl.ds(512, OUTV)], last_in[:, pl.ds(512, OUTV)])
    swap.wait_send()
    for piece in range(PIECES):
        to_other(piece).wait_send()
        to_backward(piece).wait_send()
        to_across(piece).wait_send()
    for part in range(parts):
        for step in range(1, CLASSES + 1):
            later_copy(part, step).wait_send()


def tail(terms, entries, weights, *others):
    dma = pltpu.SemaphoreType.DMA
    parts = len(PARTS)
    rows = TILES * TILE
    operands = (terms, entries, weights) + others
    blocks = [pltpu.VMEM((rows, size), jnp.bfloat16) for _, size in PARTS]
    block = pltpu.VMEM((BLOCK, WIDTH), jnp.bfloat16)
    return pl.pallas_call(
        tail_kernel,
        out_shape=(
            jax.ShapeDtypeStruct((8, 3 * WIDTH), jnp.float32),
            jax.ShapeDtypeStruct((8, WIDTH), jnp.float32),
            jax.ShapeDtypeStruct((8, OUTV), jnp.float32),
            jax.ShapeDtypeStruct((BLOCK, WIDTH), jnp.float32),
        ),
        in_specs=[pl.BlockSpec(memory_space=pl.ANY)] * len(operands),
        out_specs=(pl.BlockSpec(memory_space=pltpu.VMEM),) * 4,
        scratch_shapes=blocks * 3
        + [pltpu.VMEM((rows // 2, size), jnp.bfloat16) for _, size in PARTS]
        + [
            pltpu.VMEM((2, 8, HALF), jnp.float32),
            pltpu.VMEM((8, HALF), jnp.float32),
            pltpu.VMEM((2, WIDTH, HALF), jnp.bfloat16),
            pltpu.VMEM(terms.shape, terms.dtype),
        ]
        + [pltpu.VMEM(operand.shape, operand.dtype) for operand in others]
        + [
            pltpu.VMEM((WIDTH, BAND * BLOCK), jnp.bfloat16),
            pltpu.VMEM((WIDTH, BLOCK), jnp.bfloat16),
        ]
        + [block] * 7
        + [dma((parts, CLASSES + 1)), dma((parts, CLASSES + 1)), dma, dma]
        + [dma((PIECES,))] * 6
        + [dma, dma, dma((len(operands) + 3,))],
        compiler_params=pltpu.CompilerParams(
            collective_id=1, has_side_effects=True, vmem_limit_bytes=TAIL_VMEM
        ),
        name="tail",
    )(*operands)


def attend_kernel(q_ref, k_ref, v_ref, mixed_ref, top_ref, total_ref, context_ref, stat_ref):
    sides, tops, totals = forward_of_pair(q_ref[...], k_ref[...], v_ref[...])
    whole = []
    for head in range(2):
        own_top = top_ref[0, head : head + 1]
        top = jnp.maximum(own_top, tops[head])
        own_share = jnp.exp(own_top - top)
        share = jnp.exp(tops[head] - top)
        total = own_share * total_ref[0, head : head + 1] + share * totals[head]
        own_mixed = mixed_ref[0, head * HEAD_DIM : (head + 1) * HEAD_DIM]
        whole.append((own_share * own_mixed + share * sides[head]) / total)
        stat_ref[0, head : head + 1] = top + jnp.log(total)
    context_ref[...] = jnp.concatenate(whole, axis=0).T.astype(jnp.bfloat16)


PAIR = 2 * HEAD_DIM


def column_block(rows):
    return pl.BlockSpec((rows, PAIR), lambda i: (0, i))


STAT_BLOCK = pl.BlockSpec((1, 2, BLOCK), lambda i: (i, 0, 0))


def attend(q, k, v, mixed, tops, totals):
    keys = k.shape[0]
    return pl.pallas_call(
        attend_kernel,
        grid=(HEADS // 2,),
        out_shape=(
            jax.ShapeDtypeStruct((BLOCK, WIDTH), jnp.bfloat16),
            jax.ShapeDtypeStruct((HEADS // 2, 2, BLOCK), jnp.float32),
        ),
        in_specs=[column_block(array.shape[0]) for array in (q, k, v)]
        + [pl.BlockSpec((1, PAIR, BLOCK), lambda i: (i, 0, 0)), STAT_BLOCK, STAT_BLOCK],
        out_specs=(column_block(BLOCK), STAT_BLOCK),
        compiler_params=pltpu.CompilerParams(vmem_limit_bytes=VMEM_LIMIT),
        cost_estimate=pl.CostEstimate(
            flops=4 * BLOCK * keys * WIDTH,
            bytes_accessed=2 * WIDTH * (2 * BLOCK + 2 * keys),
            transcendentals=BLOCK * keys * HEADS,
        ),
        name="attend",
    )(q, k, v, mixed, tops, totals)


def back_of_pair(queries, keys, values, context, grads, stats):
    queries = queries * jnp.bfloat16(0.125)
    keys_t = keys.T
    products = (grads.astype(jnp.float32) * context.astype(jnp.float32)).T
    sides = []
    grad_keys = jnp.zeros(keys.shape, jnp.float32)
    grad_values = jnp.zeros(keys.shape, jnp.float32)
    for head in range(2):
        mask = head_mask(queries.shape, head)
        picked = jnp.where(mask, queries, jnp.bfloat16(0))
        grad_here = jnp.where(mask, grads, jnp.bfloat16(0))
        inner = jnp.sum(products[head * HEAD_DIM : (head + 1) * HEAD_DIM], axis=0, keepdims=True)
        scores = lax.dot_general(keys, picked, NT, preferred_element_type=jnp.float32)
        probs = jnp.exp(scores - stats[head])
        grad_probs = lax.dot_general(values, grad_here, NT, preferred_element_type=jnp.float32)
        grad_scores = (probs * (grad_probs - inner)).astype(jnp.bfloat16)
        grad_values += jnp.dot(
            probs.astype(jnp.bfloat16), grad_here, preferred_element_type=jnp.float32
        )
        grad_keys += jnp.dot(grad_scores, picked, preferred_element_type=jnp.float32)
        sides.append(
            jnp.dot(
                keys_t[head * HEAD_DIM : (head + 1) * HEAD_DIM],
                grad_scores,
                preferred_element_type=jnp.float32,
            )
        )
    grad_queries = (jnp.concatenate(sides, axis=0) * 0.125).T
    return grad_queries, grad_keys.astype(jnp.bfloat16), grad_values.astype(jnp.bfloat16)


def attend_back_kernel(q_ref, k_ref, v_ref, context_ref, grad_ref, stat_ref, dq_ref, dk_ref, dv_ref):
    dq_ref[...], dk_ref[...], dv_ref[...] = back_of_pair(
        q_ref[...],
        k_ref[...],
        v_ref[...],
        context_ref[...],
        grad_ref[...],
        [stat_ref[0, head : head + 1] for head in range(2)],
    )


def attend_back(q, k, v, context, grad_context, stats):
    rows, keys = q.shape[0], k.shape[0]
    return pl.pallas_call(
        attend_back_kernel,
        grid=(HEADS // 2,),
        out_shape=(
            jax.ShapeDtypeStruct((rows, WIDTH), jnp.float32),
            jax.ShapeDtypeStruct((keys, WIDTH), jnp.bfloat16),
            jax.ShapeDtypeStruct((keys, WIDTH), jnp.bfloat16),
        ),
        in_specs=[column_block(array.shape[0]) for array in (q, k, v, context, grad_context)]
        + [STAT_BLOCK],
        out_specs=(column_block(rows), column_block(keys), column_block(keys)),
        compiler_params=pltpu.CompilerParams(vmem_limit_bytes=VMEM_LIMIT),
        cost_estimate=pl.CostEstimate(
            flops=10 * rows * keys * WIDTH,
            bytes_accessed=2 * WIDTH * (4 * rows + 4 * keys),
            transcendentals=rows * keys * HEADS,
        ),
        name="attend_back",
    )(q, k, v, context, grad_context, stats)


def dot(left, right):
    return jnp.dot(left, right, preferred_element_type=jnp.float32)


def per_device(
    grid_point_features,
    projection_weights_qkv,
    merging_projection,
    readout_weights_table,
    observed,
    cell_surface_share,
    band_offsets,
    latitude_order,
):
    own_rows = grid_point_features[0]
    at = place()
    block = lax.axis_index("mp")
    normed_in = layer_norm(own_rows.astype(jnp.float32)).astype(jnp.bfloat16)

    near, far = jnp.int32(1), jnp.int32(2)
    above = jnp.where(at["y_lo"] == 0, near, far)
    below = jnp.where(at["y_lo"] == 0, far, near)
    minus = jnp.where(at["core"] == 0, 3, 0)
    plus = jnp.where(at["core"] == 0, 0, 3)
    offsets = lax.dynamic_slice(band_offsets, (block, 1), (1, 2))[0]
    slots = jnp.where(
        offsets == -2, below, jnp.where(offsets == -1, minus, jnp.where(offsets == 1, plus, above))
    ).astype(jnp.int32)

    q, k_own, v_own, k, v, entries, mixed, tops, totals = entry(
        slots, normed_in, projection_weights_qkv
    )
    weights_k = projection_weights_qkv[:, WIDTH : 2 * WIDTH]
    weights_v = projection_weights_qkv[:, 2 * WIDTH :]
    context, stats = attend(q, k, v, mixed, tops, totals)

    hidden = (own_rows.astype(jnp.float32) + dot(context, merging_projection)).astype(jnp.bfloat16)
    normed_mid = layer_norm(hidden.astype(jnp.float32)).astype(jnp.bfloat16)
    predictions = dot(normed_mid, readout_weights_table)
    target = observed[latitude_order[0]]
    grad_forecast = crps_grad(predictions, target, cell_surface_share[:, None])

    grad_mid = dot(grad_forecast, readout_weights_table.T)
    grad_hidden = jax.vjp(layer_norm, hidden.astype(jnp.float32))[1](grad_mid)[0]
    hidden_half = grad_hidden.astype(jnp.bfloat16)
    grad_context = dot(hidden_half, merging_projection.T).astype(jnp.bfloat16)
    dq, dk, dv = attend_back(q, k, v, context, grad_context, stats)

    grad_entries = (dot(dk, weights_k.T) + dot(dv, weights_v.T)).astype(jnp.bfloat16)
    first = grad_entries[:BLOCK]
    second = grad_entries[BLOCK:]
    terms = jnp.stack(
        [
            jnp.where(slots[0] == slot, first, jnp.where(slots[1] == slot, second, jnp.bfloat16(0)))
            for slot in range(4)
        ]
    )
    grad_input, grad_output, grad_decoder, grad_normed = tail(
        terms,
        entries,
        projection_weights_qkv,
        context,
        hidden_half,
        normed_mid,
        grad_forecast,
        q,
        k_own,
        v_own,
        grad_context,
        stats,
        dq,
        dk,
        dv,
    )
    feature_derivative = (
        grad_hidden + jax.vjp(layer_norm, own_rows.astype(jnp.float32))[1](grad_normed)[0]
    )

    return (
        predictions[None],
        feature_derivative[None],
        grad_input,
        grad_output,
        grad_decoder,
    )


def solution(mesh):
    placed = (P("member", "mp", None), P(), P(), P(), P("mp", None), P("mp"), P(), P("mp", None))
    return jax.shard_map(
        per_device,
        mesh=mesh,
        in_specs=placed,
        out_specs=(
            P("member", "mp", None),
            P("member", "mp", None),
            P(("member", "mp"), None),
            P(("member", "mp"), None),
            P(("member", "mp"), None),
        ),
        check_vma=False,
    )
```

```python
import functools

import jax
import jax.numpy as jnp
from jax import lax
from jax.experimental import pallas as pl
from jax.experimental.pallas import tpu as pltpu
from jax.sharding import PartitionSpec as P

HEADS = 16
HEAD_DIM = 64
BLOCK = 512
WIDTH = 1024
OUTV = 128
BAND = 3

norm_epsilon = 1e-05
smooth_square = 0.0625

MESH = pl.DeviceIdType.MESH
VMEM_LIMIT = 56 * 1024 * 1024

PIECE = 64
PIECES = BLOCK // PIECE

HALF = 2176
PARTS = ((0, 384), (384, 256), (640, 256), (896, 256), (1152, 256)) + tuple(
    (1408 + 128 * i, 128) for i in range(6)
)
TILE = 16
TILES = 64
CLASSES = 6
ORDER = (1, 3, 2, 4, 0, 5)
FIRST_LINK = (2, 5, 1, 3, 4, 0, 1, 2, 3, 4, 5)
TAIL_VMEM = 60 * 1024 * 1024


def layer_norm(values):
    average = jnp.mean(values, axis=-1, keepdims=True)
    centred = values - average
    spread = jnp.mean(centred * centred, axis=-1, keepdims=True)
    return centred * lax.rsqrt(spread + norm_epsilon)


def softened_derivative(difference):
    return difference * lax.rsqrt(difference * difference + smooth_square)


NT = (((1,), (1,)), ((), ()))


def head_mask(shape, head):
    lane = lax.broadcasted_iota(jnp.int32, shape, 1)
    return (lane // HEAD_DIM) == head


def forward_of_pair(queries, keys, values):
    queries = queries * jnp.bfloat16(0.125)
    values_t = values.T
    sides, tops, totals = [], [], []
    for head in range(2):
        picked = jnp.where(head_mask(queries.shape, head), queries, jnp.bfloat16(0))
        scores = lax.dot_general(keys, picked, NT, preferred_element_type=jnp.float32)
        top = jnp.max(scores, axis=0, keepdims=True)
        powers = jnp.exp(scores - top)
        tops.append(top)
        totals.append(jnp.sum(powers, axis=0, keepdims=True))
        sides.append(
            jnp.dot(
                values_t[head * HEAD_DIM : (head + 1) * HEAD_DIM],
                powers.astype(jnp.bfloat16),
                preferred_element_type=jnp.float32,
            )
        )
    return sides, tops, totals


def place():
    member = lax.axis_index("member")
    mp = lax.axis_index("mp")
    return {
        "z": member // 2,
        "y_hi": member % 2,
        "x": mp // 4,
        "y_lo": (mp // 2) % 2,
        "core": mp % 2,
    }


def device(at):
    return (at["z"] * 2 + at["y_hi"], at["x"] * 4 + at["y_lo"] * 2 + at["core"])


def moved(at, **changes):
    return device({**at, **changes})


def greet(partners):
    barrier = pltpu.get_barrier_semaphore()
    for partner in partners:
        pl.semaphore_signal(barrier, inc=1, device_id=partner, device_id_type=MESH)
    pl.semaphore_wait(barrier, len(partners))


def remote(source, target, send, receive, partner):
    return pltpu.make_async_remote_copy(
        src_ref=source,
        dst_ref=target,
        send_sem=send,
        recv_sem=receive,
        device_id=partner,
        device_id_type=MESH,
    )


def entry_kernel(
    slots,
    raw,
    weights_hbm,
    q_hbm,
    k_own_hbm,
    v_own_hbm,
    k_hbm,
    v_hbm,
    entries_hbm,
    mixed_hbm,
    tops,
    totals,
    q,
    k_own,
    v_own,
    k,
    v,
    entries,
    mixed,
    weights,
    held,
    fetched,
    stored,
    y_send,
    y_recv,
    x_send,
    x_recv,
    c_send,
    c_recv,
    o_send,
    o_recv,
):
    at = place()
    other = moved(at, core=1 - at["core"])
    across = moved(at, y_lo=1 - at["y_lo"])
    forward = moved(at, x=(at["x"] + 1 + 2 * at["y_lo"]) % 4)
    backward = moved(at, x=(at["x"] + 3 - 2 * at["y_lo"]) % 4)
    fetch = pltpu.make_async_copy(weights_hbm, weights, fetched)
    fetch.start()
    greet((other, across, forward, backward))
    near_first = (at["core"] + at["y_lo"]) % 2 == 0
    own = entries.at[pl.ds(0, BLOCK)]

    def store(source, target, place_of):
        return pltpu.make_async_copy(source, target, stored.at[place_of])

    early = [
        store(q, q_hbm, 0),
        store(k_own, k_own_hbm, 1),
        store(v_own, v_own_hbm, 2),
        store(own, entries_hbm.at[pl.ds(0, BLOCK)], 3),
        store(mixed, mixed_hbm, 4),
    ]
    late = [
        [
            store(source.at[pl.ds(begin, BLOCK)], target.at[pl.ds(begin, BLOCK)], 5 + 3 * i + j)
            for j, (source, target, begin) in enumerate(
                (
                    (k, k_hbm, i * BLOCK),
                    (v, v_hbm, i * BLOCK),
                    (entries, entries_hbm, (i + 1) * BLOCK),
                )
            )
        ]
        for i in range(BAND - 1)
    ]

    def rows(piece):
        return pl.ds(pl.multiple_of(piece * PIECE, PIECE), PIECE)

    def to_across(piece):
        return remote(
            own.at[rows(piece)], held.at[1, rows(piece)], y_send.at[piece], y_recv.at[piece], across
        )

    def to_forward(piece):
        return remote(
            held.at[1, rows(piece)],
            held.at[2, rows(piece)],
            x_send.at[piece],
            x_recv.at[piece],
            forward,
        )

    def to_other(slot, piece):
        return remote(
            held.at[slot, rows(piece)],
            held.at[3, rows(piece)],
            c_send.at[piece],
            c_recv.at[piece],
            other,
        )

    def pass_on(piece):
        to_across(piece).wait_recv()
        to_forward(piece).start()

        @pl.when(near_first)
        def _():
            to_other(1, piece).start()

    def project(target, here, source, column):
        def tile(i, carry):
            width = 256
            begin = pl.multiple_of(i * width, width)
            target[here, pl.ds(begin, width)] = jnp.dot(
                source,
                weights[:, pl.ds(pl.multiple_of(column + begin, width), width)],
                preferred_element_type=jnp.float32,
            ).astype(jnp.bfloat16)
            return carry

        lax.fori_loop(0, WIDTH // 256, tile, 0)

    def own_pair(pair, carry):
        here = pl.ds(pl.multiple_of(pair * 2 * HEAD_DIM, 2 * HEAD_DIM), 2 * HEAD_DIM)
        sides, top, total = forward_of_pair(q[:, here], k_own[:, here], v_own[:, here])
        for head in range(2):
            mixed[pair, pl.ds(head * HEAD_DIM, HEAD_DIM)] = sides[head]
            tops[pair, pl.ds(head, 1)] = top[head]
            totals[pair, pl.ds(head, 1)] = total[head]
        pass_on(pair)
        return carry

    def normalise(piece, carry):
        own[rows(piece)] = layer_norm(raw[rows(piece)].astype(jnp.float32)).astype(jnp.bfloat16)
        to_across(piece).start()
        return carry

    lax.fori_loop(0, PIECES, normalise, 0)
    swap = remote(own, held.at[0], o_send, o_recv, other)
    swap.start()
    early[3].start()
    everything = pl.ds(0, BLOCK)
    fetch.wait()
    for i, target in enumerate((q, k_own, v_own)):
        project(target, everything, own[...], i * WIDTH)
        early[i].start()
    lax.fori_loop(0, PIECES, own_pair, 0)
    early[4].start()
    for piece in range(PIECES):
        to_forward(piece).wait_recv()

        @pl.when(jnp.logical_not(near_first))
        def _():
            to_other(2, piece).start()

    for piece in range(PIECES):
        to_other(1, piece).wait_recv()
    swap.wait_recv()
    for i in range(BAND - 1):
        here = pl.ds(i * BLOCK, BLOCK)
        chosen = held[slots[i]]
        entries[pl.ds((i + 1) * BLOCK, BLOCK)] = chosen
        late[i][2].start()
        project(k, here, chosen, WIDTH)
        late[i][0].start()
        project(v, here, chosen, 2 * WIDTH)
        late[i][1].start()
    for copy in early + late[0] + late[1]:
        copy.wait()
    swap.wait_send()
    for piece in range(PIECES):
        to_across(piece).wait_send()
        to_forward(piece).wait_send()
        to_other(1, piece).wait_send()


def entry(slots, own, weights):
    dma = pltpu.SemaphoreType.DMA
    pairs = HEADS // 2

    def half(rows):
        return jax.ShapeDtypeStruct((rows, WIDTH), jnp.bfloat16)

    stat = jax.ShapeDtypeStruct((pairs, 2, BLOCK), jnp.float32)
    return pl.pallas_call(
        entry_kernel,
        out_shape=(
            half(BLOCK),
            half(BLOCK),
            half(BLOCK),
            half(2 * BLOCK),
            half(2 * BLOCK),
            half(3 * BLOCK),
            jax.ShapeDtypeStruct((pairs, 2 * HEAD_DIM, BLOCK), jnp.float32),
            stat,
            stat,
        ),
        in_specs=[
            pl.BlockSpec(memory_space=pltpu.SMEM),
            pl.BlockSpec(memory_space=pltpu.VMEM),
            pl.BlockSpec(memory_space=pl.ANY),
        ],
        out_specs=(pl.BlockSpec(memory_space=pl.ANY),) * 7
        + (pl.BlockSpec(memory_space=pltpu.VMEM),) * 2,
        scratch_shapes=[pltpu.VMEM((count * BLOCK, WIDTH), jnp.bfloat16) for count in (1, 1, 1, 2, 2, 3)]
        + [
            pltpu.VMEM((pairs, 2 * HEAD_DIM, BLOCK), jnp.float32),
            pltpu.VMEM(weights.shape, jnp.bfloat16),
            pltpu.VMEM((4, BLOCK, WIDTH), jnp.bfloat16),
            dma,
            dma((11,)),
        ]
        + [dma((PIECES,))] * 6
        + [dma, dma],
        compiler_params=pltpu.CompilerParams(
            collective_id=0, has_side_effects=True, vmem_limit_bytes=VMEM_LIMIT
        ),
        name="entry",
    )(slots, own, weights)


def crps_kernel(
    predictions,
    target,
    share,
    entries,
    context,
    out,
    entries_t,
    context_t,
    halves,
    gathered,
    grads,
    send,
    receive,
    back_send,
    back_recv,
):
    member = lax.axis_index("member")
    mp = lax.axis_index("mp")
    count = 8
    size = BLOCK // count
    greet([((member + step) % count, mp) for step in range(1, count)])

    def slice_of(index):
        return pl.ds(pl.multiple_of(index * size, size), size)

    def outward(step):
        to = (member + step) % count
        return remote(
            halves.at[slice_of(to)], gathered.at[step], send.at[step], receive.at[step], (to, mp)
        )

    def homeward(step):
        to = (member + count - step) % count
        return remote(
            grads.at[step],
            out.at[slice_of(member)],
            back_send.at[step],
            back_recv.at[step],
            (to, mp),
        )

    halves[...] = predictions[...].astype(jnp.bfloat16)
    for step in range(1, count):
        outward(step).start()
    own = slice_of(member)
    truth = target[own]
    weight = share[own]
    gathered[0] = halves[own]
    for block in range(2):
        here = pl.ds(block * BLOCK, BLOCK)
        entries_t[:, here] = entries[here].T
    for step in range(1, count):
        outward(step).wait_recv()
    each = [gathered[step].astype(jnp.float32) for step in range(count)]
    spread = [0.0] * count
    for one in range(count):
        for two in range(one + 1, count):
            slope = softened_derivative(each[one] - each[two])
            spread[one] = spread[one] + slope
            spread[two] = spread[two] - slope
    for step in range(count):
        single = softened_derivative(each[step] - truth) / count
        paired = spread[step] / (count * (count - 1))
        grads[step] = (weight * (single - paired)).astype(jnp.bfloat16)
        if step:
            homeward(step).start()
    out[own] = grads[0]
    entries_t[:, pl.ds(2 * BLOCK, BLOCK)] = entries[pl.ds(2 * BLOCK, BLOCK)].T
    context_t[...] = context[...].T
    for step in range(1, count):
        homeward(step).wait_recv()
    for step in range(1, count):
        outward(step).wait_send()
        homeward(step).wait_send()


def crps_grad(predictions, target, share, entries, context):
    dma = pltpu.SemaphoreType.DMA
    size = BLOCK // 8
    return pl.pallas_call(
        crps_kernel,
        out_shape=(
            jax.ShapeDtypeStruct(predictions.shape, jnp.bfloat16),
            jax.ShapeDtypeStruct(entries.shape[::-1], jnp.bfloat16),
            jax.ShapeDtypeStruct(context.shape[::-1], jnp.bfloat16),
        ),
        in_specs=[pl.BlockSpec(memory_space=pltpu.VMEM)] * 5,
        out_specs=(pl.BlockSpec(memory_space=pltpu.VMEM),) * 3,
        scratch_shapes=[
            pltpu.VMEM((BLOCK, OUTV), jnp.bfloat16),
            pltpu.VMEM((8, size, OUTV), jnp.bfloat16),
            pltpu.VMEM((8, size, OUTV), jnp.bfloat16),
        ]
        + [dma((8,))] * 4,
        compiler_params=pltpu.CompilerParams(
            collective_id=2, has_side_effects=True, vmem_limit_bytes=VMEM_LIMIT
        ),
        name="crps_grad",
    )(predictions, target, share, entries, context)


def flip(bit, value):
    return (bit + value) % 2


def tail_kernel(
    terms_hbm,
    entries_t_hbm,
    context_t_hbm,
    weights_hbm,
    context_hbm,
    hidden_hbm,
    mid_hbm,
    forecast_hbm,
    q_hbm,
    k_hbm,
    v_hbm,
    grad_context_hbm,
    stats_hbm,
    dq_hbm,
    dk_hbm,
    dv_hbm,
    input_out,
    output_out,
    decoder_out,
    halo_out,
    *scratch,
):
    parts = len(PARTS)
    first_in = scratch[:parts]
    later_in = scratch[parts : 2 * parts]
    total = scratch[2 * parts : 3 * parts]
    other_total = scratch[3 * parts : 4 * parts]
    (
        last,
        last_in,
        grads,
        terms,
        context,
        hidden,
        mid,
        forecast,
        q,
        k,
        v,
        grad_context,
        stats,
        dq,
        dk,
        dv,
        entries_t,
        narrow_t,
        dq_own,
        dk_own,
        dv_own,
        cross_in,
        far_in,
        near_in,
        other_in,
        send,
        receive,
        last_send,
        last_recv,
        y_send,
        y_recv,
        x_send,
        x_recv,
        c_send,
        c_recv,
        o_send,
        o_recv,
        fetched,
    ) = scratch[4 * parts :]
    at = place()
    core = at["core"]
    x_bits = (at["x"] % 2, at["x"] // 2)
    z_bits = (at["z"] % 2, at["z"] // 2)
    y_bits = (at["y_lo"], at["y_hi"])
    other = moved(at, core=1 - core)

    fetches = [
        pltpu.make_async_copy(source, target, fetched.at[i])
        for i, (source, target) in enumerate(
            (
                (terms_hbm, terms),
                (context_t_hbm, narrow_t),
                (hidden_hbm, hidden),
                (mid_hbm, mid),
                (forecast_hbm, forecast),
                (entries_t_hbm, entries_t),
                (context_hbm, context),
                (q_hbm, q),
                (k_hbm, k),
                (v_hbm, v),
                (grad_context_hbm, grad_context),
                (stats_hbm, stats),
                (dq_hbm, dq),
                (dk_hbm, dk),
                (dv_hbm, dv),
            )
        )
    ]
    fetches[0].start()

    def partner_of(link):
        low, high = 1, link // 3
        if link % 3 == 0:
            return moved(at, x=flip(x_bits[0], low) + 2 * flip(x_bits[1], high))
        if link % 3 == 1:
            return moved(at, y_lo=flip(y_bits[0], low), y_hi=flip(y_bits[1], high))
        return moved(at, z=flip(z_bits[0], low) + 2 * flip(z_bits[1], high))

    partners = [partner_of(link) for link in range(CLASSES)]
    greet([other] + partners)

    across = partners[1]
    backward = moved(at, x=(at["x"] + 3 - 2 * at["y_lo"]) % 4)
    near_first = (at["core"] + at["y_lo"]) % 2 == 0

    def rows(piece):
        return pl.ds(piece * PIECE, PIECE)

    def wide(ref, *index):
        return ref[index].astype(jnp.float32)

    def to_other(piece):
        return remote(
            terms.at[3, rows(piece)],
            cross_in.at[rows(piece)],
            c_send.at[piece],
            c_recv.at[piece],
            other,
        )

    def to_backward(piece):
        return remote(
            terms.at[2, rows(piece)], far_in.at[rows(piece)], x_send.at[piece], x_recv.at[piece], backward
        )

    def to_across(piece):
        return remote(
            terms.at[1, rows(piece)], near_in.at[rows(piece)], y_send.at[piece], y_recv.at[piece], across
        )

    swap = remote(terms.at[0], other_in, o_send, o_recv, other)

    def halo_start():
        fetches[0].wait()
        for piece in range(PIECES):
            to_other(piece).start()
        swap.start()
        for fetch in fetches[1:]:
            fetch.start()

    def over_tiles(piece, work):
        def tile(i, carry):
            work(pl.ds(pl.multiple_of(piece * PIECE + i * TILE, TILE), TILE))
            return carry

        lax.fori_loop(0, PIECE // TILE, tile, 0)

    def halo_first(pieces):
        for piece in pieces:
            to_other(piece).wait_recv()

            def add(here):
                cross = wide(cross_in, here)
                terms[2, here] = (wide(terms, 2, here) + jnp.where(near_first, 0.0, cross)).astype(
                    jnp.bfloat16
                )
                terms[1, here] = (wide(terms, 1, here) + jnp.where(near_first, cross, 0.0)).astype(
                    jnp.bfloat16
                )

            over_tiles(piece, add)
            to_backward(piece).start()

    def halo_second(pieces):
        for piece in pieces:
            to_backward(piece).wait_recv()

            def add(here):
                terms[1, here] = (wide(terms, 1, here) + wide(far_in, here)).astype(jnp.bfloat16)

            over_tiles(piece, add)
            to_across(piece).start()

    def halo_end(pieces):
        for piece in pieces:
            to_across(piece).wait_recv()

            def add(here):
                halo_out[here] = halo_out[here] + (wide(other_in, here) + wide(near_in, here))

            over_tiles(piece, add)

    def link_at(part, step):
        return ORDER[(FIRST_LINK[part] + step) % CLASSES]

    weights = (2, 1, 16, 4, 8, 32)
    places = (x_bits[0], y_bits[0], z_bits[0], x_bits[1], y_bits[1], z_bits[1])
    turns = [TILE * weight * (1 - 2 * bit) for weight, bit in zip(weights, places)]
    tile_rows = [TILE * sum(weight * bit for weight, bit in zip(weights, places))]
    for turn in turns:
        tile_rows = tile_rows + [row + turn for row in tile_rows]

    def tile_row(part, position):
        mask = 0
        for step in range(CLASSES):
            if position & (TILES >> (step + 1)):
                link = link_at(part, step)
                mask ^= (1 << link) | (1 << (link % 3))
        return pl.multiple_of(tile_rows[mask], TILE)

    def first_copy(part):
        start, size = PARTS[part]
        return remote(
            grads.at[1 - core, :, pl.ds(start, size)],
            first_in[part],
            send.at[part, 0],
            receive.at[part, 0],
            other,
        )

    def kept(step):
        return (TILES >> step) * TILE

    def pair_of(part, step):
        pair = (total[part], other_total[part])
        return pair if step % 2 else pair[::-1]

    def later_copy(part, step):
        count = kept(step)
        return remote(
            pair_of(part, step)[0].at[pl.ds(count, count)],
            later_in[part].at[pl.ds(count, count)],
            send.at[part, step],
            receive.at[part, step],
            partners[link_at(part, step - 1)],
        )

    def product(terms_of, width, column, half):
        summed = 0.0
        for left, right, begin in terms_of:
            summed = summed + jnp.dot(
                left[...], right[:, pl.ds(begin, width)], preferred_element_type=jnp.float32
            )
        grads[half, :, pl.ds(column, width)] = summed.astype(jnp.bfloat16)

    own_t = entries_t.at[:, pl.ds(0, BLOCK)]
    chosen_t = entries_t.at[:, pl.ds(BLOCK, 2 * BLOCK)]

    def products_of(group):
        column = 640 + 768 * group
        for half in range(2):
            begin = 512 * group + 256 * half
            product([(own_t, dq_own, begin)], 256, column, half)
            product([(own_t, dk_own, begin), (chosen_t, dk, begin)], 256, column + 256, half)
            product([(own_t, dv_own, begin), (chosen_t, dv, begin)], 256, column + 512, half)

    weights = (
        grads.at[0, :, pl.ds(0, WIDTH)],
        grads.at[0, :, pl.ds(WIDTH, WIDTH)],
        grads.at[1, :, pl.ds(0, WIDTH)],
    )
    weight_fetches = [
        pltpu.make_async_copy(
            weights_hbm.at[:, pl.ds(i * WIDTH, WIDTH)], weights[i], fetched.at[len(fetches) + i]
        )
        for i in range(3)
    ]

    def own_part(quarter):
        here = pl.ds(quarter * 256, 256)
        summed = 0.0
        for grad, weight in zip((dq_own, dk_own, dv_own), weights):
            summed = summed + lax.dot_general(
                grad[...], weight[here], NT, preferred_element_type=jnp.float32
            )
        halo_out[:, here] = summed

    def own_pair(pair, carry):
        here = pl.ds(pl.multiple_of(pair * 2 * HEAD_DIM, 2 * HEAD_DIM), 2 * HEAD_DIM)
        queries, grad_keys, grad_values = back_of_pair(
            q[:, here],
            k[:, here],
            v[:, here],
            context[:, here],
            grad_context[:, here],
            [stats[pair, head : head + 1] for head in range(2)],
        )
        dq_own[:, here] = (queries + dq[:, here]).astype(jnp.bfloat16)
        dk_own[:, here] = grad_keys
        dv_own[:, here] = grad_values
        return carry

    def merge_first(part):
        start, size = PARTS[part]
        first_copy(part).wait_recv()

        def merge(positions):
            for position in positions:
                source = pl.ds(tile_row(part, position), TILE)
                total[part][pl.ds(position * TILE, TILE)] = (
                    grads[core, source, pl.ds(start, size)] + first_in[part][source]
                )

        merge(range(TILES // 2, TILES))
        later_copy(part, 1).start()
        merge(range(TILES // 2))

    def merge_later(part, step):
        start, size = PARTS[part]
        count = kept(step)
        held, made = pair_of(part, step)
        later_copy(part, step).wait_recv()
        if step < CLASSES:
            half = count // 2
            for begin in (half, 0):
                made[pl.ds(begin, half)] = (
                    held[pl.ds(begin, half)] + later_in[part][pl.ds(count + begin, half)]
                )
                if begin == half:
                    later_copy(part, step + 1).start()
        else:
            final = wide(held, pl.ds(0, TILE)) + wide(later_in[part], pl.ds(TILE, TILE))
            last[:, :, pl.ds(start, size)] = final.reshape(2, 8, size)

    halo_start()
    fetches[1].wait()
    fetches[2].wait()
    for half in range(2):
        for part in range(2):
            product([(narrow_t, hidden, 512 * half + 256 * part)], 256, 256 * part, half)
    first_copy(0).start()
    halo_first(range(PIECES))
    fetches[3].wait()
    narrow_t[...] = mid[...].T
    fetches[4].wait()
    product([(narrow_t, forecast, 0)], OUTV, 512, 0)
    grads[1, :, pl.ds(512, OUTV)] = jnp.zeros((WIDTH, OUTV), jnp.bfloat16)
    first_copy(1).start()
    fetches[5].wait()
    fetches[6].wait()
    merge_first(0)
    merge_first(1)
    for i in range(7, 13):
        fetches[i].wait()
    lax.fori_loop(0, 4, own_pair, 0)
    halo_second(range(0, 2))
    fetches[13].wait()
    fetches[14].wait()
    products_of(0)
    for part in (2, 3, 4):
        first_copy(part).start()
    merge_later(0, 1)
    merge_later(1, 1)
    halo_second(range(2, 4))
    for part in (2, 3, 4):
        merge_first(part)
    lax.fori_loop(4, 8, own_pair, 0)
    merge_later(0, 2)
    merge_later(1, 2)
    halo_second(range(4, 6))
    for part in (2, 3, 4):
        merge_later(part, 1)
    products_of(1)
    for part in range(5, 11):
        first_copy(part).start()
    merge_later(0, 3)
    merge_later(1, 3)
    for part in (2, 3, 4):
        merge_later(part, 2)
    halo_second(range(6, 8))
    for part in range(5, 11):
        merge_first(part)
    for part in range(parts):
        first_copy(part).wait_send()
    for fetch in weight_fetches:
        fetch.start()
    for step in range(1, CLASSES + 1):
        for part, ahead in ((0, 3), (1, 3), (2, 2), (3, 2), (4, 2)):
            if step + ahead <= CLASSES:
                merge_later(part, step + ahead)
        if step == 1:
            for fetch in weight_fetches:
                fetch.wait()
            for quarter in range(2):
                own_part(quarter)
        if step == 2:
            for quarter in range(2, 4):
                own_part(quarter)
            swap.wait_recv()
        if step >= 3:
            halo_end(range(2 * step - 6, 2 * step - 4))
        for part in range(5, 11):
            merge_later(part, step)
    finish = remote(last.at[1 - core], last_in, last_send, last_recv, other)
    finish.start()

    def deliver(half, source):
        def columns(begin, size):
            return pl.ds(pl.multiple_of(begin, 128), size)

        output_out[:, columns(512 * half, 512)] = source[:, pl.ds(0, 512)]
        for group in range(2):
            for kind in range(3):
                input_out[:, columns(1024 * kind + 512 * group + 256 * half, 256)] = source[
                    :, pl.ds(640 + 768 * group + 256 * kind, 256)
                ]

    deliver(core, last.at[core])
    finish.wait()
    deliver(1 - core, last_in)
    decoder_out[...] = jnp.where(core == 0, last[0, :, pl.ds(512, OUTV)], last_in[:, pl.ds(512, OUTV)])
    swap.wait_send()
    for piece in range(PIECES):
        to_other(piece).wait_send()
        to_backward(piece).wait_send()
        to_across(piece).wait_send()
    for part in range(parts):
        for step in range(1, CLASSES + 1):
            later_copy(part, step).wait_send()


def tail(terms, entries_t, context_t, weights, *others):
    dma = pltpu.SemaphoreType.DMA
    parts = len(PARTS)
    rows = TILES * TILE
    operands = (terms, entries_t, context_t, weights) + others
    blocks = [pltpu.VMEM((rows, size), jnp.bfloat16) for _, size in PARTS]
    block = pltpu.VMEM((BLOCK, WIDTH), jnp.bfloat16)
    return pl.pallas_call(
        tail_kernel,
        out_shape=(
            jax.ShapeDtypeStruct((8, 3 * WIDTH), jnp.float32),
            jax.ShapeDtypeStruct((8, WIDTH), jnp.float32),
            jax.ShapeDtypeStruct((8, OUTV), jnp.float32),
            jax.ShapeDtypeStruct((BLOCK, WIDTH), jnp.float32),
        ),
        in_specs=[pl.BlockSpec(memory_space=pl.ANY)] * len(operands),
        out_specs=(pl.BlockSpec(memory_space=pltpu.VMEM),) * 4,
        scratch_shapes=blocks * 3
        + [pltpu.VMEM((rows // 2, size), jnp.bfloat16) for _, size in PARTS]
        + [
            pltpu.VMEM((2, 8, HALF), jnp.float32),
            pltpu.VMEM((8, HALF), jnp.float32),
            pltpu.VMEM((2, WIDTH, HALF), jnp.bfloat16),
            pltpu.VMEM(terms.shape, terms.dtype),
        ]
        + [pltpu.VMEM(operand.shape, operand.dtype) for operand in others]
        + [
            pltpu.VMEM((WIDTH, BAND * BLOCK), jnp.bfloat16),
            pltpu.VMEM((WIDTH, BLOCK), jnp.bfloat16),
        ]
        + [block] * 7
        + [dma((parts, CLASSES + 1)), dma((parts, CLASSES + 1)), dma, dma]
        + [dma((PIECES,))] * 6
        + [dma, dma, dma((len(operands) + 3,))],
        compiler_params=pltpu.CompilerParams(
            collective_id=1, has_side_effects=True, vmem_limit_bytes=TAIL_VMEM
        ),
        name="tail",
    )(*operands)


def attend_kernel(q_ref, k_ref, v_ref, mixed_ref, top_ref, total_ref, context_ref, stat_ref):
    sides, tops, totals = forward_of_pair(q_ref[...], k_ref[...], v_ref[...])
    whole = []
    for head in range(2):
        own_top = top_ref[0, head : head + 1]
        top = jnp.maximum(own_top, tops[head])
        own_share = jnp.exp(own_top - top)
        share = jnp.exp(tops[head] - top)
        total = own_share * total_ref[0, head : head + 1] + share * totals[head]
        own_mixed = mixed_ref[0, head * HEAD_DIM : (head + 1) * HEAD_DIM]
        whole.append((own_share * own_mixed + share * sides[head]) / total)
        stat_ref[0, head : head + 1] = top + jnp.log(total)
    context_ref[...] = jnp.concatenate(whole, axis=0).T.astype(jnp.bfloat16)


PAIR = 2 * HEAD_DIM


def column_block(rows):
    return pl.BlockSpec((rows, PAIR), lambda i: (0, i))


STAT_BLOCK = pl.BlockSpec((1, 2, BLOCK), lambda i: (i, 0, 0))


def attend(q, k, v, mixed, tops, totals):
    keys = k.shape[0]
    return pl.pallas_call(
        attend_kernel,
        grid=(HEADS // 2,),
        out_shape=(
            jax.ShapeDtypeStruct((BLOCK, WIDTH), jnp.bfloat16),
            jax.ShapeDtypeStruct((HEADS // 2, 2, BLOCK), jnp.float32),
        ),
        in_specs=[column_block(array.shape[0]) for array in (q, k, v)]
        + [pl.BlockSpec((1, PAIR, BLOCK), lambda i: (i, 0, 0)), STAT_BLOCK, STAT_BLOCK],
        out_specs=(column_block(BLOCK), STAT_BLOCK),
        compiler_params=pltpu.CompilerParams(vmem_limit_bytes=VMEM_LIMIT),
        cost_estimate=pl.CostEstimate(
            flops=4 * BLOCK * keys * WIDTH,
            bytes_accessed=2 * WIDTH * (2 * BLOCK + 2 * keys),
            transcendentals=BLOCK * keys * HEADS,
        ),
        name="attend",
    )(q, k, v, mixed, tops, totals)


def back_of_pair(queries, keys, values, context, grads, stats):
    queries = queries * jnp.bfloat16(0.125)
    keys_t = keys.T
    products = (grads.astype(jnp.float32) * context.astype(jnp.float32)).T
    sides = []
    grad_keys = jnp.zeros(keys.shape, jnp.float32)
    grad_values = jnp.zeros(keys.shape, jnp.float32)
    for head in range(2):
        mask = head_mask(queries.shape, head)
        picked = jnp.where(mask, queries, jnp.bfloat16(0))
        grad_here = jnp.where(mask, grads, jnp.bfloat16(0))
        inner = jnp.sum(products[head * HEAD_DIM : (head + 1) * HEAD_DIM], axis=0, keepdims=True)
        scores = lax.dot_general(keys, picked, NT, preferred_element_type=jnp.float32)
        probs = jnp.exp(scores - stats[head])
        grad_probs = lax.dot_general(values, grad_here, NT, preferred_element_type=jnp.float32)
        grad_scores = (probs * (grad_probs - inner)).astype(jnp.bfloat16)
        grad_values += jnp.dot(
            probs.astype(jnp.bfloat16), grad_here, preferred_element_type=jnp.float32
        )
        grad_keys += jnp.dot(grad_scores, picked, preferred_element_type=jnp.float32)
        sides.append(
            jnp.dot(
                keys_t[head * HEAD_DIM : (head + 1) * HEAD_DIM],
                grad_scores,
                preferred_element_type=jnp.float32,
            )
        )
    grad_queries = (jnp.concatenate(sides, axis=0) * 0.125).T
    return grad_queries, grad_keys.astype(jnp.bfloat16), grad_values.astype(jnp.bfloat16)


def attend_back_kernel(q_ref, k_ref, v_ref, context_ref, grad_ref, stat_ref, dq_ref, dk_ref, dv_ref):
    dq_ref[...], dk_ref[...], dv_ref[...] = back_of_pair(
        q_ref[...],
        k_ref[...],
        v_ref[...],
        context_ref[...],
        grad_ref[...],
        [stat_ref[0, head : head + 1] for head in range(2)],
    )


def attend_back(q, k, v, context, grad_context, stats):
    rows, keys = q.shape[0], k.shape[0]
    return pl.pallas_call(
        attend_back_kernel,
        grid=(HEADS // 2,),
        out_shape=(
            jax.ShapeDtypeStruct((rows, WIDTH), jnp.float32),
            jax.ShapeDtypeStruct((keys, WIDTH), jnp.bfloat16),
            jax.ShapeDtypeStruct((keys, WIDTH), jnp.bfloat16),
        ),
        in_specs=[column_block(array.shape[0]) for array in (q, k, v, context, grad_context)]
        + [STAT_BLOCK],
        out_specs=(column_block(rows), column_block(keys), column_block(keys)),
        compiler_params=pltpu.CompilerParams(vmem_limit_bytes=VMEM_LIMIT),
        cost_estimate=pl.CostEstimate(
            flops=10 * rows * keys * WIDTH,
            bytes_accessed=2 * WIDTH * (4 * rows + 4 * keys),
            transcendentals=rows * keys * HEADS,
        ),
        name="attend_back",
    )(q, k, v, context, grad_context, stats)


def chosen_kernel(slots, dk, dv, weights_k, weights_v, terms):
    found = []
    for block in range(2):
        here = pl.ds(block * BLOCK, BLOCK)
        found.append(
            (
                lax.dot_general(dk[here], weights_k[...], NT, preferred_element_type=jnp.float32)
                + lax.dot_general(dv[here], weights_v[...], NT, preferred_element_type=jnp.float32)
            ).astype(jnp.bfloat16)
        )
    for slot in range(4):
        terms[slot] = jnp.zeros(terms.shape[1:], jnp.bfloat16)
    for block in range(2):
        terms[slots[block]] = found[block]


def chosen_terms(slots, dk, dv, weights):
    rows, columns = dk.shape[0], 256
    whole = pl.BlockSpec((rows, WIDTH), lambda i: (0, 0))
    return pl.pallas_call(
        chosen_kernel,
        grid=(WIDTH // columns,),
        out_shape=jax.ShapeDtypeStruct((4, BLOCK, WIDTH), jnp.bfloat16),
        in_specs=[
            pl.BlockSpec(memory_space=pltpu.SMEM),
            whole,
            whole,
            pl.BlockSpec((columns, WIDTH), lambda i: (i, 1)),
            pl.BlockSpec((columns, WIDTH), lambda i: (i, 2)),
        ],
        out_specs=pl.BlockSpec((4, BLOCK, columns), lambda i: (0, 0, i)),
        compiler_params=pltpu.CompilerParams(vmem_limit_bytes=VMEM_LIMIT),
        name="chosen_terms",
    )(slots, dk, dv, weights, weights)


def dot(left, right):
    return jnp.dot(left, right, preferred_element_type=jnp.float32)


def per_device(
    grid_point_features,
    projection_weights_qkv,
    merging_projection,
    readout_weights_table,
    observed,
    cell_surface_share,
    band_offsets,
    latitude_order,
):
    own_rows = grid_point_features[0]
    at = place()
    block = lax.axis_index("mp")
    near, far = jnp.int32(1), jnp.int32(2)
    above = jnp.where(at["y_lo"] == 0, near, far)
    below = jnp.where(at["y_lo"] == 0, far, near)
    minus = jnp.where(at["core"] == 0, 3, 0)
    plus = jnp.where(at["core"] == 0, 0, 3)
    offsets = lax.dynamic_slice(band_offsets, (block, 1), (1, 2))[0]
    slots = jnp.where(
        offsets == -2, below, jnp.where(offsets == -1, minus, jnp.where(offsets == 1, plus, above))
    ).astype(jnp.int32)

    q, k_own, v_own, k, v, entries, mixed, tops, totals = entry(
        slots, own_rows, projection_weights_qkv
    )
    context, stats = attend(q, k, v, mixed, tops, totals)

    hidden = (own_rows.astype(jnp.float32) + dot(context, merging_projection)).astype(jnp.bfloat16)
    normed_mid = layer_norm(hidden.astype(jnp.float32)).astype(jnp.bfloat16)
    predictions = dot(normed_mid, readout_weights_table)
    target = observed[latitude_order[0]]
    grad_forecast, entries_t, context_t = crps_grad(
        predictions, target, cell_surface_share[:, None], entries, context
    )

    grad_mid = dot(grad_forecast, readout_weights_table.T)
    grad_hidden = jax.vjp(layer_norm, hidden.astype(jnp.float32))[1](grad_mid)[0]
    hidden_half = grad_hidden.astype(jnp.bfloat16)
    grad_context = dot(hidden_half, merging_projection.T).astype(jnp.bfloat16)
    dq, dk, dv = attend_back(q, k, v, context, grad_context, stats)

    terms = chosen_terms(slots, dk, dv, projection_weights_qkv)
    grad_input, grad_output, grad_decoder, grad_normed = tail(
        terms,
        entries_t,
        context_t,
        projection_weights_qkv,
        context,
        hidden_half,
        normed_mid,
        grad_forecast,
        q,
        k_own,
        v_own,
        grad_context,
        stats,
        dq,
        dk,
        dv,
    )
    feature_derivative = (
        grad_hidden + jax.vjp(layer_norm, own_rows.astype(jnp.float32))[1](grad_normed)[0]
    )

    return (
        predictions[None],
        feature_derivative[None],
        grad_input,
        grad_output,
        grad_decoder,
    )


def solution(mesh):
    placed = (P("member", "mp", None), P(), P(), P(), P("mp", None), P("mp"), P(), P("mp", None))
    return jax.shard_map(
        per_device,
        mesh=mesh,
        in_specs=placed,
        out_specs=(
            P("member", "mp", None),
            P("member", "mp", None),
            P(("member", "mp"), None),
            P(("member", "mp"), None),
            P(("member", "mp"), None),
        ),
        check_vma=False,
    )
```

```python
import functools

import jax
import jax.numpy as jnp
from jax import lax
from jax.experimental import pallas as pl
from jax.experimental.pallas import tpu as pltpu
from jax.sharding import PartitionSpec as P

HEADS = 16
HEAD_DIM = 64
BLOCK = 512
WIDTH = 1024
OUTV = 128
BAND = 3

norm_epsilon = 1e-05
smooth_square = 0.0625

MESH = pl.DeviceIdType.MESH
VMEM_LIMIT = 56 * 1024 * 1024

PIECE = 64
PIECES = BLOCK // PIECE

HALF = 2176
PARTS = ((0, 384), (384, 256), (640, 256), (896, 256), (1152, 256)) + tuple(
    (1408 + 128 * i, 128) for i in range(6)
)
TILE = 16
TILES = 64
CLASSES = 6
ORDER = (1, 3, 2, 4, 0, 5)
FIRST_LINK = (2, 5, 1, 3, 4, 0, 1, 2, 3, 4, 5)
TAIL_VMEM = 60 * 1024 * 1024


def layer_norm(values):
    average = jnp.mean(values, axis=-1, keepdims=True)
    centred = values - average
    spread = jnp.mean(centred * centred, axis=-1, keepdims=True)
    return centred * lax.rsqrt(spread + norm_epsilon)


def softened_derivative(difference):
    return difference * lax.rsqrt(difference * difference + smooth_square)


NT = (((1,), (1,)), ((), ()))


def head_mask(shape, head):
    lane = lax.broadcasted_iota(jnp.int32, shape, 1)
    return (lane // HEAD_DIM) == head


def forward_of_pair(queries, keys, values):
    queries = queries * jnp.bfloat16(0.125)
    values_t = values.T
    sides, tops, totals = [], [], []
    for head in range(2):
        picked = jnp.where(head_mask(queries.shape, head), queries, jnp.bfloat16(0))
        scores = lax.dot_general(keys, picked, NT, preferred_element_type=jnp.float32)
        top = jnp.max(scores, axis=0, keepdims=True)
        powers = jnp.exp(scores - top)
        tops.append(top)
        totals.append(jnp.sum(powers, axis=0, keepdims=True))
        sides.append(
            jnp.dot(
                values_t[head * HEAD_DIM : (head + 1) * HEAD_DIM],
                powers.astype(jnp.bfloat16),
                preferred_element_type=jnp.float32,
            )
        )
    return sides, tops, totals


def place():
    member = lax.axis_index("member")
    mp = lax.axis_index("mp")
    return {
        "z": member // 2,
        "y_hi": member % 2,
        "x": mp // 4,
        "y_lo": (mp // 2) % 2,
        "core": mp % 2,
    }


def device(at):
    return (at["z"] * 2 + at["y_hi"], at["x"] * 4 + at["y_lo"] * 2 + at["core"])


def moved(at, **changes):
    return device({**at, **changes})


def greet(partners):
    barrier = pltpu.get_barrier_semaphore()
    for partner in partners:
        pl.semaphore_signal(barrier, inc=1, device_id=partner, device_id_type=MESH)
    pl.semaphore_wait(barrier, len(partners))


def remote(source, target, send, receive, partner):
    return pltpu.make_async_remote_copy(
        src_ref=source,
        dst_ref=target,
        send_sem=send,
        recv_sem=receive,
        device_id=partner,
        device_id_type=MESH,
    )


def entry_kernel(
    slots,
    raw,
    weights_hbm,
    q_hbm,
    k_own_hbm,
    v_own_hbm,
    k_hbm,
    v_hbm,
    entries_hbm,
    mixed_hbm,
    tops,
    totals,
    q,
    k_own,
    v_own,
    k,
    v,
    entries,
    mixed,
    weights,
    held,
    fetched,
    stored,
    y_send,
    y_recv,
    x_send,
    x_recv,
    c_send,
    c_recv,
    o_send,
    o_recv,
):
    at = place()
    other = moved(at, core=1 - at["core"])
    across = moved(at, y_lo=1 - at["y_lo"])
    forward = moved(at, x=(at["x"] + 1 + 2 * at["y_lo"]) % 4)
    backward = moved(at, x=(at["x"] + 3 - 2 * at["y_lo"]) % 4)
    fetch = pltpu.make_async_copy(weights_hbm, weights, fetched)
    fetch.start()
    greet((other, across, forward, backward))
    near_first = (at["core"] + at["y_lo"]) % 2 == 0
    own = entries.at[pl.ds(0, BLOCK)]

    def store(source, target, place_of):
        return pltpu.make_async_copy(source, target, stored.at[place_of])

    early = [
        store(q, q_hbm, 0),
        store(k_own, k_own_hbm, 1),
        store(v_own, v_own_hbm, 2),
        store(own, entries_hbm.at[pl.ds(0, BLOCK)], 3),
        store(mixed, mixed_hbm, 4),
    ]
    late = [
        [
            store(source.at[pl.ds(begin, BLOCK)], target.at[pl.ds(begin, BLOCK)], 5 + 3 * i + j)
            for j, (source, target, begin) in enumerate(
                (
                    (k, k_hbm, i * BLOCK),
                    (v, v_hbm, i * BLOCK),
                    (entries, entries_hbm, (i + 1) * BLOCK),
                )
            )
        ]
        for i in range(BAND - 1)
    ]

    def rows(piece):
        return pl.ds(pl.multiple_of(piece * PIECE, PIECE), PIECE)

    def to_across(piece):
        return remote(
            own.at[rows(piece)], held.at[1, rows(piece)], y_send.at[piece], y_recv.at[piece], across
        )

    def to_forward(piece):
        return remote(
            held.at[1, rows(piece)],
            held.at[2, rows(piece)],
            x_send.at[piece],
            x_recv.at[piece],
            forward,
        )

    def to_other(slot, piece):
        return remote(
            held.at[slot, rows(piece)],
            held.at[3, rows(piece)],
            c_send.at[piece],
            c_recv.at[piece],
            other,
        )

    def pass_on(piece):
        to_across(piece).wait_recv()
        to_forward(piece).start()

        @pl.when(near_first)
        def _():
            to_other(1, piece).start()

    def project(target, here, source, column):
        def tile(i, carry):
            width = 256
            begin = pl.multiple_of(i * width, width)
            target[here, pl.ds(begin, width)] = jnp.dot(
                source,
                weights[:, pl.ds(pl.multiple_of(column + begin, width), width)],
                preferred_element_type=jnp.float32,
            ).astype(jnp.bfloat16)
            return carry

        lax.fori_loop(0, WIDTH // 256, tile, 0)

    def own_pair(pair, carry):
        here = pl.ds(pl.multiple_of(pair * 2 * HEAD_DIM, 2 * HEAD_DIM), 2 * HEAD_DIM)
        sides, top, total = forward_of_pair(q[:, here], k_own[:, here], v_own[:, here])
        for head in range(2):
            mixed[pair, pl.ds(head * HEAD_DIM, HEAD_DIM)] = sides[head]
            tops[pair, pl.ds(head, 1)] = top[head]
            totals[pair, pl.ds(head, 1)] = total[head]
        pass_on(pair)
        return carry

    def normalise(piece, carry):
        own[rows(piece)] = layer_norm(raw[rows(piece)].astype(jnp.float32)).astype(jnp.bfloat16)
        to_across(piece).start()
        return carry

    lax.fori_loop(0, PIECES, normalise, 0)
    swap = remote(own, held.at[0], o_send, o_recv, other)
    swap.start()
    early[3].start()
    everything = pl.ds(0, BLOCK)
    fetch.wait()
    for i, target in enumerate((q, k_own, v_own)):
        project(target, everything, own[...], i * WIDTH)
        early[i].start()
    lax.fori_loop(0, PIECES, own_pair, 0)
    early[4].start()
    for piece in range(PIECES):
        to_forward(piece).wait_recv()

        @pl.when(jnp.logical_not(near_first))
        def _():
            to_other(2, piece).start()

    for piece in range(PIECES):
        to_other(1, piece).wait_recv()
    swap.wait_recv()
    for i in range(BAND - 1):
        here = pl.ds(i * BLOCK, BLOCK)
        chosen = held[slots[i]]
        entries[pl.ds((i + 1) * BLOCK, BLOCK)] = chosen
        late[i][2].start()
        project(k, here, chosen, WIDTH)
        late[i][0].start()
        project(v, here, chosen, 2 * WIDTH)
        late[i][1].start()
    for copy in early + late[0] + late[1]:
        copy.wait()
    swap.wait_send()
    for piece in range(PIECES):
        to_across(piece).wait_send()
        to_forward(piece).wait_send()
        to_other(1, piece).wait_send()


def entry(slots, own, weights):
    dma = pltpu.SemaphoreType.DMA
    pairs = HEADS // 2

    def half(rows):
        return jax.ShapeDtypeStruct((rows, WIDTH), jnp.bfloat16)

    stat = jax.ShapeDtypeStruct((pairs, 2, BLOCK), jnp.float32)
    return pl.pallas_call(
        entry_kernel,
        out_shape=(
            half(BLOCK),
            half(BLOCK),
            half(BLOCK),
            half(2 * BLOCK),
            half(2 * BLOCK),
            half(3 * BLOCK),
            jax.ShapeDtypeStruct((pairs, 2 * HEAD_DIM, BLOCK), jnp.float32),
            stat,
            stat,
        ),
        in_specs=[
            pl.BlockSpec(memory_space=pltpu.SMEM),
            pl.BlockSpec(memory_space=pltpu.VMEM),
            pl.BlockSpec(memory_space=pl.ANY),
        ],
        out_specs=(pl.BlockSpec(memory_space=pl.ANY),) * 7
        + (pl.BlockSpec(memory_space=pltpu.VMEM),) * 2,
        scratch_shapes=[pltpu.VMEM((count * BLOCK, WIDTH), jnp.bfloat16) for count in (1, 1, 1, 2, 2, 3)]
        + [
            pltpu.VMEM((pairs, 2 * HEAD_DIM, BLOCK), jnp.float32),
            pltpu.VMEM(weights.shape, jnp.bfloat16),
            pltpu.VMEM((4, BLOCK, WIDTH), jnp.bfloat16),
            dma,
            dma((11,)),
        ]
        + [dma((PIECES,))] * 6
        + [dma, dma],
        compiler_params=pltpu.CompilerParams(
            collective_id=0, has_side_effects=True, vmem_limit_bytes=VMEM_LIMIT
        ),
        name="entry",
    )(slots, own, weights)


def crps_kernel(
    predictions,
    target,
    share,
    entries,
    context,
    out,
    entries_t,
    context_t,
    halves,
    gathered,
    grads,
    send,
    receive,
    back_send,
    back_recv,
):
    member = lax.axis_index("member")
    mp = lax.axis_index("mp")
    count = 8
    size = BLOCK // count
    greet([((member + step) % count, mp) for step in range(1, count)])

    def slice_of(index):
        return pl.ds(pl.multiple_of(index * size, size), size)

    def outward(step):
        to = (member + step) % count
        return remote(
            halves.at[slice_of(to)], gathered.at[step], send.at[step], receive.at[step], (to, mp)
        )

    def homeward(step):
        to = (member + count - step) % count
        return remote(
            grads.at[step],
            out.at[slice_of(member)],
            back_send.at[step],
            back_recv.at[step],
            (to, mp),
        )

    halves[...] = predictions[...].astype(jnp.bfloat16)
    for step in range(1, count):
        outward(step).start()
    own = slice_of(member)
    truth = target[own]
    weight = share[own]
    gathered[0] = halves[own]
    for block in range(2):
        here = pl.ds(block * BLOCK, BLOCK)
        entries_t[:, here] = entries[here].T
    for step in range(1, count):
        outward(step).wait_recv()
    each = [gathered[step].astype(jnp.float32) for step in range(count)]
    spread = [0.0] * count
    for one in range(count):
        for two in range(one + 1, count):
            slope = softened_derivative(each[one] - each[two])
            spread[one] = spread[one] + slope
            spread[two] = spread[two] - slope
    for step in range(count):
        single = softened_derivative(each[step] - truth) / count
        paired = spread[step] / (count * (count - 1))
        grads[step] = (weight * (single - paired)).astype(jnp.bfloat16)
        if step:
            homeward(step).start()
    out[own] = grads[0]
    entries_t[:, pl.ds(2 * BLOCK, BLOCK)] = entries[pl.ds(2 * BLOCK, BLOCK)].T
    context_t[...] = context[...].T
    for step in range(1, count):
        homeward(step).wait_recv()
    for step in range(1, count):
        outward(step).wait_send()
        homeward(step).wait_send()


def crps_grad(predictions, target, share, entries, context):
    dma = pltpu.SemaphoreType.DMA
    size = BLOCK // 8
    return pl.pallas_call(
        crps_kernel,
        out_shape=(
            jax.ShapeDtypeStruct(predictions.shape, jnp.bfloat16),
            jax.ShapeDtypeStruct(entries.shape[::-1], jnp.bfloat16),
            jax.ShapeDtypeStruct(context.shape[::-1], jnp.bfloat16),
        ),
        in_specs=[pl.BlockSpec(memory_space=pltpu.VMEM)] * 5,
        out_specs=(pl.BlockSpec(memory_space=pltpu.VMEM),) * 3,
        scratch_shapes=[
            pltpu.VMEM((BLOCK, OUTV), jnp.bfloat16),
            pltpu.VMEM((8, size, OUTV), jnp.bfloat16),
            pltpu.VMEM((8, size, OUTV), jnp.bfloat16),
        ]
        + [dma((8,))] * 4,
        compiler_params=pltpu.CompilerParams(
            collective_id=2, has_side_effects=True, vmem_limit_bytes=VMEM_LIMIT
        ),
        name="crps_grad",
    )(predictions, target, share, entries, context)


def flip(bit, value):
    return (bit + value) % 2


def tail_kernel(
    terms_hbm,
    entries_t_hbm,
    context_t_hbm,
    weights_hbm,
    context_hbm,
    hidden_hbm,
    mid_hbm,
    forecast_hbm,
    q_hbm,
    k_hbm,
    v_hbm,
    grad_context_hbm,
    stats_hbm,
    dq_hbm,
    dk_hbm,
    dv_hbm,
    input_out,
    output_out,
    decoder_out,
    halo_out,
    *scratch,
):
    parts = len(PARTS)
    first_in = scratch[:parts]
    later_in = scratch[parts : 2 * parts]
    total = scratch[2 * parts : 3 * parts]
    other_total = scratch[3 * parts : 4 * parts]
    (
        last,
        last_in,
        grads,
        terms,
        context,
        hidden,
        mid,
        forecast,
        q,
        k,
        v,
        grad_context,
        stats,
        dq,
        dk,
        dv,
        entries_t,
        narrow_t,
        dq_own,
        dk_own,
        dv_own,
        cross_in,
        far_in,
        near_in,
        other_in,
        send,
        receive,
        last_send,
        last_recv,
        y_send,
        y_recv,
        x_send,
        x_recv,
        c_send,
        c_recv,
        o_send,
        o_recv,
        fetched,
    ) = scratch[4 * parts :]
    at = place()
    core = at["core"]
    x_bits = (at["x"] % 2, at["x"] // 2)
    z_bits = (at["z"] % 2, at["z"] // 2)
    y_bits = (at["y_lo"], at["y_hi"])
    other = moved(at, core=1 - core)

    fetches = [
        pltpu.make_async_copy(source, target, fetched.at[i])
        for i, (source, target) in enumerate(
            (
                (terms_hbm, terms),
                (context_t_hbm, narrow_t),
                (hidden_hbm, hidden),
                (mid_hbm, mid),
                (forecast_hbm, forecast),
                (entries_t_hbm, entries_t),
                (context_hbm, context),
                (q_hbm, q),
                (k_hbm, k),
                (v_hbm, v),
                (grad_context_hbm, grad_context),
                (stats_hbm, stats),
                (dq_hbm, dq),
                (dk_hbm, dk),
                (dv_hbm, dv),
            )
        )
    ]
    fetches[0].start()

    def partner_of(link):
        low, high = 1, link // 3
        if link % 3 == 0:
            return moved(at, x=flip(x_bits[0], low) + 2 * flip(x_bits[1], high))
        if link % 3 == 1:
            return moved(at, y_lo=flip(y_bits[0], low), y_hi=flip(y_bits[1], high))
        return moved(at, z=flip(z_bits[0], low) + 2 * flip(z_bits[1], high))

    partners = [partner_of(link) for link in range(CLASSES)]
    greet([other] + partners)

    across = partners[1]
    backward = moved(at, x=(at["x"] + 3 - 2 * at["y_lo"]) % 4)
    near_first = (at["core"] + at["y_lo"]) % 2 == 0

    def rows(piece):
        return pl.ds(piece * PIECE, PIECE)

    def wide(ref, *index):
        return ref[index].astype(jnp.float32)

    def to_other(piece):
        return remote(
            terms.at[3, rows(piece)],
            cross_in.at[rows(piece)],
            c_send.at[piece],
            c_recv.at[piece],
            other,
        )

    def to_backward(piece):
        return remote(
            terms.at[2, rows(piece)], far_in.at[rows(piece)], x_send.at[piece], x_recv.at[piece], backward
        )

    def to_across(piece):
        return remote(
            terms.at[1, rows(piece)], near_in.at[rows(piece)], y_send.at[piece], y_recv.at[piece], across
        )

    swap = remote(terms.at[0], other_in, o_send, o_recv, other)

    def halo_start():
        fetches[0].wait()
        for piece in range(PIECES):
            to_other(piece).start()
        swap.start()
        for fetch in fetches[1:]:
            fetch.start()

    def over_tiles(piece, work):
        def tile(i, carry):
            work(pl.ds(pl.multiple_of(piece * PIECE + i * TILE, TILE), TILE))
            return carry

        lax.fori_loop(0, PIECE // TILE, tile, 0)

    def halo_first(pieces):
        for piece in pieces:
            to_other(piece).wait_recv()

            def add(here):
                cross = wide(cross_in, here)
                terms[2, here] = (wide(terms, 2, here) + jnp.where(near_first, 0.0, cross)).astype(
                    jnp.bfloat16
                )
                terms[1, here] = (wide(terms, 1, here) + jnp.where(near_first, cross, 0.0)).astype(
                    jnp.bfloat16
                )

            over_tiles(piece, add)
            to_backward(piece).start()

    def halo_second(pieces):
        for piece in pieces:
            to_backward(piece).wait_recv()

            def add(here):
                terms[1, here] = (wide(terms, 1, here) + wide(far_in, here)).astype(jnp.bfloat16)

            over_tiles(piece, add)
            to_across(piece).start()

    def halo_end(pieces):
        for piece in pieces:
            to_across(piece).wait_recv()

            def add(here):
                halo_out[here] = halo_out[here] + (wide(other_in, here) + wide(near_in, here))

            over_tiles(piece, add)

    def link_at(part, step):
        return ORDER[(FIRST_LINK[part] + step) % CLASSES]

    weights = (2, 1, 16, 4, 8, 32)
    places = (x_bits[0], y_bits[0], z_bits[0], x_bits[1], y_bits[1], z_bits[1])
    turns = [TILE * weight * (1 - 2 * bit) for weight, bit in zip(weights, places)]
    tile_rows = [TILE * sum(weight * bit for weight, bit in zip(weights, places))]
    for turn in turns:
        tile_rows = tile_rows + [row + turn for row in tile_rows]

    def tile_row(part, position):
        mask = 0
        for step in range(CLASSES):
            if position & (TILES >> (step + 1)):
                link = link_at(part, step)
                mask ^= (1 << link) | (1 << (link % 3))
        return pl.multiple_of(tile_rows[mask], TILE)

    def first_copy(part):
        start, size = PARTS[part]
        return remote(
            grads.at[1 - core, :, pl.ds(start, size)],
            first_in[part],
            send.at[part, 0],
            receive.at[part, 0],
            other,
        )

    def kept(step):
        return (TILES >> step) * TILE

    def pair_of(part, step):
        pair = (total[part], other_total[part])
        return pair if step % 2 else pair[::-1]

    def later_copy(part, step):
        count = kept(step)
        return remote(
            pair_of(part, step)[0].at[pl.ds(count, count)],
            later_in[part].at[pl.ds(count, count)],
            send.at[part, step],
            receive.at[part, step],
            partners[link_at(part, step - 1)],
        )

    def product(terms_of, width, column, half):
        summed = 0.0
        for left, right, begin in terms_of:
            summed = summed + jnp.dot(
                left[...], right[:, pl.ds(begin, width)], preferred_element_type=jnp.float32
            )
        grads[half, :, pl.ds(column, width)] = summed.astype(jnp.bfloat16)

    own_t = entries_t.at[:, pl.ds(0, BLOCK)]
    chosen_t = entries_t.at[:, pl.ds(BLOCK, 2 * BLOCK)]

    def products_of(group):
        column = 640 + 768 * group
        for half in range(2):
            begin = 512 * group + 256 * half
            product([(own_t, dq_own, begin)], 256, column, half)
            product([(own_t, dk_own, begin), (chosen_t, dk, begin)], 256, column + 256, half)
            product([(own_t, dv_own, begin), (chosen_t, dv, begin)], 256, column + 512, half)

    weights = (
        grads.at[0, :, pl.ds(0, WIDTH)],
        grads.at[0, :, pl.ds(WIDTH, WIDTH)],
        grads.at[1, :, pl.ds(0, WIDTH)],
    )
    weight_fetches = [
        pltpu.make_async_copy(
            weights_hbm.at[:, pl.ds(i * WIDTH, WIDTH)], weights[i], fetched.at[len(fetches) + i]
        )
        for i in range(3)
    ]

    def own_part(quarter):
        here = pl.ds(quarter * 256, 256)
        summed = 0.0
        for grad, weight in zip((dq_own, dk_own, dv_own), weights):
            summed = summed + lax.dot_general(
                grad[...], weight[here], NT, preferred_element_type=jnp.float32
            )
        halo_out[:, here] = summed

    def own_pair(pair, carry):
        here = pl.ds(pl.multiple_of(pair * 2 * HEAD_DIM, 2 * HEAD_DIM), 2 * HEAD_DIM)
        queries, grad_keys, grad_values = back_of_pair(
            q[:, here],
            k[:, here],
            v[:, here],
            context[:, here],
            grad_context[:, here],
            [stats[pair, head : head + 1] for head in range(2)],
        )
        dq_own[:, here] = (queries + dq[:, here]).astype(jnp.bfloat16)
        dk_own[:, here] = grad_keys
        dv_own[:, here] = grad_values
        return carry

    def merge_first(part):
        start, size = PARTS[part]
        first_copy(part).wait_recv()

        def merge(positions):
            for position in positions:
                source = pl.ds(tile_row(part, position), TILE)
                total[part][pl.ds(position * TILE, TILE)] = (
                    grads[core, source, pl.ds(start, size)] + first_in[part][source]
                )

        merge(range(TILES // 2, TILES))
        later_copy(part, 1).start()
        merge(range(TILES // 2))

    def merge_later(part, step):
        start, size = PARTS[part]
        count = kept(step)
        held, made = pair_of(part, step)
        later_copy(part, step).wait_recv()
        if step < CLASSES:
            half = count // 2
            for begin in (half, 0):
                made[pl.ds(begin, half)] = (
                    held[pl.ds(begin, half)] + later_in[part][pl.ds(count + begin, half)]
                )
                if begin == half:
                    later_copy(part, step + 1).start()
        else:
            final = wide(held, pl.ds(0, TILE)) + wide(later_in[part], pl.ds(TILE, TILE))
            last[:, :, pl.ds(start, size)] = final.reshape(2, 8, size)

    halo_start()
    fetches[1].wait()
    fetches[2].wait()
    for half in range(2):
        for part in range(2):
            product([(narrow_t, hidden, 512 * half + 256 * part)], 256, 256 * part, half)
    first_copy(0).start()
    halo_first(range(PIECES))
    fetches[3].wait()
    narrow_t[...] = mid[...].T
    fetches[4].wait()
    product([(narrow_t, forecast, 0)], OUTV, 512, 0)
    grads[1, :, pl.ds(512, OUTV)] = jnp.zeros((WIDTH, OUTV), jnp.bfloat16)
    first_copy(1).start()
    fetches[5].wait()
    fetches[6].wait()
    merge_first(0)
    merge_first(1)
    for i in range(7, 13):
        fetches[i].wait()
    lax.fori_loop(0, 4, own_pair, 0)
    halo_second(range(0, 2))
    fetches[13].wait()
    fetches[14].wait()
    products_of(0)
    for part in (2, 3, 4):
        first_copy(part).start()
    halo_second(range(2, 4))
    lax.fori_loop(4, 6, own_pair, 0)
    for part in (2, 3, 4):
        merge_first(part)
    lax.fori_loop(6, 8, own_pair, 0)
    halo_second(range(4, 6))
    products_of(1)
    for part in range(5, 11):
        first_copy(part).start()
    merge_later(0, 1)
    merge_later(1, 1)
    for part in range(5, 11):
        merge_first(part)
    for part in range(parts):
        first_copy(part).wait_send()
    for fetch in weight_fetches:
        fetch.start()
    halo_second(range(6, 8))
    for part in (2, 3, 4):
        merge_later(part, 1)
    for fetch in weight_fetches:
        fetch.wait()
    for step in range(1, CLASSES + 1):
        for part, ahead in ((0, 1), (1, 1), (2, 1), (3, 1), (4, 1)):
            if step + ahead <= CLASSES:
                merge_later(part, step + ahead)
        if step <= 4:
            own_part(step - 1)
        if step == 4:
            swap.wait_recv()
        if step >= 5:
            halo_end(range(4 * step - 20, 4 * step - 16))
        for part in range(5, 11):
            merge_later(part, step)
    finish = remote(last.at[1 - core], last_in, last_send, last_recv, other)
    finish.start()

    def deliver(half, source):
        def columns(begin, size):
            return pl.ds(pl.multiple_of(begin, 128), size)

        output_out[:, columns(512 * half, 512)] = source[:, pl.ds(0, 512)]
        for group in range(2):
            for kind in range(3):
                input_out[:, columns(1024 * kind + 512 * group + 256 * half, 256)] = source[
                    :, pl.ds(640 + 768 * group + 256 * kind, 256)
                ]

    deliver(core, last.at[core])
    finish.wait()
    deliver(1 - core, last_in)
    decoder_out[...] = jnp.where(core == 0, last[0, :, pl.ds(512, OUTV)], last_in[:, pl.ds(512, OUTV)])
    swap.wait_send()
    for piece in range(PIECES):
        to_other(piece).wait_send()
        to_backward(piece).wait_send()
        to_across(piece).wait_send()
    for part in range(parts):
        for step in range(1, CLASSES + 1):
            later_copy(part, step).wait_send()


def tail(terms, entries_t, context_t, weights, *others):
    dma = pltpu.SemaphoreType.DMA
    parts = len(PARTS)
    rows = TILES * TILE
    operands = (terms, entries_t, context_t, weights) + others
    blocks = [pltpu.VMEM((rows, size), jnp.bfloat16) for _, size in PARTS]
    block = pltpu.VMEM((BLOCK, WIDTH), jnp.bfloat16)
    return pl.pallas_call(
        tail_kernel,
        out_shape=(
            jax.ShapeDtypeStruct((8, 3 * WIDTH), jnp.float32),
            jax.ShapeDtypeStruct((8, WIDTH), jnp.float32),
            jax.ShapeDtypeStruct((8, OUTV), jnp.float32),
            jax.ShapeDtypeStruct((BLOCK, WIDTH), jnp.float32),
        ),
        in_specs=[pl.BlockSpec(memory_space=pl.ANY)] * len(operands),
        out_specs=(pl.BlockSpec(memory_space=pltpu.VMEM),) * 4,
        scratch_shapes=blocks * 3
        + [pltpu.VMEM((rows // 2, size), jnp.bfloat16) for _, size in PARTS]
        + [
            pltpu.VMEM((2, 8, HALF), jnp.float32),
            pltpu.VMEM((8, HALF), jnp.float32),
            pltpu.VMEM((2, WIDTH, HALF), jnp.bfloat16),
            pltpu.VMEM(terms.shape, terms.dtype),
        ]
        + [pltpu.VMEM(operand.shape, operand.dtype) for operand in others]
        + [
            pltpu.VMEM((WIDTH, BAND * BLOCK), jnp.bfloat16),
            pltpu.VMEM((WIDTH, BLOCK), jnp.bfloat16),
        ]
        + [block] * 7
        + [dma((parts, CLASSES + 1)), dma((parts, CLASSES + 1)), dma, dma]
        + [dma((PIECES,))] * 6
        + [dma, dma, dma((len(operands) + 3,))],
        compiler_params=pltpu.CompilerParams(
            collective_id=1, has_side_effects=True, vmem_limit_bytes=TAIL_VMEM
        ),
        name="tail",
    )(*operands)


def attend_kernel(q_ref, k_ref, v_ref, mixed_ref, top_ref, total_ref, context_ref, stat_ref):
    sides, tops, totals = forward_of_pair(q_ref[...], k_ref[...], v_ref[...])
    whole = []
    for head in range(2):
        own_top = top_ref[0, head : head + 1]
        top = jnp.maximum(own_top, tops[head])
        own_share = jnp.exp(own_top - top)
        share = jnp.exp(tops[head] - top)
        total = own_share * total_ref[0, head : head + 1] + share * totals[head]
        own_mixed = mixed_ref[0, head * HEAD_DIM : (head + 1) * HEAD_DIM]
        whole.append((own_share * own_mixed + share * sides[head]) / total)
        stat_ref[0, head : head + 1] = top + jnp.log(total)
    context_ref[...] = jnp.concatenate(whole, axis=0).T.astype(jnp.bfloat16)


PAIR = 2 * HEAD_DIM


def column_block(rows):
    return pl.BlockSpec((rows, PAIR), lambda i: (0, i))


STAT_BLOCK = pl.BlockSpec((1, 2, BLOCK), lambda i: (i, 0, 0))


def attend(q, k, v, mixed, tops, totals):
    keys = k.shape[0]
    return pl.pallas_call(
        attend_kernel,
        grid=(HEADS // 2,),
        out_shape=(
            jax.ShapeDtypeStruct((BLOCK, WIDTH), jnp.bfloat16),
            jax.ShapeDtypeStruct((HEADS // 2, 2, BLOCK), jnp.float32),
        ),
        in_specs=[column_block(array.shape[0]) for array in (q, k, v)]
        + [pl.BlockSpec((1, PAIR, BLOCK), lambda i: (i, 0, 0)), STAT_BLOCK, STAT_BLOCK],
        out_specs=(column_block(BLOCK), STAT_BLOCK),
        compiler_params=pltpu.CompilerParams(vmem_limit_bytes=VMEM_LIMIT),
        cost_estimate=pl.CostEstimate(
            flops=4 * BLOCK * keys * WIDTH,
            bytes_accessed=2 * WIDTH * (2 * BLOCK + 2 * keys),
            transcendentals=BLOCK * keys * HEADS,
        ),
        name="attend",
    )(q, k, v, mixed, tops, totals)


def back_of_pair(queries, keys, values, context, grads, stats):
    queries = queries * jnp.bfloat16(0.125)
    keys_t = keys.T
    products = (grads.astype(jnp.float32) * context.astype(jnp.float32)).T
    sides = []
    grad_keys = jnp.zeros(keys.shape, jnp.float32)
    grad_values = jnp.zeros(keys.shape, jnp.float32)
    for head in range(2):
        mask = head_mask(queries.shape, head)
        picked = jnp.where(mask, queries, jnp.bfloat16(0))
        grad_here = jnp.where(mask, grads, jnp.bfloat16(0))
        inner = jnp.sum(products[head * HEAD_DIM : (head + 1) * HEAD_DIM], axis=0, keepdims=True)
        scores = lax.dot_general(keys, picked, NT, preferred_element_type=jnp.float32)
        probs = jnp.exp(scores - stats[head])
        grad_probs = lax.dot_general(values, grad_here, NT, preferred_element_type=jnp.float32)
        grad_scores = (probs * (grad_probs - inner)).astype(jnp.bfloat16)
        grad_values += jnp.dot(
            probs.astype(jnp.bfloat16), grad_here, preferred_element_type=jnp.float32
        )
        grad_keys += jnp.dot(grad_scores, picked, preferred_element_type=jnp.float32)
        sides.append(
            jnp.dot(
                keys_t[head * HEAD_DIM : (head + 1) * HEAD_DIM],
                grad_scores,
                preferred_element_type=jnp.float32,
            )
        )
    grad_queries = (jnp.concatenate(sides, axis=0) * 0.125).T
    return grad_queries, grad_keys.astype(jnp.bfloat16), grad_values.astype(jnp.bfloat16)


def attend_back_kernel(q_ref, k_ref, v_ref, context_ref, grad_ref, stat_ref, dq_ref, dk_ref, dv_ref):
    dq_ref[...], dk_ref[...], dv_ref[...] = back_of_pair(
        q_ref[...],
        k_ref[...],
        v_ref[...],
        context_ref[...],
        grad_ref[...],
        [stat_ref[0, head : head + 1] for head in range(2)],
    )


def attend_back(q, k, v, context, grad_context, stats):
    rows, keys = q.shape[0], k.shape[0]
    return pl.pallas_call(
        attend_back_kernel,
        grid=(HEADS // 2,),
        out_shape=(
            jax.ShapeDtypeStruct((rows, WIDTH), jnp.float32),
            jax.ShapeDtypeStruct((keys, WIDTH), jnp.bfloat16),
            jax.ShapeDtypeStruct((keys, WIDTH), jnp.bfloat16),
        ),
        in_specs=[column_block(array.shape[0]) for array in (q, k, v, context, grad_context)]
        + [STAT_BLOCK],
        out_specs=(column_block(rows), column_block(keys), column_block(keys)),
        compiler_params=pltpu.CompilerParams(vmem_limit_bytes=VMEM_LIMIT),
        cost_estimate=pl.CostEstimate(
            flops=10 * rows * keys * WIDTH,
            bytes_accessed=2 * WIDTH * (4 * rows + 4 * keys),
            transcendentals=rows * keys * HEADS,
        ),
        name="attend_back",
    )(q, k, v, context, grad_context, stats)


def chosen_kernel(slots, dk, dv, weights_k, weights_v, terms):
    found = []
    for block in range(2):
        here = pl.ds(block * BLOCK, BLOCK)
        found.append(
            (
                lax.dot_general(dk[here], weights_k[...], NT, preferred_element_type=jnp.float32)
                + lax.dot_general(dv[here], weights_v[...], NT, preferred_element_type=jnp.float32)
            ).astype(jnp.bfloat16)
        )
    for slot in range(4):
        terms[slot] = jnp.zeros(terms.shape[1:], jnp.bfloat16)
    for block in range(2):
        terms[slots[block]] = found[block]


def chosen_terms(slots, dk, dv, weights):
    rows, columns = dk.shape[0], 256
    whole = pl.BlockSpec((rows, WIDTH), lambda i: (0, 0))
    return pl.pallas_call(
        chosen_kernel,
        grid=(WIDTH // columns,),
        out_shape=jax.ShapeDtypeStruct((4, BLOCK, WIDTH), jnp.bfloat16),
        in_specs=[
            pl.BlockSpec(memory_space=pltpu.SMEM),
            whole,
            whole,
            pl.BlockSpec((columns, WIDTH), lambda i: (i, 1)),
            pl.BlockSpec((columns, WIDTH), lambda i: (i, 2)),
        ],
        out_specs=pl.BlockSpec((4, BLOCK, columns), lambda i: (0, 0, i)),
        compiler_params=pltpu.CompilerParams(vmem_limit_bytes=VMEM_LIMIT),
        name="chosen_terms",
    )(slots, dk, dv, weights, weights)


def dot(left, right):
    return jnp.dot(left, right, preferred_element_type=jnp.float32)


def per_device(
    grid_point_features,
    projection_weights_qkv,
    merging_projection,
    readout_weights_table,
    observed,
    cell_surface_share,
    band_offsets,
    latitude_order,
):
    own_rows = grid_point_features[0]
    at = place()
    block = lax.axis_index("mp")
    near, far = jnp.int32(1), jnp.int32(2)
    above = jnp.where(at["y_lo"] == 0, near, far)
    below = jnp.where(at["y_lo"] == 0, far, near)
    minus = jnp.where(at["core"] == 0, 3, 0)
    plus = jnp.where(at["core"] == 0, 0, 3)
    offsets = lax.dynamic_slice(band_offsets, (block, 1), (1, 2))[0]
    slots = jnp.where(
        offsets == -2, below, jnp.where(offsets == -1, minus, jnp.where(offsets == 1, plus, above))
    ).astype(jnp.int32)

    q, k_own, v_own, k, v, entries, mixed, tops, totals = entry(
        slots, own_rows, projection_weights_qkv
    )
    context, stats = attend(q, k, v, mixed, tops, totals)

    hidden = (own_rows.astype(jnp.float32) + dot(context, merging_projection)).astype(jnp.bfloat16)
    normed_mid = layer_norm(hidden.astype(jnp.float32)).astype(jnp.bfloat16)
    predictions = dot(normed_mid, readout_weights_table)
    target = observed[latitude_order[0]]
    grad_forecast, entries_t, context_t = crps_grad(
        predictions, target, cell_surface_share[:, None], entries, context
    )

    grad_mid = dot(grad_forecast, readout_weights_table.T)
    grad_hidden = jax.vjp(layer_norm, hidden.astype(jnp.float32))[1](grad_mid)[0]
    hidden_half = grad_hidden.astype(jnp.bfloat16)
    grad_context = dot(hidden_half, merging_projection.T).astype(jnp.bfloat16)
    dq, dk, dv = attend_back(q, k, v, context, grad_context, stats)

    terms = chosen_terms(slots, dk, dv, projection_weights_qkv)
    grad_input, grad_output, grad_decoder, grad_normed = tail(
        terms,
        entries_t,
        context_t,
        projection_weights_qkv,
        context,
        hidden_half,
        normed_mid,
        grad_forecast,
        q,
        k_own,
        v_own,
        grad_context,
        stats,
        dq,
        dk,
        dv,
    )
    feature_derivative = (
        grad_hidden + jax.vjp(layer_norm, own_rows.astype(jnp.float32))[1](grad_normed)[0]
    )

    return (
        predictions[None],
        feature_derivative[None],
        grad_input,
        grad_output,
        grad_decoder,
    )


def solution(mesh):
    placed = (P("member", "mp", None), P(), P(), P(), P("mp", None), P("mp"), P(), P("mp", None))
    return jax.shard_map(
        per_device,
        mesh=mesh,
        in_specs=placed,
        out_specs=(
            P("member", "mp", None),
            P("member", "mp", None),
            P(("member", "mp"), None),
            P(("member", "mp"), None),
            P(("member", "mp"), None),
        ),
        check_vma=False,
    )
```

```python
import functools

import jax
import jax.numpy as jnp
from jax import lax
from jax.experimental import pallas as pl
from jax.experimental.pallas import tpu as pltpu
from jax.sharding import PartitionSpec as P

HEADS = 16
HEAD_DIM = 64
BLOCK = 512
WIDTH = 1024
OUTV = 128
BAND = 3

norm_epsilon = 1e-05
smooth_square = 0.0625

MESH = pl.DeviceIdType.MESH
VMEM_LIMIT = 56 * 1024 * 1024

PIECE = 64
PIECES = BLOCK // PIECE

HALF = 2176
PARTS = ((0, 384), (384, 256), (640, 256), (896, 256), (1152, 256)) + tuple(
    (1408 + 128 * i, 128) for i in range(6)
)
TILE = 16
TILES = 64
CLASSES = 6
ORDER = (1, 3, 2, 4, 0, 5)
FIRST_LINK = (2, 5, 1, 3, 4, 0, 1, 2, 3, 4, 5)
TAIL_VMEM = 60 * 1024 * 1024


def layer_norm(values):
    average = jnp.mean(values, axis=-1, keepdims=True)
    centred = values - average
    spread = jnp.mean(centred * centred, axis=-1, keepdims=True)
    return centred * lax.rsqrt(spread + norm_epsilon)


def softened_derivative(difference):
    return difference * lax.rsqrt(difference * difference + smooth_square)


NT = (((1,), (1,)), ((), ()))


def head_mask(shape, head):
    lane = lax.broadcasted_iota(jnp.int32, shape, 1)
    return (lane // HEAD_DIM) == head


def forward_of_pair(queries, keys, values):
    queries = queries * jnp.bfloat16(0.125)
    values_t = values.T
    sides, tops, totals = [], [], []
    for head in range(2):
        picked = jnp.where(head_mask(queries.shape, head), queries, jnp.bfloat16(0))
        scores = lax.dot_general(keys, picked, NT, preferred_element_type=jnp.float32)
        top = jnp.max(scores, axis=0, keepdims=True)
        powers = jnp.exp(scores - top)
        tops.append(top)
        totals.append(jnp.sum(powers, axis=0, keepdims=True))
        sides.append(
            jnp.dot(
                values_t[head * HEAD_DIM : (head + 1) * HEAD_DIM],
                powers.astype(jnp.bfloat16),
                preferred_element_type=jnp.float32,
            )
        )
    return sides, tops, totals


def place():
    member = lax.axis_index("member")
    mp = lax.axis_index("mp")
    return {
        "z": member // 2,
        "y_hi": member % 2,
        "x": mp // 4,
        "y_lo": (mp // 2) % 2,
        "core": mp % 2,
    }


def device(at):
    return (at["z"] * 2 + at["y_hi"], at["x"] * 4 + at["y_lo"] * 2 + at["core"])


def moved(at, **changes):
    return device({**at, **changes})


def greet(partners):
    barrier = pltpu.get_barrier_semaphore()
    for partner in partners:
        pl.semaphore_signal(barrier, inc=1, device_id=partner, device_id_type=MESH)
    pl.semaphore_wait(barrier, len(partners))


def remote(source, target, send, receive, partner):
    return pltpu.make_async_remote_copy(
        src_ref=source,
        dst_ref=target,
        send_sem=send,
        recv_sem=receive,
        device_id=partner,
        device_id_type=MESH,
    )


def entry_kernel(
    slots,
    raw,
    weights_hbm,
    q_hbm,
    k_own_hbm,
    v_own_hbm,
    k_hbm,
    v_hbm,
    entries_hbm,
    mixed_hbm,
    tops,
    totals,
    q,
    k_own,
    v_own,
    k,
    v,
    entries,
    mixed,
    weights,
    held,
    fetched,
    stored,
    y_send,
    y_recv,
    x_send,
    x_recv,
    c_send,
    c_recv,
    o_send,
    o_recv,
):
    at = place()
    other = moved(at, core=1 - at["core"])
    across = moved(at, y_lo=1 - at["y_lo"])
    forward = moved(at, x=(at["x"] + 1 + 2 * at["y_lo"]) % 4)
    backward = moved(at, x=(at["x"] + 3 - 2 * at["y_lo"]) % 4)
    fetch = pltpu.make_async_copy(weights_hbm, weights, fetched)
    fetch.start()
    greet((other, across, forward, backward))
    near_first = (at["core"] + at["y_lo"]) % 2 == 0
    own = entries.at[pl.ds(0, BLOCK)]

    def store(source, target, place_of):
        return pltpu.make_async_copy(source, target, stored.at[place_of])

    early = [
        store(q, q_hbm, 0),
        store(k_own, k_own_hbm, 1),
        store(v_own, v_own_hbm, 2),
        store(own, entries_hbm.at[pl.ds(0, BLOCK)], 3),
        store(mixed, mixed_hbm, 4),
    ]
    late = [
        [
            store(source.at[pl.ds(begin, BLOCK)], target.at[pl.ds(begin, BLOCK)], 5 + 3 * i + j)
            for j, (source, target, begin) in enumerate(
                (
                    (k, k_hbm, i * BLOCK),
                    (v, v_hbm, i * BLOCK),
                    (entries, entries_hbm, (i + 1) * BLOCK),
                )
            )
        ]
        for i in range(BAND - 1)
    ]

    def rows(piece):
        return pl.ds(pl.multiple_of(piece * PIECE, PIECE), PIECE)

    def to_across(piece):
        return remote(
            own.at[rows(piece)], held.at[1, rows(piece)], y_send.at[piece], y_recv.at[piece], across
        )

    def to_forward(piece):
        return remote(
            held.at[1, rows(piece)],
            held.at[2, rows(piece)],
            x_send.at[piece],
            x_recv.at[piece],
            forward,
        )

    def to_other(slot, piece):
        return remote(
            held.at[slot, rows(piece)],
            held.at[3, rows(piece)],
            c_send.at[piece],
            c_recv.at[piece],
            other,
        )

    def pass_on(piece):
        to_across(piece).wait_recv()
        to_forward(piece).start()

        @pl.when(near_first)
        def _():
            to_other(1, piece).start()

    def project(target, here, source, column):
        def tile(i, carry):
            width = 256
            begin = pl.multiple_of(i * width, width)
            target[here, pl.ds(begin, width)] = jnp.dot(
                source,
                weights[:, pl.ds(pl.multiple_of(column + begin, width), width)],
                preferred_element_type=jnp.float32,
            ).astype(jnp.bfloat16)
            return carry

        lax.fori_loop(0, WIDTH // 256, tile, 0)

    def own_pair(pair, carry):
        here = pl.ds(pl.multiple_of(pair * 2 * HEAD_DIM, 2 * HEAD_DIM), 2 * HEAD_DIM)
        sides, top, total = forward_of_pair(q[:, here], k_own[:, here], v_own[:, here])
        for head in range(2):
            mixed[pair, pl.ds(head * HEAD_DIM, HEAD_DIM)] = sides[head]
            tops[pair, pl.ds(head, 1)] = top[head]
            totals[pair, pl.ds(head, 1)] = total[head]
        pass_on(pair)
        return carry

    def normalise(piece, carry):
        own[rows(piece)] = layer_norm(raw[rows(piece)].astype(jnp.float32)).astype(jnp.bfloat16)
        to_across(piece).start()
        return carry

    lax.fori_loop(0, PIECES, normalise, 0)
    swap = remote(own, held.at[0], o_send, o_recv, other)
    swap.start()
    early[3].start()
    everything = pl.ds(0, BLOCK)
    fetch.wait()
    for i, target in enumerate((q, k_own, v_own)):
        project(target, everything, own[...], i * WIDTH)
        early[i].start()
    lax.fori_loop(0, PIECES, own_pair, 0)
    early[4].start()
    for piece in range(PIECES):
        to_forward(piece).wait_recv()

        @pl.when(jnp.logical_not(near_first))
        def _():
            to_other(2, piece).start()

    for piece in range(PIECES):
        to_other(1, piece).wait_recv()
    swap.wait_recv()
    for i in range(BAND - 1):
        entries[pl.ds((i + 1) * BLOCK, BLOCK)] = held[slots[i]]
        late[i][2].start()
    chosen = entries[pl.ds(BLOCK, 2 * BLOCK)]
    for j, target in enumerate((k, v)):
        project(target, pl.ds(0, 2 * BLOCK), chosen, (j + 1) * WIDTH)
        late[0][j].start()
        late[1][j].start()
    for copy in early + late[0] + late[1]:
        copy.wait()
    swap.wait_send()
    for piece in range(PIECES):
        to_across(piece).wait_send()
        to_forward(piece).wait_send()
        to_other(1, piece).wait_send()


def entry(slots, own, weights):
    dma = pltpu.SemaphoreType.DMA
    pairs = HEADS // 2

    def half(rows):
        return jax.ShapeDtypeStruct((rows, WIDTH), jnp.bfloat16)

    stat = jax.ShapeDtypeStruct((pairs, 2, BLOCK), jnp.float32)
    return pl.pallas_call(
        entry_kernel,
        out_shape=(
            half(BLOCK),
            half(BLOCK),
            half(BLOCK),
            half(2 * BLOCK),
            half(2 * BLOCK),
            half(3 * BLOCK),
            jax.ShapeDtypeStruct((pairs, 2 * HEAD_DIM, BLOCK), jnp.float32),
            stat,
            stat,
        ),
        in_specs=[
            pl.BlockSpec(memory_space=pltpu.SMEM),
            pl.BlockSpec(memory_space=pltpu.VMEM),
            pl.BlockSpec(memory_space=pl.ANY),
        ],
        out_specs=(pl.BlockSpec(memory_space=pl.ANY),) * 7
        + (pl.BlockSpec(memory_space=pltpu.VMEM),) * 2,
        scratch_shapes=[pltpu.VMEM((count * BLOCK, WIDTH), jnp.bfloat16) for count in (1, 1, 1, 2, 2, 3)]
        + [
            pltpu.VMEM((pairs, 2 * HEAD_DIM, BLOCK), jnp.float32),
            pltpu.VMEM(weights.shape, jnp.bfloat16),
            pltpu.VMEM((4, BLOCK, WIDTH), jnp.bfloat16),
            dma,
            dma((11,)),
        ]
        + [dma((PIECES,))] * 6
        + [dma, dma],
        compiler_params=pltpu.CompilerParams(
            collective_id=0, has_side_effects=True, vmem_limit_bytes=VMEM_LIMIT
        ),
        name="entry",
    )(slots, own, weights)


def crps_kernel(
    predictions,
    target,
    share,
    entries,
    context,
    out,
    entries_t,
    context_t,
    halves,
    gathered,
    grads,
    send,
    receive,
    back_send,
    back_recv,
):
    member = lax.axis_index("member")
    mp = lax.axis_index("mp")
    count = 8
    size = BLOCK // count
    greet([((member + step) % count, mp) for step in range(1, count)])

    def slice_of(index):
        return pl.ds(pl.multiple_of(index * size, size), size)

    def outward(step):
        to = (member + step) % count
        return remote(
            halves.at[slice_of(to)], gathered.at[step], send.at[step], receive.at[step], (to, mp)
        )

    def homeward(step):
        to = (member + count - step) % count
        return remote(
            grads.at[step],
            out.at[slice_of(member)],
            back_send.at[step],
            back_recv.at[step],
            (to, mp),
        )

    halves[...] = predictions[...].astype(jnp.bfloat16)
    for step in range(1, count):
        outward(step).start()
    own = slice_of(member)
    truth = target[own]
    weight = share[own]
    gathered[0] = halves[own]
    for block in range(2):
        here = pl.ds(block * BLOCK, BLOCK)
        entries_t[:, here] = entries[here].T
    for step in range(1, count):
        outward(step).wait_recv()
    each = [gathered[step].astype(jnp.float32) for step in range(count)]
    spread = [0.0] * count
    for one in range(count):
        for two in range(one + 1, count):
            slope = softened_derivative(each[one] - each[two])
            spread[one] = spread[one] + slope
            spread[two] = spread[two] - slope
    for step in range(count):
        single = softened_derivative(each[step] - truth) / count
        paired = spread[step] / (count * (count - 1))
        grads[step] = (weight * (single - paired)).astype(jnp.bfloat16)
        if step:
            homeward(step).start()
    out[own] = grads[0]
    entries_t[:, pl.ds(2 * BLOCK, BLOCK)] = entries[pl.ds(2 * BLOCK, BLOCK)].T
    context_t[...] = context[...].T
    for step in range(1, count):
        homeward(step).wait_recv()
    for step in range(1, count):
        outward(step).wait_send()
        homeward(step).wait_send()


def crps_grad(predictions, target, share, entries, context):
    dma = pltpu.SemaphoreType.DMA
    size = BLOCK // 8
    return pl.pallas_call(
        crps_kernel,
        out_shape=(
            jax.ShapeDtypeStruct(predictions.shape, jnp.bfloat16),
            jax.ShapeDtypeStruct(entries.shape[::-1], jnp.bfloat16),
            jax.ShapeDtypeStruct(context.shape[::-1], jnp.bfloat16),
        ),
        in_specs=[pl.BlockSpec(memory_space=pltpu.VMEM)] * 5,
        out_specs=(pl.BlockSpec(memory_space=pltpu.VMEM),) * 3,
        scratch_shapes=[
            pltpu.VMEM((BLOCK, OUTV), jnp.bfloat16),
            pltpu.VMEM((8, size, OUTV), jnp.bfloat16),
            pltpu.VMEM((8, size, OUTV), jnp.bfloat16),
        ]
        + [dma((8,))] * 4,
        compiler_params=pltpu.CompilerParams(
            collective_id=2, has_side_effects=True, vmem_limit_bytes=VMEM_LIMIT
        ),
        name="crps_grad",
    )(predictions, target, share, entries, context)


def flip(bit, value):
    return (bit + value) % 2


def tail_kernel(
    terms_hbm,
    entries_t_hbm,
    context_t_hbm,
    weights_hbm,
    context_hbm,
    hidden_hbm,
    mid_hbm,
    forecast_hbm,
    q_hbm,
    k_hbm,
    v_hbm,
    grad_context_hbm,
    stats_hbm,
    dq_hbm,
    dk_hbm,
    dv_hbm,
    input_out,
    output_out,
    decoder_out,
    halo_out,
    *scratch,
):
    parts = len(PARTS)
    first_in = scratch[:parts]
    later_in = scratch[parts : 2 * parts]
    total = scratch[2 * parts : 3 * parts]
    other_total = scratch[3 * parts : 4 * parts]
    (
        last,
        last_in,
        grads,
        terms,
        context,
        hidden,
        mid,
        forecast,
        q,
        k,
        v,
        grad_context,
        stats,
        dq,
        dk,
        dv,
        entries_t,
        narrow_t,
        dq_own,
        dk_own,
        dv_own,
        cross_in,
        far_in,
        near_in,
        other_in,
        send,
        receive,
        last_send,
        last_recv,
        y_send,
        y_recv,
        x_send,
        x_recv,
        c_send,
        c_recv,
        o_send,
        o_recv,
        fetched,
    ) = scratch[4 * parts :]
    at = place()
    core = at["core"]
    x_bits = (at["x"] % 2, at["x"] // 2)
    z_bits = (at["z"] % 2, at["z"] // 2)
    y_bits = (at["y_lo"], at["y_hi"])
    other = moved(at, core=1 - core)

    fetches = [
        pltpu.make_async_copy(source, target, fetched.at[i])
        for i, (source, target) in enumerate(
            (
                (terms_hbm, terms),
                (context_t_hbm, narrow_t),
                (hidden_hbm, hidden),
                (mid_hbm, mid),
                (forecast_hbm, forecast),
                (entries_t_hbm, entries_t),
                (context_hbm, context),
                (q_hbm, q),
                (k_hbm, k),
                (v_hbm, v),
                (grad_context_hbm, grad_context),
                (stats_hbm, stats),
                (dq_hbm, dq),
                (dk_hbm, dk),
                (dv_hbm, dv),
            )
        )
    ]
    fetches[0].start()

    def partner_of(link):
        low, high = 1, link // 3
        if link % 3 == 0:
            return moved(at, x=flip(x_bits[0], low) + 2 * flip(x_bits[1], high))
        if link % 3 == 1:
            return moved(at, y_lo=flip(y_bits[0], low), y_hi=flip(y_bits[1], high))
        return moved(at, z=flip(z_bits[0], low) + 2 * flip(z_bits[1], high))

    partners = [partner_of(link) for link in range(CLASSES)]
    greet([other] + partners)

    across = partners[1]
    backward = moved(at, x=(at["x"] + 3 - 2 * at["y_lo"]) % 4)
    near_first = (at["core"] + at["y_lo"]) % 2 == 0

    def rows(piece):
        return pl.ds(piece * PIECE, PIECE)

    def wide(ref, *index):
        return ref[index].astype(jnp.float32)

    def to_other(piece):
        return remote(
            terms.at[3, rows(piece)],
            cross_in.at[rows(piece)],
            c_send.at[piece],
            c_recv.at[piece],
            other,
        )

    def to_backward(piece):
        return remote(
            terms.at[2, rows(piece)], far_in.at[rows(piece)], x_send.at[piece], x_recv.at[piece], backward
        )

    def to_across(piece):
        return remote(
            terms.at[1, rows(piece)], near_in.at[rows(piece)], y_send.at[piece], y_recv.at[piece], across
        )

    swap = remote(terms.at[0], other_in, o_send, o_recv, other)

    def halo_start():
        fetches[0].wait()
        for piece in range(PIECES):
            to_other(piece).start()
        swap.start()
        for fetch in fetches[1:]:
            fetch.start()

    def over_tiles(piece, work):
        def tile(i, carry):
            work(pl.ds(pl.multiple_of(piece * PIECE + i * TILE, TILE), TILE))
            return carry

        lax.fori_loop(0, PIECE // TILE, tile, 0)

    def halo_first(pieces):
        for piece in pieces:
            to_other(piece).wait_recv()

            def add(here):
                cross = wide(cross_in, here)
                terms[2, here] = (wide(terms, 2, here) + jnp.where(near_first, 0.0, cross)).astype(
                    jnp.bfloat16
                )
                terms[1, here] = (wide(terms, 1, here) + jnp.where(near_first, cross, 0.0)).astype(
                    jnp.bfloat16
                )

            over_tiles(piece, add)
            to_backward(piece).start()

    def halo_second(pieces):
        for piece in pieces:
            to_backward(piece).wait_recv()

            def add(here):
                terms[1, here] = (wide(terms, 1, here) + wide(far_in, here)).astype(jnp.bfloat16)

            over_tiles(piece, add)
            to_across(piece).start()

    def halo_end(pieces):
        for piece in pieces:
            to_across(piece).wait_recv()

            def add(here):
                halo_out[here] = halo_out[here] + (wide(other_in, here) + wide(near_in, here))

            over_tiles(piece, add)

    def link_at(part, step):
        return ORDER[(FIRST_LINK[part] + step) % CLASSES]

    weights = (2, 1, 16, 4, 8, 32)
    places = (x_bits[0], y_bits[0], z_bits[0], x_bits[1], y_bits[1], z_bits[1])
    turns = [TILE * weight * (1 - 2 * bit) for weight, bit in zip(weights, places)]
    tile_rows = [TILE * sum(weight * bit for weight, bit in zip(weights, places))]
    for turn in turns:
        tile_rows = tile_rows + [row + turn for row in tile_rows]

    def tile_row(part, position):
        mask = 0
        for step in range(CLASSES):
            if position & (TILES >> (step + 1)):
                link = link_at(part, step)
                mask ^= (1 << link) | (1 << (link % 3))
        return pl.multiple_of(tile_rows[mask], TILE)

    def first_copy(part):
        start, size = PARTS[part]
        return remote(
            grads.at[1 - core, :, pl.ds(start, size)],
            first_in[part],
            send.at[part, 0],
            receive.at[part, 0],
            other,
        )

    def kept(step):
        return (TILES >> step) * TILE

    def pair_of(part, step):
        pair = (total[part], other_total[part])
        return pair if step % 2 else pair[::-1]

    def later_copy(part, step):
        count = kept(step)
        return remote(
            pair_of(part, step)[0].at[pl.ds(count, count)],
            later_in[part].at[pl.ds(count, count)],
            send.at[part, step],
            receive.at[part, step],
            partners[link_at(part, step - 1)],
        )

    def product(terms_of, width, column, half):
        summed = 0.0
        for left, right, begin in terms_of:
            summed = summed + jnp.dot(
                left[...], right[:, pl.ds(begin, width)], preferred_element_type=jnp.float32
            )
        grads[half, :, pl.ds(column, width)] = summed.astype(jnp.bfloat16)

    own_t = entries_t.at[:, pl.ds(0, BLOCK)]
    chosen_t = entries_t.at[:, pl.ds(BLOCK, 2 * BLOCK)]

    def products_of(group):
        column = 640 + 768 * group
        for half in range(2):
            begin = 512 * group + 256 * half
            product([(own_t, dq_own, begin)], 256, column, half)
            product([(own_t, dk_own, begin), (chosen_t, dk, begin)], 256, column + 256, half)
            product([(own_t, dv_own, begin), (chosen_t, dv, begin)], 256, column + 512, half)

    weights = (
        grads.at[0, :, pl.ds(0, WIDTH)],
        grads.at[0, :, pl.ds(WIDTH, WIDTH)],
        grads.at[1, :, pl.ds(0, WIDTH)],
    )
    weight_fetches = [
        pltpu.make_async_copy(
            weights_hbm.at[:, pl.ds(i * WIDTH, WIDTH)], weights[i], fetched.at[len(fetches) + i]
        )
        for i in range(3)
    ]

    def own_part(quarter):
        here = pl.ds(quarter * 256, 256)
        summed = 0.0
        for grad, weight in zip((dq_own, dk_own, dv_own), weights):
            summed = summed + lax.dot_general(
                grad[...], weight[here], NT, preferred_element_type=jnp.float32
            )
        halo_out[:, here] = summed

    def own_pair(pair, carry):
        here = pl.ds(pl.multiple_of(pair * 2 * HEAD_DIM, 2 * HEAD_DIM), 2 * HEAD_DIM)
        queries, grad_keys, grad_values = back_of_pair(
            q[:, here],
            k[:, here],
            v[:, here],
            context[:, here],
            grad_context[:, here],
            [stats[pair, head : head + 1] for head in range(2)],
        )
        dq_own[:, here] = (queries + dq[:, here]).astype(jnp.bfloat16)
        dk_own[:, here] = grad_keys
        dv_own[:, here] = grad_values
        return carry

    def merge_first(part):
        start, size = PARTS[part]
        first_copy(part).wait_recv()

        def merge(positions):
            for position in positions:
                source = pl.ds(tile_row(part, position), TILE)
                total[part][pl.ds(position * TILE, TILE)] = (
                    grads[core, source, pl.ds(start, size)] + first_in[part][source]
                )

        merge(range(TILES // 2, TILES))
        later_copy(part, 1).start()
        merge(range(TILES // 2))

    def merge_later(part, step):
        start, size = PARTS[part]
        count = kept(step)
        held, made = pair_of(part, step)
        later_copy(part, step).wait_recv()
        if step < CLASSES:
            half = count // 2
            for begin in (half, 0):
                made[pl.ds(begin, half)] = (
                    held[pl.ds(begin, half)] + later_in[part][pl.ds(count + begin, half)]
                )
                if begin == half:
                    later_copy(part, step + 1).start()
        else:
            final = wide(held, pl.ds(0, TILE)) + wide(later_in[part], pl.ds(TILE, TILE))
            last[:, :, pl.ds(start, size)] = final.reshape(2, 8, size)

    halo_start()
    fetches[1].wait()
    fetches[2].wait()
    for half in range(2):
        for part in range(2):
            product([(narrow_t, hidden, 512 * half + 256 * part)], 256, 256 * part, half)
    first_copy(0).start()
    halo_first(range(PIECES))
    fetches[3].wait()
    narrow_t[...] = mid[...].T
    fetches[4].wait()
    product([(narrow_t, forecast, 0)], OUTV, 512, 0)
    grads[1, :, pl.ds(512, OUTV)] = jnp.zeros((WIDTH, OUTV), jnp.bfloat16)
    first_copy(1).start()
    fetches[5].wait()
    fetches[6].wait()
    merge_first(0)
    merge_first(1)
    for i in range(7, 13):
        fetches[i].wait()
    lax.fori_loop(0, 4, own_pair, 0)
    halo_second(range(0, 2))
    fetches[13].wait()
    fetches[14].wait()
    products_of(0)
    for part in (2, 3, 4):
        first_copy(part).start()
    halo_second(range(2, 4))
    lax.fori_loop(4, 6, own_pair, 0)
    for part in (2, 3, 4):
        merge_first(part)
    lax.fori_loop(6, 8, own_pair, 0)
    halo_second(range(4, 6))
    products_of(1)
    for part in range(5, 11):
        first_copy(part).start()
    merge_later(0, 1)
    merge_later(1, 1)
    for part in range(5, 11):
        merge_first(part)
    for part in range(parts):
        first_copy(part).wait_send()
    for fetch in weight_fetches:
        fetch.start()
    halo_second(range(6, 8))
    for part in (2, 3, 4):
        merge_later(part, 1)
    for fetch in weight_fetches:
        fetch.wait()
    for step in range(1, CLASSES + 1):
        for part, ahead in ((0, 1), (1, 1), (2, 1), (3, 1), (4, 1)):
            if step + ahead <= CLASSES:
                merge_later(part, step + ahead)
        if step <= 4:
            own_part(step - 1)
        if step == 4:
            swap.wait_recv()
        if step >= 5:
            halo_end(range(4 * step - 20, 4 * step - 16))
        for part in range(5, 11):
            merge_later(part, step)
    finish = remote(last.at[1 - core], last_in, last_send, last_recv, other)
    finish.start()

    def deliver(half, source):
        def columns(begin, size):
            return pl.ds(pl.multiple_of(begin, 128), size)

        output_out[:, columns(512 * half, 512)] = source[:, pl.ds(0, 512)]
        for group in range(2):
            for kind in range(3):
                input_out[:, columns(1024 * kind + 512 * group + 256 * half, 256)] = source[
                    :, pl.ds(640 + 768 * group + 256 * kind, 256)
                ]

    deliver(core, last.at[core])
    finish.wait()
    deliver(1 - core, last_in)
    decoder_out[...] = jnp.where(core == 0, last[0, :, pl.ds(512, OUTV)], last_in[:, pl.ds(512, OUTV)])
    swap.wait_send()
    for piece in range(PIECES):
        to_other(piece).wait_send()
        to_backward(piece).wait_send()
        to_across(piece).wait_send()
    for part in range(parts):
        for step in range(1, CLASSES + 1):
            later_copy(part, step).wait_send()


def tail(terms, entries_t, context_t, weights, *others):
    dma = pltpu.SemaphoreType.DMA
    parts = len(PARTS)
    rows = TILES * TILE
    operands = (terms, entries_t, context_t, weights) + others
    blocks = [pltpu.VMEM((rows, size), jnp.bfloat16) for _, size in PARTS]
    block = pltpu.VMEM((BLOCK, WIDTH), jnp.bfloat16)
    return pl.pallas_call(
        tail_kernel,
        out_shape=(
            jax.ShapeDtypeStruct((8, 3 * WIDTH), jnp.float32),
            jax.ShapeDtypeStruct((8, WIDTH), jnp.float32),
            jax.ShapeDtypeStruct((8, OUTV), jnp.float32),
            jax.ShapeDtypeStruct((BLOCK, WIDTH), jnp.float32),
        ),
        in_specs=[pl.BlockSpec(memory_space=pl.ANY)] * len(operands),
        out_specs=(pl.BlockSpec(memory_space=pltpu.VMEM),) * 4,
        scratch_shapes=blocks * 3
        + [pltpu.VMEM((rows // 2, size), jnp.bfloat16) for _, size in PARTS]
        + [
            pltpu.VMEM((2, 8, HALF), jnp.float32),
            pltpu.VMEM((8, HALF), jnp.float32),
            pltpu.VMEM((2, WIDTH, HALF), jnp.bfloat16),
            pltpu.VMEM(terms.shape, terms.dtype),
        ]
        + [pltpu.VMEM(operand.shape, operand.dtype) for operand in others]
        + [
            pltpu.VMEM((WIDTH, BAND * BLOCK), jnp.bfloat16),
            pltpu.VMEM((WIDTH, BLOCK), jnp.bfloat16),
        ]
        + [block] * 7
        + [dma((parts, CLASSES + 1)), dma((parts, CLASSES + 1)), dma, dma]
        + [dma((PIECES,))] * 6
        + [dma, dma, dma((len(operands) + 3,))],
        compiler_params=pltpu.CompilerParams(
            collective_id=1, has_side_effects=True, vmem_limit_bytes=TAIL_VMEM
        ),
        name="tail",
    )(*operands)


def attend_kernel(q_ref, k_ref, v_ref, mixed_ref, top_ref, total_ref, context_ref, stat_ref):
    sides, tops, totals = forward_of_pair(q_ref[...], k_ref[...], v_ref[...])
    whole = []
    for head in range(2):
        own_top = top_ref[0, head : head + 1]
        top = jnp.maximum(own_top, tops[head])
        own_share = jnp.exp(own_top - top)
        share = jnp.exp(tops[head] - top)
        total = own_share * total_ref[0, head : head + 1] + share * totals[head]
        own_mixed = mixed_ref[0, head * HEAD_DIM : (head + 1) * HEAD_DIM]
        whole.append((own_share * own_mixed + share * sides[head]) / total)
        stat_ref[0, head : head + 1] = top + jnp.log(total)
    context_ref[...] = jnp.concatenate(whole, axis=0).T.astype(jnp.bfloat16)


PAIR = 2 * HEAD_DIM


def column_block(rows):
    return pl.BlockSpec((rows, PAIR), lambda i: (0, i))


STAT_BLOCK = pl.BlockSpec((1, 2, BLOCK), lambda i: (i, 0, 0))


def attend(q, k, v, mixed, tops, totals):
    keys = k.shape[0]
    return pl.pallas_call(
        attend_kernel,
        grid=(HEADS // 2,),
        out_shape=(
            jax.ShapeDtypeStruct((BLOCK, WIDTH), jnp.bfloat16),
            jax.ShapeDtypeStruct((HEADS // 2, 2, BLOCK), jnp.float32),
        ),
        in_specs=[column_block(array.shape[0]) for array in (q, k, v)]
        + [pl.BlockSpec((1, PAIR, BLOCK), lambda i: (i, 0, 0)), STAT_BLOCK, STAT_BLOCK],
        out_specs=(column_block(BLOCK), STAT_BLOCK),
        compiler_params=pltpu.CompilerParams(vmem_limit_bytes=VMEM_LIMIT),
        cost_estimate=pl.CostEstimate(
            flops=4 * BLOCK * keys * WIDTH,
            bytes_accessed=2 * WIDTH * (2 * BLOCK + 2 * keys),
            transcendentals=BLOCK * keys * HEADS,
        ),
        name="attend",
    )(q, k, v, mixed, tops, totals)


def back_of_pair(queries, keys, values, context, grads, stats):
    queries = queries * jnp.bfloat16(0.125)
    keys_t = keys.T
    products = (grads.astype(jnp.float32) * context.astype(jnp.float32)).T
    sides = []
    grad_keys = jnp.zeros(keys.shape, jnp.float32)
    grad_values = jnp.zeros(keys.shape, jnp.float32)
    for head in range(2):
        mask = head_mask(queries.shape, head)
        picked = jnp.where(mask, queries, jnp.bfloat16(0))
        grad_here = jnp.where(mask, grads, jnp.bfloat16(0))
        inner = jnp.sum(products[head * HEAD_DIM : (head + 1) * HEAD_DIM], axis=0, keepdims=True)
        scores = lax.dot_general(keys, picked, NT, preferred_element_type=jnp.float32)
        probs = jnp.exp(scores - stats[head])
        grad_probs = lax.dot_general(values, grad_here, NT, preferred_element_type=jnp.float32)
        grad_scores = (probs * (grad_probs - inner)).astype(jnp.bfloat16)
        grad_values += jnp.dot(
            probs.astype(jnp.bfloat16), grad_here, preferred_element_type=jnp.float32
        )
        grad_keys += jnp.dot(grad_scores, picked, preferred_element_type=jnp.float32)
        sides.append(
            jnp.dot(
                keys_t[head * HEAD_DIM : (head + 1) * HEAD_DIM],
                grad_scores,
                preferred_element_type=jnp.float32,
            )
        )
    grad_queries = (jnp.concatenate(sides, axis=0) * 0.125).T
    return grad_queries, grad_keys.astype(jnp.bfloat16), grad_values.astype(jnp.bfloat16)


def attend_back_kernel(q_ref, k_ref, v_ref, context_ref, grad_ref, stat_ref, dq_ref, dk_ref, dv_ref):
    dq_ref[...], dk_ref[...], dv_ref[...] = back_of_pair(
        q_ref[...],
        k_ref[...],
        v_ref[...],
        context_ref[...],
        grad_ref[...],
        [stat_ref[0, head : head + 1] for head in range(2)],
    )


def attend_back(q, k, v, context, grad_context, stats):
    rows, keys = q.shape[0], k.shape[0]
    return pl.pallas_call(
        attend_back_kernel,
        grid=(HEADS // 2,),
        out_shape=(
            jax.ShapeDtypeStruct((rows, WIDTH), jnp.float32),
            jax.ShapeDtypeStruct((keys, WIDTH), jnp.bfloat16),
            jax.ShapeDtypeStruct((keys, WIDTH), jnp.bfloat16),
        ),
        in_specs=[column_block(array.shape[0]) for array in (q, k, v, context, grad_context)]
        + [STAT_BLOCK],
        out_specs=(column_block(rows), column_block(keys), column_block(keys)),
        compiler_params=pltpu.CompilerParams(vmem_limit_bytes=VMEM_LIMIT),
        cost_estimate=pl.CostEstimate(
            flops=10 * rows * keys * WIDTH,
            bytes_accessed=2 * WIDTH * (4 * rows + 4 * keys),
            transcendentals=rows * keys * HEADS,
        ),
        name="attend_back",
    )(q, k, v, context, grad_context, stats)


def chosen_kernel(slots, dk, dv, weights_k, weights_v, terms):
    found = []
    for block in range(2):
        here = pl.ds(block * BLOCK, BLOCK)
        found.append(
            (
                lax.dot_general(dk[here], weights_k[...], NT, preferred_element_type=jnp.float32)
                + lax.dot_general(dv[here], weights_v[...], NT, preferred_element_type=jnp.float32)
            ).astype(jnp.bfloat16)
        )
    for slot in range(4):
        terms[slot] = jnp.zeros(terms.shape[1:], jnp.bfloat16)
    for block in range(2):
        terms[slots[block]] = found[block]


def chosen_terms(slots, dk, dv, weights):
    rows, columns = dk.shape[0], 256
    whole = pl.BlockSpec((rows, WIDTH), lambda i: (0, 0))
    return pl.pallas_call(
        chosen_kernel,
        grid=(WIDTH // columns,),
        out_shape=jax.ShapeDtypeStruct((4, BLOCK, WIDTH), jnp.bfloat16),
        in_specs=[
            pl.BlockSpec(memory_space=pltpu.SMEM),
            whole,
            whole,
            pl.BlockSpec((columns, WIDTH), lambda i: (i, 1)),
            pl.BlockSpec((columns, WIDTH), lambda i: (i, 2)),
        ],
        out_specs=pl.BlockSpec((4, BLOCK, columns), lambda i: (0, 0, i)),
        compiler_params=pltpu.CompilerParams(vmem_limit_bytes=VMEM_LIMIT),
        name="chosen_terms",
    )(slots, dk, dv, weights, weights)


def dot(left, right):
    return jnp.dot(left, right, preferred_element_type=jnp.float32)


def per_device(
    grid_point_features,
    projection_weights_qkv,
    merging_projection,
    readout_weights_table,
    observed,
    cell_surface_share,
    band_offsets,
    latitude_order,
):
    own_rows = grid_point_features[0]
    at = place()
    block = lax.axis_index("mp")
    near, far = jnp.int32(1), jnp.int32(2)
    above = jnp.where(at["y_lo"] == 0, near, far)
    below = jnp.where(at["y_lo"] == 0, far, near)
    minus = jnp.where(at["core"] == 0, 3, 0)
    plus = jnp.where(at["core"] == 0, 0, 3)
    offsets = lax.dynamic_slice(band_offsets, (block, 1), (1, 2))[0]
    slots = jnp.where(
        offsets == -2, below, jnp.where(offsets == -1, minus, jnp.where(offsets == 1, plus, above))
    ).astype(jnp.int32)

    q, k_own, v_own, k, v, entries, mixed, tops, totals = entry(
        slots, own_rows, projection_weights_qkv
    )
    context, stats = attend(q, k, v, mixed, tops, totals)

    hidden = (own_rows.astype(jnp.float32) + dot(context, merging_projection)).astype(jnp.bfloat16)
    normed_mid = layer_norm(hidden.astype(jnp.float32)).astype(jnp.bfloat16)
    predictions = dot(normed_mid, readout_weights_table)
    target = observed[latitude_order[0]]
    grad_forecast, entries_t, context_t = crps_grad(
        predictions, target, cell_surface_share[:, None], entries, context
    )

    grad_mid = dot(grad_forecast, readout_weights_table.T)
    grad_hidden = jax.vjp(layer_norm, hidden.astype(jnp.float32))[1](grad_mid)[0]
    hidden_half = grad_hidden.astype(jnp.bfloat16)
    grad_context = dot(hidden_half, merging_projection.T).astype(jnp.bfloat16)
    dq, dk, dv = attend_back(q, k, v, context, grad_context, stats)

    terms = chosen_terms(slots, dk, dv, projection_weights_qkv)
    grad_input, grad_output, grad_decoder, grad_normed = tail(
        terms,
        entries_t,
        context_t,
        projection_weights_qkv,
        context,
        hidden_half,
        normed_mid,
        grad_forecast,
        q,
        k_own,
        v_own,
        grad_context,
        stats,
        dq,
        dk,
        dv,
    )
    feature_derivative = (
        grad_hidden + jax.vjp(layer_norm, own_rows.astype(jnp.float32))[1](grad_normed)[0]
    )

    return (
        predictions[None],
        feature_derivative[None],
        grad_input,
        grad_output,
        grad_decoder,
    )


def solution(mesh):
    placed = (P("member", "mp", None), P(), P(), P(), P("mp", None), P("mp"), P(), P("mp", None))
    return jax.shard_map(
        per_device,
        mesh=mesh,
        in_specs=placed,
        out_specs=(
            P("member", "mp", None),
            P("member", "mp", None),
            P(("member", "mp"), None),
            P(("member", "mp"), None),
            P(("member", "mp"), None),
        ),
        check_vma=False,
    )
```
